32 devices in a mesh: scene: 1, space: 32 (over z, y, x, core).
Axes of the slice: x: 2, y: 2, z: 4, core: 2. Of those that a mesh axis runs over, the one named last changes fastest.
Arguments:
- feats: bfloat16 [16384, 256], P(('scene', 'space')), may hold values from -6 to 6
- pre_act: bfloat16 [16384, 256], P(('scene', 'space')), may hold values from -6 to 6
- coarse_grad: bfloat16 [4096, 512], P(('scene', 'space')), may hold values from -12 to 12
- w_sub: bfloat16 [6912, 256], replicated, may hold values from -0.078125 to 0.078125
- w_down: bfloat16 [2048, 512], replicated, may hold values from -0.125 to 0.125
- pair_src: int32 [32, 27, 8], P(('scene', 'space')), may hold values from 0 to 3, as said below
- pair_tgt: int32 [32, 27, 8], P(('scene', 'space')), may hold values from 0 to 7, as said below
- pair_rows: int32 [32, 27, 8, 128], P(('scene', 'space')), may hold values from 0 to 128, as said below
- down_rows: int32 [32, 8, 128], P(('scene', 'space')), may hold values from 0 to 512, as said below
- down_parent: int32 [32, 8, 128], P(('scene', 'space')), may hold values from 0 to 255, as said below
Outputs:
- grad_feats: bfloat16 [16384, 256], P(('scene', 'space'))
- sub_grads: float32 [1769472], P(('scene', 'space'))
- down_grads: float32 [2048, 512], P(('scene', 'space'))
The draws below stay inside these ranges and needn't reach their ends.
Inputs may be any that keep to these rules, and one draw needn't show every extreme that they name: `pair_src`: source block of each slot among the device's own blocks; at every offset each block of a device is the source of at least one slot. `pair_tgt`: target block among the device's blocks extended by 2 blocks of the previous device in front and 2 of the next device behind (index 2 is its own first block); on every device and offset some slot names 0 and some slot names 7. `pair_rows`: for each row of the source block, the row of the target block that it is paired with, 128 for none; for one device, offset and source block the rows that are not 128 are disjoint between slots. `down_rows`: the device's fine rows of each child offset in no order, 512 marking an empty slot; every fine row of a device stands in exactly one of its lists, and on every device one list is full. `down_parent`: parent row among the device's coarse rows extended in front by the last coarse block of the previous device (indices below 128 are that block); any valid value in an empty slot.
All inputs are finite; a program needn't handle non-finite values.
Results may differ from the reference program's by a relative error of at most 0.0049.
Values may be sent and summed in bfloat16 or wider, within the bound.
No kernel may reach another device: no remote copies, remote signals or barrier semaphores. Data moves between devices by JAX's collectives and lax.ppermute only.
A program may use at most 128 MiB of HBM per device.

```python
import math
import jax
import jax.numpy as jnp
from jax import lax

C = 256
CO = 512
KV = 27
CH = 8
BR = 128
HB = 2
NB = 4
NC = 1
PK = 8
RC = 128
FINE = 16384
COARSE = 4096
N_SPACE = 32


def pair_tables(key):

    def one_device(dev_key):

        def one_offset(off_key):
            subkeys = jax.random.split(off_key, 6)
            extra_src = jax.random.randint(subkeys[0], (2 * HB,), 0, NB).astype(jnp.int32)
            sources = jnp.concatenate([jnp.arange(NB, dtype=jnp.int32), extra_src])
            random_tgt = jax.random.randint(subkeys[1], (2 * HB,), 0, NB + 2 * HB).astype(jnp.int32)
            fixed_ends = jnp.array([0, NB + 2 * HB - 1], jnp.int32)
            extra_tgt = jnp.concatenate([fixed_ends, random_tgt[2:]])
            targets = jnp.concatenate([HB + jnp.arange(NB, dtype=jnp.int32), extra_tgt])
            scores = jax.random.randint(subkeys[2], (PK, BR), 0, 1 << 20) * PK + jnp.arange(PK)[:, None]
            same_src = sources[:, None] == sources[None, :]
            best_score = jnp.max(jnp.where(same_src[:, :, None], scores[None, :, :], -1), axis=1)
            owner_row = scores == best_score
            alive_row = jax.random.randint(subkeys[3], (PK, BR), 0, 4) > 0
            row_order = jax.vmap(lambda one_key: jax.random.permutation(one_key, BR))(jax.random.split(subkeys[4], PK))
            tables = jnp.where(owner_row & alive_row, row_order, BR).astype(jnp.int32)
            shuffle = jax.random.permutation(subkeys[5], PK)
            return (sources[shuffle], targets[shuffle], tables[shuffle])
        return jax.vmap(one_offset)(jax.random.split(dev_key, KV))
    return jax.vmap(one_device)(jax.random.split(key, N_SPACE))


def child_lists(key):

    def one_device(dev_key, dev_index):
        subkeys = jax.random.split(dev_key, 6)
        row_count = NB * BR
        rest_count = row_count - RC
        full_child = jax.random.randint(subkeys[0], (), 0, CH).astype(jnp.int32)
        chosen = jax.random.permutation(subkeys[1], 7 * RC)[:rest_count]
        other_child = (chosen // RC).astype(jnp.int32)
        other_child = other_child + (other_child >= full_child).astype(jnp.int32)
        assign = jnp.concatenate([jnp.full((RC,), full_child, jnp.int32), other_child])
        child_of_row = jax.random.permutation(subkeys[2], assign)
        block_of_row = jnp.arange(row_count) // BR
        parent_block = block_of_row * NC // NB + 1
        coin_flip = jax.random.randint(subkeys[4], (row_count,), 0, 2) == 1
        straddle = (block_of_row == 0) & coin_flip & (dev_index > 0)
        parent_block = jnp.where(straddle, 0, parent_block)
        row_perms = jax.vmap(lambda one_key: jax.random.permutation(one_key, BR))(jax.random.split(subkeys[3], NB))
        parent_index = (parent_block * BR + row_perms.reshape(-1)).astype(jnp.int32)
        rank_key = jax.random.permutation(subkeys[5], row_count)

        def one_child(child_id):
            keyval = jnp.where(child_of_row == child_id, rank_key, row_count)
            picked = jnp.argsort(keyval, stable=True)[:RC]
            live_slot = keyval[picked] < row_count
            rows_list = jnp.where(live_slot, picked, row_count).astype(jnp.int32)
            parent_list = parent_index[picked]
            slot_perm = jax.random.permutation(jax.random.fold_in(dev_key, 100 + child_id), RC)
            return (rows_list[slot_perm], parent_list[slot_perm])
        return jax.vmap(one_child)(jnp.arange(CH, dtype=jnp.int32))
    return jax.vmap(one_device)(jax.random.split(key, N_SPACE), jnp.arange(N_SPACE, dtype=jnp.int32))


def draw_pair_src(key, part):
    shared = pair_tables(key)
    return shared[0]


def draw_pair_tgt(key, part):
    shared = pair_tables(key)
    return shared[1]


def draw_pair_rows(key, part):
    shared = pair_tables(key)
    return shared[2]


def draw_down_rows(key, part):
    shared = child_lists(key)
    return shared[0]


def draw_down_parent(key, part):
    shared = child_lists(key)
    return shared[1]


def block_levels(stream_key, shape, shards, least, top_value):
    level = 1.0
    for position, parts in shards:
        steps = jax.random.uniform(jax.random.fold_in(jax.random.fold_in(stream_key, 6), position), (parts,), jnp.float32, least / len(shards), top_value / len(shards))
        level = level * jnp.repeat(jnp.exp(steps), shape[position] // parts).reshape((-1,) + (1,) * (len(shape) - 1 - position))
    return level


def centred(stream_key, dims, spread, bound, cuts=(), held_as=jnp.bfloat16):
    result = jax.random.normal(stream_key, dims, jnp.float32) * spread
    if len(cuts) > 0:
        result = block_levels(stream_key, dims, cuts, -0.22, 0.18) * result
    return jnp.clip(result, min=-bound, max=bound).astype(held_as)


def setup_inputs(seed: int = 0, part: int = 0) -> dict:
    streams_of = jax.random.split(jax.random.key(seed), 11)
    part_splits = jax.random.split(jax.random.fold_in(streams_of[10], part), 11)
    feats = centred(part_splits[0], (FINE, C), 1.0, 6.0, ((0, 32),))
    pre_act = centred(part_splits[1], (FINE, C), 1.0, 6.0, ((0, 32),))
    coarse_grad = centred(part_splits[2], (COARSE, CO), 2.0, 12.0, ((0, 32),))
    w_sub = centred(streams_of[3], (KV * C, C), (KV * C) ** -0.5, 0.078125)
    w_down = centred(streams_of[4], (CH * C, CO), (CH * C) ** -0.5, 0.125)
    pair_src = draw_pair_src(jax.random.fold_in(jax.random.fold_in(streams_of[10], part), 71), part)
    pair_tgt = draw_pair_tgt(jax.random.fold_in(jax.random.fold_in(streams_of[10], part), 71), part)
    pair_rows = draw_pair_rows(jax.random.fold_in(jax.random.fold_in(streams_of[10], part), 71), part)
    down_rows = draw_down_rows(jax.random.fold_in(jax.random.fold_in(streams_of[10], part), 71), part)
    down_parent = draw_down_parent(jax.random.fold_in(jax.random.fold_in(streams_of[10], part), 71), part)
    return {"feats": feats, "pre_act": pre_act, "coarse_grad": coarse_grad, "w_sub": w_sub, "w_down": w_down, "pair_src": pair_src, "pair_tgt": pair_tgt, "pair_rows": pair_rows, "down_rows": down_rows, "down_parent": down_parent}


def reference(feats, pre_act, coarse_grad, w_sub, w_down, pair_src, pair_tgt, pair_rows, down_rows, down_parent):
    row_count = NB * BR
    coarse_count = NC * BR
    highest = lax.Precision.HIGHEST
    coarse_pad = jnp.concatenate([jnp.zeros((BR, CO), coarse_grad.dtype), coarse_grad], 0)
    w_children = w_down.reshape(CH, C, CO).astype(jnp.float32)
    pre_dev = pre_act.reshape(N_SPACE, row_count, C)
    dev_ids = jnp.arange(N_SPACE, dtype=jnp.int32)

    def down_step(running, inputs):
        dev_index, pre_rows, rows_dev, parent_dev = inputs
        start = (dev_index * coarse_count).astype(jnp.int32)
        coarse_ext = lax.dynamic_slice_in_dim(coarse_pad, start, BR + coarse_count, 0)
        coarse_ext = jnp.concatenate([coarse_ext, jnp.zeros((1, CO), coarse_ext.dtype)], 0)
        gathered = coarse_ext[parent_dev].astype(jnp.float32)
        contrib = jnp.einsum('crd,cfd->crf', gathered, w_children, precision=highest)
        grad_out = jnp.zeros((row_count + 1, C), jnp.float32).at[rows_dev.reshape(-1)].add(contrib.reshape(-1, C))
        active = jnp.concatenate([jnp.maximum(pre_rows, 0), jnp.zeros((1, C), pre_rows.dtype)], 0)
        down_term = jnp.einsum('crf,crd->cfd', active[rows_dev].astype(jnp.float32), gathered, precision=highest)
        grad_pre = jnp.where(pre_rows > 0, grad_out[:row_count], 0.0).astype(jnp.bfloat16)
        return (running + down_term, grad_pre)
    down_sum, grad_pre = lax.scan(down_step, jnp.zeros((CH, C, CO), jnp.float32), (dev_ids, pre_dev, down_rows, down_parent))
    fine_zero = jnp.zeros((HB * BR, C), jnp.bfloat16)
    fine_all = jnp.concatenate([fine_zero, grad_pre.reshape(-1, C), fine_zero], 0)
    w_kernel = w_sub.reshape(KV, C, C).astype(jnp.float32)
    feat_dev = feats.reshape(N_SPACE, row_count, C)

    def conv_step(running, inputs):
        dev_index, feat_rows, src_dev, tgt_dev, table_dev = inputs
        start = (dev_index * row_count).astype(jnp.int32)
        fine_ext = lax.dynamic_slice_in_dim(fine_all, start, row_count + 2 * HB * BR, 0).reshape(NB + 2 * HB, BR, C)
        padded = jnp.concatenate([fine_ext, jnp.zeros((NB + 2 * HB, 1, C), fine_ext.dtype)], 1)
        pieces = padded[tgt_dev[:, :, None], table_dev].astype(jnp.float32)
        owner_mask = (src_dev[:, None, :] == jnp.arange(NB)[None, :, None]).astype(jnp.float32)
        columns = jnp.einsum('knp,kprf->knrf', owner_mask, pieces, precision=highest).reshape(KV, row_count, C)
        grad_in = jnp.einsum('krf,kif->ri', columns, w_kernel, precision=highest)
        sub_term = jnp.einsum('ri,krf->kif', feat_rows.astype(jnp.float32), columns, precision=highest)
        return (running + sub_term, grad_in.astype(jnp.bfloat16))
    sub_sum, grad_rows = lax.scan(conv_step, jnp.zeros((KV, C, C), jnp.float32), (dev_ids, feat_dev, pair_src, pair_tgt, pair_rows))
    grad_scale = 1.0 / math.sqrt(FINE)
    grad_feats = grad_rows.reshape(FINE, C)
    sub_grads = sub_sum.reshape(KV * C * C) * grad_scale
    down_grads = down_sum.reshape(CH * C, CO) * grad_scale
    return (grad_feats, sub_grads, down_grads)
```

```python
import functools
import math

import jax
import jax.numpy as jnp
from jax import lax
from jax.experimental import pallas as pl
from jax.experimental.pallas import tpu as pltpu
from jax.sharding import PartitionSpec as P

HB = 2
BF = jnp.bfloat16
F32 = jnp.float32


def dot(a, b):
    return lax.dot_general(a, b, (((1,), (0,)), ((), ())), preferred_element_type=F32)


def dot_nt(a, b):
    return lax.dot_general(a, b, (((1,), (1,)), ((), ())), preferred_element_type=F32)


def one_hot(index, shape, axis):
    return jnp.where(index == lax.broadcasted_iota(jnp.int32, shape, axis), 1.0, 0.0).astype(BF)


def cost(flops, nbytes):
    return pl.CostEstimate(flops=flops, bytes_accessed=nbytes, transcendentals=0)


def down_grad_kernel(prev, cur, par_t, rows, pre, w, gpre, gath, contrib, pick):
    children, slots = rows.shape
    count, channels = pre.shape
    ext = jnp.concatenate([prev[...], cur[...]], 0)
    for c in range(children):
        mine = pl.ds(c * slots, slots)
        parents = one_hot(par_t[:, c : c + 1], (slots, ext.shape[0]), 1)
        got = dot(parents, ext).astype(BF)
        gath[mine, :] = got
        contrib[mine, :] = dot_nt(got, w[pl.ds(c * channels, channels), :]).astype(BF)
        pick[:, mine] = one_hot(rows[c : c + 1, :], (count, slots), 0)
    grad = dot(pick[...], contrib[...])
    gpre[...] = jnp.where(pre[...].astype(F32) > 0, grad, 0.0).astype(BF)


def down_grad(prev, cur, par_t, rows, pre, w):
    children, slots = rows.shape
    count, channels = pre.shape
    width = cur.shape[1]
    return pl.pallas_call(
        down_grad_kernel,
        out_shape=(
            jax.ShapeDtypeStruct((count, channels), BF),
            jax.ShapeDtypeStruct((children * slots, width), BF),
        ),
        scratch_shapes=[
            pltpu.VMEM((children * slots, channels), BF),
            pltpu.VMEM((count, children * slots), BF),
        ],
        compiler_params=pltpu.CompilerParams(vmem_limit_bytes=24 << 20),
        cost_estimate=cost(1 << 30, 4 << 20),
        name="down_grad",
    )(prev, cur, par_t, rows, pre, w)


def down_weight_kernel(act_t, rows, gath, out):
    children, slots = rows.shape
    channels, count = act_t.shape
    for c in range(children):
        pick = one_hot(rows[c : c + 1, :], (count, slots), 0)
        chosen = dot(act_t[...], pick).astype(BF)
        out[pl.ds(c * channels, channels), :] = dot(chosen, gath[pl.ds(c * slots, slots), :])


def down_weight(act_t, rows, gath):
    channels = act_t.shape[0]
    children = rows.shape[0]
    width = gath.shape[1]
    return pl.pallas_call(
        down_weight_kernel,
        out_shape=jax.ShapeDtypeStruct((children * channels, width), F32),
        compiler_params=pltpu.CompilerParams(vmem_limit_bytes=24 << 20),
        cost_estimate=cost(1 << 30, 6 << 20),
        name="down_weight",
    )(act_t, rows, gath)


def conv_plan(kernel, channels, quarters):
    quarter = kernel * channels // 4
    plan, out = [], 0
    for q in quarters:
        row = q * quarter
        while row < (q + 1) * quarter:
            k, first = divmod(row, channels)
            last = min(channels, (q + 1) * quarter - k * channels)
            plan.append((k, first, last, out))
            out += last - first
            row += last - first
    return plan


def conv_kernel(plan, slots, final, *refs):
    src, tgt, tab, ext, feats_t, w, *rest = refs
    if final:
        before, *rest = rest
    grad, sub, wbuf, acc, col0, col1, sems = rest
    rows = tab.shape[0]
    cols = (col0, col1)
    channels = ext.shape[2]
    count = feats_t.shape[1]
    steps = len(plan)
    copies = []
    for at, (k, first, last, out) in enumerate(plan):
        if first == 0:
            copy = pltpu.make_async_copy(
                w.at[pl.ds(k * channels, channels), :], wbuf.at[at], sems.at[at]
            )
            copy.start()
            copies.append(copy)
        else:
            copies.append(None)
    if final:
        acc[...] = before[...]
    else:
        acc[...] = jnp.zeros_like(acc)

    def gather(k, col):
        col[...] = jnp.zeros_like(col)
        for p in range(slots):
            q = k * slots + p
            pick = one_hot(tab[:, q : q + 1], (rows, rows), 1)
            piece = dot(pick, ext[tgt[q]]).astype(BF)
            owner = src[q]
            col[owner] = col[owner] + piece

    gather(plan[0][0], cols[0])
    for at, (k, first, last, out) in enumerate(plan):
        if at + 1 < steps:
            gather(plan[at + 1][0], cols[(at + 1) % 2])
        column = cols[at % 2][...].reshape(count, channels)
        sub[pl.ds(out, last - first), :] = dot(feats_t[pl.ds(first, last - first), :], column)
        if copies[at] is not None:
            copies[at].wait()
            acc[...] += dot_nt(column, wbuf[at])
    grad[...] = acc[...].astype(grad.dtype)


def conv(src, tgt, tab, ext, feats_t, w, quarters, slots, before=None):
    channels, count = feats_t.shape
    kernel = w.shape[0] // channels
    plan = conv_plan(kernel, channels, quarters)
    final = before is not None
    smem = pl.BlockSpec(memory_space=pltpu.SMEM)
    vmem = pl.BlockSpec(memory_space=pltpu.VMEM)
    block = ext.shape[1:]
    return pl.pallas_call(
        functools.partial(conv_kernel, plan, slots, final),
        out_shape=(
            jax.ShapeDtypeStruct((count, channels), BF if final else F32),
            jax.ShapeDtypeStruct((len(quarters) * kernel * channels // 4, channels), F32),
        ),
        in_specs=[smem, smem, vmem, vmem, vmem, pl.BlockSpec(memory_space=pl.ANY)]
        + [vmem] * final,
        out_specs=(vmem, vmem),
        scratch_shapes=[
            pltpu.VMEM((len(plan), channels, channels), BF),
            pltpu.VMEM((count, channels), F32),
            pltpu.VMEM((count // block[0],) + block, BF),
            pltpu.VMEM((count // block[0],) + block, BF),
            pltpu.SemaphoreType.DMA((len(plan),)),
        ],
        compiler_params=pltpu.CompilerParams(vmem_limit_bytes=32 << 20),
        cost_estimate=cost(8 << 30, 8 << 20),
        name="conv",
    )(src, tgt, tab, ext, feats_t, w, *([before] if final else []))


def moved(x, peers, to):
    pairs = [(i, to(i)) for i in range(peers)]
    return lax.ppermute(x, "space", [(i, j) for i, j in pairs if j is not None and 0 <= j < peers])


def at_digit(x, digit):
    return lax.dynamic_index_in_dim(x, digit, axis=1, keepdims=False)


def fold(x, me, peers, radix, stride):
    digit = me // stride % radix
    total = at_digit(x, digit).astype(F32)
    for d in range(1, radix):
        sent = at_digit(x, digit ^ d).astype(BF)
        total = total + moved(sent, peers, lambda i: i ^ (d * stride)).astype(F32)
    return total


def fold_low(x, me, peers, high, rows, width):
    stride = 1
    low = peers // 4
    while stride < low:
        radix = 2 if (low // stride).bit_length() % 2 == 0 else 4
        x = fold(x.reshape(-1, radix, rows, width), me, peers, radix, stride)
        stride *= radix
    return x.reshape(high, rows, width)


def fold_top(x, me, peers, quarters):
    stride = peers // 4
    digit = me // stride
    place = (lambda g: g) if len(quarters) == 4 else (lambda g: g // 2)
    pick = lambda g: lax.dynamic_index_in_dim(x, place(g), axis=0, keepdims=False)
    total = pick(digit).astype(F32)
    for d in range(1, 4):
        to = lambda i: (i ^ (d * stride)) if (i // stride) ^ d in quarters else None
        total = total + moved(pick(digit ^ d).astype(BF), peers, to).astype(F32)
    return total


def per_device(
    feats,
    pre_act,
    coarse_grad,
    w_sub,
    w_down,
    pair_src,
    pair_tgt,
    pair_rows,
    down_rows,
    down_parent,
):
    peers = lax.axis_size("space")
    me = lax.axis_index("space")
    row_count, channels = feats.shape
    block_rows = pair_rows.shape[-1]
    out_width = coarse_grad.shape[1]
    kernel, slots = pair_src.shape[1:]
    children = down_rows.shape[1]
    scale = 1.0 / math.sqrt(peers * row_count)

    previous = moved(coarse_grad[-block_rows:], peers, lambda i: i + 1)
    feats_t = feats.T
    act_t = jnp.maximum(pre_act, 0).T
    tab = pair_rows[0].reshape(kernel * slots, block_rows).T
    src = pair_src[0].reshape(-1)
    tgt = pair_tgt[0].reshape(-1)

    grad_pre, gathered = down_grad(
        previous, coarse_grad, down_parent[0].T, down_rows[0], pre_act, w_down
    )
    halo = HB * block_rows
    before = moved(grad_pre[-halo:], peers, lambda i: i + 1)
    after = moved(grad_pre[:halo], peers, lambda i: i - 1)
    down_term = down_weight(act_t, down_rows[0], gathered)
    ext = jnp.concatenate([before, grad_pre, after], 0).reshape(-1, block_rows, channels)

    down_rows_own = children * channels // peers
    down = fold_low(down_term, me, peers, 4, down_rows_own, out_width)
    down_sum = fold_top(down, me, peers, (0, 1, 2, 3))

    sub_rows_own = kernel * channels // peers
    outer, inner = (0, 3), (1, 2)
    partial, sub_outer = conv(src, tgt, tab, ext, feats_t, w_sub, outer, slots)
    grad_in, sub_inner = conv(src, tgt, tab, ext, feats_t, w_sub, inner, slots, partial)
    sums = [
        fold_top(fold_low(x, me, peers, 2, sub_rows_own, channels), me, peers, quarters)
        for x, quarters in ((sub_outer, outer), (sub_inner, inner))
    ]
    digit = me // (peers // 4)
    sub_sum = jnp.where((digit == 0) | (digit == 3), sums[0], sums[1])
    return (grad_in, sub_sum.reshape(-1) * scale, down_sum * scale)


def solution(mesh):
    rows = ("scene", "space")
    placed = (
        P(rows, None),
        P(rows, None),
        P(rows, None),
        P(),
        P(),
        P(rows, None, None),
        P(rows, None, None),
        P(rows, None, None, None),
        P(rows, None, None),
        P(rows, None, None),
    )
    return jax.shard_map(
        per_device,
        mesh=mesh,
        in_specs=placed,
        out_specs=(P(rows, None), P(rows), P(rows, None)),
        check_vma=False,
    )
```

```python
import functools
import math

import jax
import jax.numpy as jnp
from jax import lax
from jax.experimental import pallas as pl
from jax.experimental.pallas import tpu as pltpu
from jax.sharding import PartitionSpec as P

HB = 2
BF = jnp.bfloat16
F32 = jnp.float32


def dot(a, b):
    return lax.dot_general(a, b, (((1,), (0,)), ((), ())), preferred_element_type=F32)


def dot_nt(a, b):
    return lax.dot_general(a, b, (((1,), (1,)), ((), ())), preferred_element_type=F32)


def one_hot(index, shape, axis):
    return jnp.where(index == lax.broadcasted_iota(jnp.int32, shape, axis), 1.0, 0.0).astype(BF)


def cost(flops, nbytes):
    return pl.CostEstimate(flops=flops, bytes_accessed=nbytes, transcendentals=0)


def fetch(pairs, sems):
    copies = [pltpu.make_async_copy(a, b, sems.at[i]) for i, (a, b) in enumerate(pairs)]
    for copy in copies:
        copy.start()
    return copies


def down_grad_kernel(
    prev, cur, par_t, rows_in, pre_in, w_in, gpre, gath, ext, rows, pre, w, contrib, pick, sems
):
    children, slots = rows.shape
    count, channels = pre.shape
    coarse = prev.shape[0]
    pieces = [
        (rows_in, rows),
        (cur, ext.at[pl.ds(coarse, cur.shape[0]), :]),
        (prev, ext.at[pl.ds(0, coarse), :]),
        (pre_in, pre),
    ]
    own = [pl.ds(c * channels, channels) for c in range(children)]
    copies = fetch(pieces + [(w_in.at[at, :], w.at[at, :]) for at in own], sems)
    copies[0].wait()
    for c in range(children):
        pick[:, pl.ds(c * slots, slots)] = one_hot(rows[c : c + 1, :], (count, slots), 0)
    copies[1].wait()
    copies[2].wait()
    for c in range(children):
        mine = pl.ds(c * slots, slots)
        parents = one_hot(par_t[:, c : c + 1], (slots, ext.shape[0]), 1)
        got = dot(parents, ext[...]).astype(BF)
        gath[mine, :] = got
        copies[4 + c].wait()
        contrib[mine, :] = dot_nt(got, w[own[c], :]).astype(BF)
    grad = dot(pick[...], contrib[...])
    copies[3].wait()
    gpre[...] = jnp.where(pre[...].astype(F32) > 0, grad, 0.0).astype(BF)


def down_grad(prev, cur, par_t, rows, pre, w):
    children, slots = rows.shape
    count, channels = pre.shape
    width = cur.shape[1]
    anywhere = pl.BlockSpec(memory_space=pl.ANY)
    vmem = pl.BlockSpec(memory_space=pltpu.VMEM)
    return pl.pallas_call(
        down_grad_kernel,
        out_shape=(
            jax.ShapeDtypeStruct((count, channels), BF),
            jax.ShapeDtypeStruct((children * slots, width), BF),
        ),
        in_specs=[anywhere, anywhere, vmem, anywhere, anywhere, anywhere],
        out_specs=(vmem, vmem),
        scratch_shapes=[
            pltpu.VMEM((prev.shape[0] + cur.shape[0], width), BF),
            pltpu.VMEM(rows.shape, jnp.int32),
            pltpu.VMEM(pre.shape, BF),
            pltpu.VMEM(w.shape, BF),
            pltpu.VMEM((children * slots, channels), BF),
            pltpu.VMEM((count, children * slots), BF),
            pltpu.SemaphoreType.DMA((4 + children,)),
        ],
        compiler_params=pltpu.CompilerParams(vmem_limit_bytes=48 << 20),
        cost_estimate=cost(1 << 30, 4 << 20),
        name="down_grad",
    )(prev, cur, par_t, rows, pre, w)


def down_weight_kernel(act_t, rows_in, gath, out, rows, total, sems):
    children, slots = rows.shape
    channels, count = act_t.shape
    fetch([(rows_in, rows)], sems.at[pl.ds(children, 1)])[0].wait()
    copies = []
    for c in range(children):
        mine = pl.ds(c * channels, channels)
        pick = one_hot(rows[c : c + 1, :], (count, slots), 0)
        chosen = dot(act_t[...], pick).astype(BF)
        total[mine, :] = dot(chosen, gath[pl.ds(c * slots, slots), :])
        copies += fetch([(total.at[mine, :], out.at[mine, :])], sems.at[pl.ds(c, 1)])
    for copy in copies:
        copy.wait()


def down_weight(act_t, rows, gath):
    channels = act_t.shape[0]
    children = rows.shape[0]
    width = gath.shape[1]
    anywhere = pl.BlockSpec(memory_space=pl.ANY)
    vmem = pl.BlockSpec(memory_space=pltpu.VMEM)
    return pl.pallas_call(
        down_weight_kernel,
        out_shape=jax.ShapeDtypeStruct((children * channels, width), F32),
        in_specs=[vmem, anywhere, vmem],
        out_specs=anywhere,
        scratch_shapes=[
            pltpu.VMEM(rows.shape, jnp.int32),
            pltpu.VMEM((children * channels, width), F32),
            pltpu.SemaphoreType.DMA((children + 1,)),
        ],
        compiler_params=pltpu.CompilerParams(vmem_limit_bytes=48 << 20),
        cost_estimate=cost(1 << 30, 6 << 20),
        name="down_weight",
    )(act_t, rows, gath)


GROUP = 4


def conv_plan(kernel, channels, quarters):
    quarter = kernel * channels // 4
    plan, out = [], 0
    for q in quarters:
        row = q * quarter
        while row < (q + 1) * quarter:
            k, first = divmod(row, channels)
            last = min(channels, (q + 1) * quarter - k * channels)
            plan.append((k, first, last, out))
            out += last - first
            row += last - first
    return plan


def conv_kernel(plan, blocks, final, *refs):
    tab_in, before, own, after, feats_in, w, *rest = refs
    if final:
        partial_in, *rest = rest
    grad, sub, tab, ext, feats_t, wbuf, acc, total, cols, spare, pick0, pick1, sems = rest
    picks = (pick0, pick1)
    rows = tab.shape[0]
    channels, count = feats_t.shape
    halo = before.shape[0]
    pieces = [
        (tab_in, tab),
        (own, ext.at[pl.ds(halo, count), :]),
        (before, ext.at[pl.ds(0, halo), :]),
        (after, ext.at[pl.ds(halo + count, halo), :]),
        (feats_in, feats_t),
    ]
    if final:
        pieces.append((partial_in, acc))
    whole = [k for k, first, last, out in plan if first == 0]
    for at, k in enumerate(whole):
        pieces.append(
            (
                w.at[pl.ds(k * channels, channels), :],
                wbuf.at[:, pl.ds(at * channels, channels)],
            )
        )
    copies = fetch(pieces, sems)
    loads = copies[len(copies) - len(whole) :]
    lanes = lax.broadcasted_iota(jnp.int32, (rows, rows), 1).astype(jnp.int16)
    one, zero = jnp.ones((), BF), jnp.zeros((), BF)

    def build(k, pick):
        for b in range(blocks):
            at = k * blocks + b
            index = jnp.broadcast_to(tab[:, at : at + 1], (rows, rows)).astype(jnp.int16)
            for e in range(ext.shape[0] // rows):
                hit = index == lanes + jnp.int16(e * rows)
                pick[pl.ds(b * rows, rows), pl.ds(e * rows, rows)] = jnp.where(hit, one, zero)

    copies[0].wait()
    build(plan[0][0], picks[0])
    for copy in copies[1 : len(copies) - len(whole)]:
        copy.wait()
    if not final:
        acc[...] = jnp.zeros_like(acc)
    done, added, outs = 0, 0, []
    for at, (k, first, last, out) in enumerate(plan):
        column = dot(picks[at % 2][...], ext[...]).astype(BF)
        if at + 1 < len(plan):
            build(plan[at + 1][0], picks[(at + 1) % 2])
        if first == 0:
            col = cols.at[:, pl.ds(done * channels, channels)]
            done += 1
        else:
            col = spare
        col[...] = column
        mine = pl.ds(out, last - first)
        total[mine, :] = dot(feats_t[pl.ds(first, last - first), :], col[...])
        outs += fetch([(total.at[mine, :], sub.at[mine, :])], sems.at[pl.ds(len(pieces) + at, 1)])
        if first == 0 and (done - added == GROUP or done == len(whole)):
            for load in loads[added:done]:
                load.wait()
            span = pl.ds(added * channels, (done - added) * channels)
            acc[...] += dot_nt(cols[:, span], wbuf[:, span])
            added = done
    grad[...] = acc[...].astype(grad.dtype)
    for copy in outs:
        copy.wait()


def conv(tab, before, own, after, feats_t, w, quarters, partial=None):
    channels, count = feats_t.shape
    kernel = w.shape[0] // channels
    rows = tab.shape[0]
    blocks = count // rows
    plan = conv_plan(kernel, channels, quarters)
    whole = sum(first == 0 for k, first, last, out in plan)
    final = partial is not None
    anywhere = pl.BlockSpec(memory_space=pl.ANY)
    vmem = pl.BlockSpec(memory_space=pltpu.VMEM)
    total = (len(quarters) * kernel * channels // 4, channels)
    ext_rows = count + before.shape[0] + after.shape[0]
    return pl.pallas_call(
        functools.partial(conv_kernel, plan, blocks, final),
        out_shape=(
            jax.ShapeDtypeStruct((count, channels), BF if final else F32),
            jax.ShapeDtypeStruct(total, F32),
        ),
        in_specs=[anywhere] * (6 + final),
        out_specs=(vmem, anywhere),
        scratch_shapes=[
            pltpu.VMEM(tab.shape, jnp.int32),
            pltpu.VMEM((ext_rows, channels), BF),
            pltpu.VMEM((channels, count), BF),
            pltpu.VMEM((channels, whole * channels), BF),
            pltpu.VMEM((count, channels), F32),
            pltpu.VMEM(total, F32),
            pltpu.VMEM((count, whole * channels), BF),
            pltpu.VMEM((count, channels), BF),
            pltpu.VMEM((count, ext_rows), BF),
            pltpu.VMEM((count, ext_rows), BF),
            pltpu.SemaphoreType.DMA((6 + whole + len(plan),)),
        ],
        compiler_params=pltpu.CompilerParams(vmem_limit_bytes=48 << 20),
        cost_estimate=cost(8 << 30, 8 << 20),
        name="conv",
    )(tab, before, own, after, feats_t, w, *([partial] if final else []))


def moved(x, peers, to):
    pairs = [(i, to(i)) for i in range(peers)]
    return lax.ppermute(x, "space", [(i, j) for i, j in pairs if j is not None and 0 <= j < peers])


def taken(x, axis, digit):
    return lax.dynamic_index_in_dim(x, digit, axis=axis, keepdims=False)


def fold_core(x, kept, me, peers):
    core = me % 2
    axis = x.ndim - 3
    got = moved(taken(x, axis, 1 - core).astype(BF), peers, lambda i: i ^ 1)
    return taken(kept, axis, core), got


def low_steps(bits):
    left = [list(range(bits - 1, -1, -1)) for core in range(2)]
    steps = []
    for j in range(bits):
        by = (j, (j + bits // 2) % bits)
        steps.append((by, [left[core].index(by[core]) for core in range(2)]))
        for core in range(2):
            left[core].remove(by[core])
    return steps


def fold_low(keep, got, me, peers, step):
    core = me % 2
    by, axes = step
    bit = jnp.where(core == 0, me >> (1 + by[0]), me >> (1 + by[1])) % 2

    def half(x, digit):
        if axes[0] == axes[1]:
            return taken(x, 1 + axes[0], digit)
        return jnp.where(core == 0, taken(x, 1 + axes[0], digit), taken(x, 1 + axes[1], digit))

    def piece(digit):
        return half(keep, digit) + half(got, digit).astype(F32)

    sent = piece(1 - bit).astype(BF)
    return piece(bit), moved(sent, peers, lambda i: i ^ (2 << by[i % 2]))


def fold_bit(keep, got, me, peers, stride, first):
    bit = me // stride % 2
    axis = keep.ndim - 3

    def piece(digit):
        return taken(keep, axis, digit) + taken(got, axis, digit).astype(F32)

    mine = bit ^ first
    sent = piece(1 - mine).astype(BF)
    return piece(mine), moved(sent, peers, lambda i: i ^ stride)


def per_device(
    feats,
    pre_act,
    coarse_grad,
    w_sub,
    w_down,
    pair_src,
    pair_tgt,
    pair_rows,
    down_rows,
    down_parent,
):
    peers = lax.axis_size("space")
    me = lax.axis_index("space")
    row_count, channels = feats.shape
    block_rows = pair_rows.shape[-1]
    blocks = row_count // block_rows
    out_width = coarse_grad.shape[1]
    kernel = pair_src.shape[1]
    children = down_rows.shape[1]
    scale = 1.0 / math.sqrt(peers * row_count)
    bits = (peers // 8).bit_length() - 1
    steps = low_steps(bits)
    near, far = peers // 4, peers // 2

    previous = moved(coarse_grad[-block_rows:], peers, lambda i: i + 1)
    grad_pre, gathered = down_grad(
        previous, coarse_grad, down_parent[0].T, down_rows[0], pre_act, w_down
    )
    halo = HB * block_rows
    before = moved(grad_pre[-halo:], peers, lambda i: i + 1)
    after = moved(grad_pre[:halo], peers, lambda i: i - 1)

    feats_t = feats.T
    act_t = jnp.maximum(pre_act, 0).T
    owned = pair_src[0][:, None, :, None] == jnp.arange(blocks)[None, :, None, None]
    there = (pair_rows[0] < block_rows)[:, None]
    spot = (pair_tgt[0][:, :, None] * block_rows + pair_rows[0] + 1)[:, None]
    merged = jnp.sum(jnp.where(owned & there, spot, 0), axis=2) - 1
    tab = merged.reshape(kernel * blocks, block_rows).T

    down_term = down_weight(act_t, down_rows[0], gathered)
    own, down_tied = lax.optimization_barrier((grad_pre, down_term))

    down_shards = (4,) + (2,) * (bits + 1) + (children * channels // peers, out_width)
    down_keep, down_got = fold_core(
        down_term.reshape(down_shards), down_tied.reshape(down_shards), me, peers
    )

    def sub_shards(x):
        return x.reshape((2,) + (2,) * (bits + 1) + (kernel * channels // peers, channels))

    partial, outer = conv(tab, before, own, after, feats_t, w_sub, (0, 3))
    outer = sub_shards(outer)
    outer_keep, outer_got = fold_core(outer, outer, me, peers)
    partial, down_got = lax.optimization_barrier((partial, down_got))
    grad_in, inner = conv(tab, before, own, after, feats_t, w_sub, (1, 2), partial)
    inner = sub_shards(inner)
    inner_keep, inner_got = fold_core(inner, inner, me, peers)

    for step in steps:
        down_keep, down_got = fold_low(down_keep, down_got, me, peers, step)
        outer_keep, outer_got = fold_low(outer_keep, outer_got, me, peers, step)
        inner_keep, inner_got = fold_low(inner_keep, inner_got, me, peers, step)

    down_keep = down_keep.reshape((2, 2) + down_keep.shape[-2:])
    down_got = down_got.reshape((2, 2) + down_got.shape[-2:])
    down_keep, down_got = fold_bit(down_keep, down_got, me, peers, near, 0)
    outer_keep, outer_got = fold_bit(outer_keep, outer_got, me, peers, near, 0)
    inner_keep, inner_got = fold_bit(inner_keep, inner_got, me, peers, near, 1)
    down_keep, down_got = fold_bit(down_keep, down_got, me, peers, far, 0)
    down_sum = down_keep + down_got.astype(F32)

    digit = me // near
    is_outer = (digit == 0) | (digit == 3)
    outer_sum = outer_keep + outer_got.astype(F32)
    inner_sum = inner_keep + inner_got.astype(F32)
    sent = jnp.where(is_outer, inner_sum, outer_sum).astype(BF)
    sub_sum = jnp.where(is_outer, outer_sum, inner_sum)
    sub_sum = sub_sum + moved(sent, peers, lambda i: i ^ far).astype(F32)
    return (grad_in, sub_sum.reshape(-1) * scale, down_sum * scale)


def solution(mesh):
    rows = ("scene", "space")
    placed = (
        P(rows, None),
        P(rows, None),
        P(rows, None),
        P(),
        P(),
        P(rows, None, None),
        P(rows, None, None),
        P(rows, None, None, None),
        P(rows, None, None),
        P(rows, None, None),
    )
    return jax.shard_map(
        per_device,
        mesh=mesh,
        in_specs=placed,
        out_specs=(P(rows, None), P(rows), P(rows, None)),
        check_vma=False,
    )
```

```python
import functools
import math

import jax
import jax.numpy as jnp
from jax import lax
from jax.experimental import pallas as pl
from jax.experimental.pallas import tpu as pltpu
from jax.sharding import PartitionSpec as P

HB = 2
BF = jnp.bfloat16
F32 = jnp.float32


def dot(a, b):
    return lax.dot_general(a, b, (((1,), (0,)), ((), ())), preferred_element_type=F32)


def dot_nt(a, b):
    return lax.dot_general(a, b, (((1,), (1,)), ((), ())), preferred_element_type=F32)


def one_hot(index, shape, axis):
    return jnp.where(index == lax.broadcasted_iota(jnp.int32, shape, axis), 1.0, 0.0).astype(BF)


def split(total, keep, send, core):
    pairs, rows = keep.shape[:2]
    for j in range(pairs):
        mine = pl.multiple_of((2 * j + core) * rows, 8)
        other = pl.multiple_of((2 * j + 1 - core) * rows, 8)
        keep[j] = total[pl.ds(mine, rows), :]
        send[j] = total[pl.ds(other, rows), :].astype(BF)


def halves(total, rows):
    shape = (total[0] // (2 * rows), rows, total[1])
    return (jax.ShapeDtypeStruct(shape, F32), jax.ShapeDtypeStruct(shape, BF))


def split_outside(total, rows, core):
    pairs = total.reshape(-1, 2, rows, total.shape[1])
    return taken(pairs, 1, core), taken(pairs, 1, 1 - core).astype(BF)


def cost(flops, nbytes):
    return pl.CostEstimate(flops=flops, bytes_accessed=nbytes, transcendentals=0)


def fetch(pairs, sems):
    copies = [pltpu.make_async_copy(a, b, sems.at[i]) for i, (a, b) in enumerate(pairs)]
    for copy in copies:
        copy.start()
    return copies


def down_grad_kernel(
    prev, cur, par_t, rows_in, pre_in, w_in, gpre, gath, ext, rows, pre, w, contrib, pick, sems
):
    children, slots = rows.shape
    count, channels = pre.shape
    coarse = prev.shape[0]
    pieces = [
        (rows_in, rows),
        (cur, ext.at[pl.ds(coarse, cur.shape[0]), :]),
        (prev, ext.at[pl.ds(0, coarse), :]),
        (pre_in, pre),
    ]
    own = [pl.ds(c * channels, channels) for c in range(children)]
    copies = fetch(pieces + [(w_in.at[at, :], w.at[at, :]) for at in own], sems)
    copies[0].wait()
    for c in range(children):
        pick[:, pl.ds(c * slots, slots)] = one_hot(rows[c : c + 1, :], (count, slots), 0)
    copies[1].wait()
    copies[2].wait()
    for c in range(children):
        mine = pl.ds(c * slots, slots)
        parents = one_hot(par_t[:, c : c + 1], (slots, ext.shape[0]), 1)
        got = dot(parents, ext[...]).astype(BF)
        gath[mine, :] = got
        copies[4 + c].wait()
        contrib[mine, :] = dot_nt(got, w[own[c], :]).astype(BF)
    grad = dot(pick[...], contrib[...])
    copies[3].wait()
    gpre[...] = jnp.where(pre[...].astype(F32) > 0, grad, 0.0).astype(BF)


def down_grad(prev, cur, par_t, rows, pre, w):
    children, slots = rows.shape
    count, channels = pre.shape
    width = cur.shape[1]
    anywhere = pl.BlockSpec(memory_space=pl.ANY)
    hbm = pl.BlockSpec(memory_space=pltpu.HBM)
    vmem = pl.BlockSpec(memory_space=pltpu.VMEM)
    return pl.pallas_call(
        down_grad_kernel,
        out_shape=(
            jax.ShapeDtypeStruct((count, channels), BF),
            jax.ShapeDtypeStruct((children * slots, width), BF),
        ),
        in_specs=[anywhere, hbm, vmem, hbm, hbm, hbm],
        out_specs=(vmem, vmem),
        scratch_shapes=[
            pltpu.VMEM((prev.shape[0] + cur.shape[0], width), BF),
            pltpu.VMEM(rows.shape, jnp.int32),
            pltpu.VMEM(pre.shape, BF),
            pltpu.VMEM(w.shape, BF),
            pltpu.VMEM((children * slots, channels), BF),
            pltpu.VMEM((count, children * slots), BF),
            pltpu.SemaphoreType.DMA((4 + children,)),
        ],
        compiler_params=pltpu.CompilerParams(vmem_limit_bytes=62 << 20),
        cost_estimate=cost(1 << 30, 4 << 20),
        name="down_grad",
    )(prev, cur, par_t, rows, pre, w)


def down_weight_kernel(core, act_t, rows_in, gath, *refs):
    *outs, total, rows, sems = refs
    children, slots = rows.shape
    channels, count = act_t.shape
    fetch([(rows_in, rows)], sems)[0].wait()
    for c in range(children):
        pick = one_hot(rows[c : c + 1, :], (count, slots), 0)
        chosen = dot(act_t[...], pick).astype(BF)
        total[pl.ds(c * channels, channels), :] = dot(chosen, gath[pl.ds(c * slots, slots), :])
    if outs:
        split(total, *outs, core[0])


def down_weight(core, act_t, rows, gath, shard):
    channels = act_t.shape[0]
    children = rows.shape[0]
    total = (children * channels, gath.shape[1])
    hbm = pl.BlockSpec(memory_space=pltpu.HBM)
    vmem = pl.BlockSpec(memory_space=pltpu.VMEM)
    inside = shard % 8 == 0
    out = pl.pallas_call(
        down_weight_kernel,
        out_shape=halves(total, shard) if inside else jax.ShapeDtypeStruct(total, F32),
        in_specs=[pl.BlockSpec(memory_space=pltpu.SMEM), vmem, hbm, vmem],
        out_specs=(vmem, vmem) if inside else vmem,
        scratch_shapes=[pltpu.VMEM(total, F32)] * inside
        + [
            pltpu.VMEM(rows.shape, jnp.int32),
            pltpu.SemaphoreType.DMA((1,)),
        ],
        compiler_params=pltpu.CompilerParams(vmem_limit_bytes=56 << 20),
        cost_estimate=cost(1 << 30, 6 << 20),
        name="down_weight",
    )(core, act_t, rows, gath)
    return out if inside else split_outside(out, shard, core[0])


def conv_plan(kernel, channels, quarters):
    quarter = kernel * channels // 4
    plan, out = [], 0
    for q in quarters:
        row = q * quarter
        while row < (q + 1) * quarter:
            k, first = divmod(row, channels)
            last = min(channels, (q + 1) * quarter - k * channels)
            plan.append((k, first, last, out))
            out += last - first
            row += last - first
    return plan


def conv_kernel(plan, slots, final, inside, *refs):
    core, src, tgt, tab_in, before, own, after, feats_in, w, *rest = refs
    if final:
        partial_in, *rest = rest
    grad, *rest = rest
    if inside:
        keep, send, *rest = rest
    total, tab, ext, feats_t, wbuf, acc, col0, col1, sems = rest
    cols = (col0, col1)
    rows = tab.shape[0]
    blocks = col0.shape[0]
    channels, count = feats_t.shape
    halo = before.shape[0]
    side = halo // rows
    pieces = [(tab_in, tab)]
    pieces += [(own.at[pl.ds(b * rows, rows), :], ext.at[side + b]) for b in range(blocks)]
    pieces += [(before.at[pl.ds(b * rows, rows), :], ext.at[b]) for b in range(side)]
    pieces += [
        (after.at[pl.ds(b * rows, rows), :], ext.at[side + blocks + b]) for b in range(side)
    ]
    pieces.append((feats_in, feats_t))
    if final:
        pieces.append((partial_in, acc))
    early = len(pieces)
    for at, (k, first, last, out) in enumerate(plan):
        pieces.append((w.at[pl.ds(k * channels, channels), :], wbuf.at[at]))
    copies = fetch(pieces, sems)
    lanes = lax.broadcasted_iota(jnp.int32, (rows, rows), 1).astype(jnp.int16)
    one, zero = jnp.ones((), BF), jnp.zeros((), BF)

    def gather(k, col):
        col[...] = jnp.zeros_like(col)
        for p in range(slots):
            q = k * slots + p
            index = jnp.broadcast_to(tab[:, q : q + 1], (rows, rows)).astype(jnp.int16)
            pick = jnp.where(index == lanes, one, zero)
            piece = dot(pick, ext[tgt[q]]).astype(BF)
            owner = src[q]
            col[owner] = col[owner] + piece

    for copy in copies[:early]:
        copy.wait()
    if not final:
        acc[...] = jnp.zeros_like(acc)
    gather(plan[0][0], cols[0])
    for at, (k, first, last, out) in enumerate(plan):
        if at + 1 < len(plan):
            gather(plan[at + 1][0], cols[(at + 1) % 2])
        column = cols[at % 2][...].reshape(count, channels)
        total[pl.ds(out, last - first), :] = dot(feats_t[pl.ds(first, last - first), :], column)
        copies[early + at].wait()
        if first == 0:
            acc[...] += dot_nt(column, wbuf[at])
    grad[...] = acc[...].astype(grad.dtype)
    if inside:
        split(total, keep, send, core[0])


def conv(core, src, tgt, tab, before, own, after, feats_t, w, quarters, shard, partial=None):
    channels, count = feats_t.shape
    kernel = w.shape[0] // channels
    rows = tab.shape[0]
    slots = tab.shape[1] // kernel
    plan = conv_plan(kernel, channels, quarters)
    final = partial is not None
    inside = shard % 8 == 0
    anywhere = pl.BlockSpec(memory_space=pl.ANY)
    hbm = pl.BlockSpec(memory_space=pltpu.HBM)
    vmem = pl.BlockSpec(memory_space=pltpu.VMEM)
    smem = pl.BlockSpec(memory_space=pltpu.SMEM)
    total = (len(quarters) * kernel * channels // 4, channels)
    ext_rows = count + before.shape[0] + after.shape[0]
    block = (rows, channels)
    grad = jax.ShapeDtypeStruct((count, channels), BF if final else F32)
    weight = halves(total, shard) if inside else (jax.ShapeDtypeStruct(total, F32),)
    out = pl.pallas_call(
        functools.partial(conv_kernel, plan, slots, final, inside),
        out_shape=(grad,) + weight,
        in_specs=[smem] * 3 + [anywhere] * 5 + [hbm] + [anywhere] * final,
        out_specs=(vmem,) * (1 + len(weight)),
        scratch_shapes=[pltpu.VMEM(total, F32)] * inside
        + [
            pltpu.VMEM(tab.shape, jnp.int32),
            pltpu.VMEM((ext_rows // rows,) + block, BF),
            pltpu.VMEM((channels, count), BF),
            pltpu.VMEM((len(plan), channels, channels), BF),
            pltpu.VMEM((count, channels), F32),
            pltpu.VMEM((count // rows,) + block, BF),
            pltpu.VMEM((count // rows,) + block, BF),
            pltpu.SemaphoreType.DMA((3 + ext_rows // rows + len(plan),)),
        ],
        compiler_params=pltpu.CompilerParams(vmem_limit_bytes=56 << 20),
        cost_estimate=cost(12 << 30, 8 << 20),
        name="conv",
    )(core, src, tgt, tab, before, own, after, feats_t, w, *([partial] if final else []))
    return out if inside else (out[0],) + split_outside(out[1], shard, core[0])


def moved(x, peers, to):
    pairs = [(i, to(i)) for i in range(peers)]
    return lax.ppermute(x, "space", [(i, j) for i, j in pairs if j is not None and 0 <= j < peers])


def taken(x, axis, digit):
    return lax.dynamic_index_in_dim(x, digit, axis=axis, keepdims=False)


def low_steps(bits):
    left = [list(range(bits - 1, -1, -1)) for core in range(2)]
    steps = []
    for j in range(bits):
        by = (j, (j + bits // 2) % bits)
        steps.append((by, [left[core].index(by[core]) for core in range(2)]))
        for core in range(2):
            left[core].remove(by[core])
    return steps


def fold_low(keep, got, me, step):
    core = me % 2
    by, axes = step
    bit = jnp.where(core == 0, me >> (1 + by[0]), me >> (1 + by[1])) % 2

    def half(x, digit):
        if axes[0] == axes[1]:
            return taken(x, 1 + axes[0], digit)
        return jnp.where(core == 0, taken(x, 1 + axes[0], digit), taken(x, 1 + axes[1], digit))

    def piece(digit):
        return half(keep, digit) + half(got, digit).astype(F32)

    return piece(bit), piece(1 - bit).astype(BF), lambda i: i ^ (2 << by[i % 2])


def fold_bit(keep, got, me, peers, stride, first):
    bit = me // stride % 2
    axis = keep.ndim - 3

    def piece(digit):
        return taken(keep, axis, digit) + taken(got, axis, digit).astype(F32)

    mine = bit ^ first
    sent = piece(1 - mine).astype(BF)
    return piece(mine), moved(sent, peers, lambda i: i ^ stride)


def per_device(
    feats,
    pre_act,
    coarse_grad,
    w_sub,
    w_down,
    pair_src,
    pair_tgt,
    pair_rows,
    down_rows,
    down_parent,
):
    peers = lax.axis_size("space")
    me = lax.axis_index("space")
    row_count, channels = feats.shape
    block_rows = pair_rows.shape[-1]
    out_width = coarse_grad.shape[1]
    kernel = pair_src.shape[1]
    children = down_rows.shape[1]
    scale = 1.0 / math.sqrt(peers * row_count)
    bits = (peers // 8).bit_length() - 1
    steps = low_steps(bits)
    near, far = peers // 4, peers // 2

    previous = moved(coarse_grad[-block_rows:], peers, lambda i: i + 1)
    grad_pre, gathered = down_grad(
        previous, coarse_grad, down_parent[0].T, down_rows[0], pre_act, w_down
    )
    halo = HB * block_rows
    before = moved(grad_pre[-halo:], peers, lambda i: i + 1)
    after = moved(grad_pre[:halo], peers, lambda i: i - 1)

    feats_t = feats.T
    act_t = jnp.maximum(pre_act, 0).T
    src = pair_src[0].reshape(-1)
    tgt = pair_tgt[0].reshape(-1)
    tab = pair_rows[0].reshape(-1, block_rows).T
    core = (me % 2).reshape(1)

    def across(x):
        return moved(x, peers, lambda i: i ^ 1)

    def spread(x, high):
        return x.reshape((high,) + (2,) * bits + x.shape[-2:])

    down_keep, down_send = down_weight(
        core, act_t, down_rows[0], gathered, children * channels // peers
    )
    shard = kernel * channels // peers
    common = (core, src, tgt, tab, before, grad_pre, after, feats_t, w_sub)
    pinned = lax.optimization_barrier

    down_got = across(down_send)
    partial, outer_keep, outer_send = conv(*common, (0, 3), shard)
    partial, outer_keep, outer_send, down_got = pinned(
        (partial, outer_keep, outer_send, down_got)
    )
    down_keep, down_got = spread(down_keep, 4), spread(down_got, 4)
    down_keep, down_send, to = fold_low(down_keep, down_got, me, steps[0])
    down_got = moved(down_send, peers, to)
    outer_got = across(outer_send)
    grad_in, inner_keep, inner_send = conv(*common, (1, 2), shard, partial)
    grad_in, inner_keep, inner_send, down_got, outer_got = pinned(
        (grad_in, inner_keep, inner_send, down_got, outer_got)
    )
    inner_got = across(inner_send)
    outer_keep, outer_got = spread(outer_keep, 2), spread(outer_got, 2)
    inner_keep, inner_got = spread(inner_keep, 2), spread(inner_got, 2)

    for at, step in enumerate(steps):
        if at > 0:
            down_keep, down_send, to = fold_low(down_keep, down_got, me, step)
            down_got = moved(down_send, peers, to)
        outer_keep, outer_send, to = fold_low(outer_keep, outer_got, me, step)
        outer_got = moved(outer_send, peers, to)
        inner_keep, inner_send, to = fold_low(inner_keep, inner_got, me, step)
        inner_got = moved(inner_send, peers, to)

    down_keep = down_keep.reshape((2, 2) + down_keep.shape[-2:])
    down_got = down_got.reshape((2, 2) + down_got.shape[-2:])
    down_keep, down_got = fold_bit(down_keep, down_got, me, peers, near, 0)
    outer_keep, outer_got = fold_bit(outer_keep, outer_got, me, peers, near, 0)
    inner_keep, inner_got = fold_bit(inner_keep, inner_got, me, peers, near, 1)
    down_keep, down_got = fold_bit(down_keep, down_got, me, peers, far, 0)
    down_sum = down_keep + down_got.astype(F32)

    digit = me // near
    is_outer = (digit == 0) | (digit == 3)
    outer_sum = outer_keep + outer_got.astype(F32)
    inner_sum = inner_keep + inner_got.astype(F32)
    sent = jnp.where(is_outer, inner_sum, outer_sum).astype(BF)
    sub_sum = jnp.where(is_outer, outer_sum, inner_sum)
    sub_sum = sub_sum + moved(sent, peers, lambda i: i ^ far).astype(F32)
    return (grad_in, sub_sum.reshape(-1) * scale, down_sum * scale)


def solution(mesh):
    rows = ("scene", "space")
    placed = (
        P(rows, None),
        P(rows, None),
        P(rows, None),
        P(),
        P(),
        P(rows, None, None),
        P(rows, None, None),
        P(rows, None, None, None),
        P(rows, None, None),
        P(rows, None, None),
    )
    return jax.shard_map(
        per_device,
        mesh=mesh,
        in_specs=placed,
        out_specs=(P(rows, None), P(rows), P(rows, None)),
        check_vma=False,
    )
```

```python
import functools
import math

import jax
import jax.numpy as jnp
from jax import lax
from jax.experimental import pallas as pl
from jax.experimental.pallas import tpu as pltpu
from jax.sharding import PartitionSpec as P

HB = 2
BF = jnp.bfloat16
F32 = jnp.float32


def dot(a, b):
    return lax.dot_general(a, b, (((1,), (0,)), ((), ())), preferred_element_type=F32)


def dot_nt(a, b):
    return lax.dot_general(a, b, (((1,), (1,)), ((), ())), preferred_element_type=F32)


def one_hot(index, shape, axis):
    return jnp.where(index == lax.broadcasted_iota(jnp.int32, shape, axis), 1.0, 0.0).astype(BF)


def segments(first, count, shard):
    row, cuts = first, []
    while row < first + count:
        number, inside = divmod(row, shard)
        rows = min(shard - inside, first + count - row)
        cuts.append((row - first, number, inside, rows))
        row += rows
    return cuts


def place(both, value, first, core):
    for at, number, inside, rows in segments(first, value.shape[0], both.shape[2]):
        both[(number % 2) ^ core, number // 2, pl.ds(inside, rows), :] = value[at : at + rows]


def halves(total, shard):
    pairs = total[0] // (2 * shard)
    return (
        jax.ShapeDtypeStruct((2, pairs, shard, total[1]), F32),
        jax.ShapeDtypeStruct((pairs, shard, total[1]), BF),
    )


VMEM = pl.BlockSpec(memory_space=pltpu.VMEM)
SMEM = pl.BlockSpec(memory_space=pltpu.SMEM)


def cost(flops, nbytes):
    return pl.CostEstimate(flops=flops, bytes_accessed=nbytes, transcendentals=0)


def prep_kernel(feats, pre, pairs, rows, parents, feats_t, act, tab, pick, parent_pick, chosen):
    children, slots = rows.shape
    count, channels = feats.shape
    square = (channels, channels)
    wide = one_hot(lax.broadcasted_iota(jnp.int32, square, 0), square, 1)
    eye = wide[:slots, :slots]
    for c in range(children):
        pick[:, pl.ds(c * slots, slots)] = one_hot(rows[c : c + 1, :], (count, slots), 0)
    columns = dot_nt(eye, parents[...].astype(F32).astype(BF)).astype(jnp.int32)
    for c in range(children):
        parent_pick[pl.ds(c * slots, slots), :] = one_hot(
            columns[:, c : c + 1], (slots, parent_pick.shape[1]), 1
        )
    act[...] = jnp.maximum(pre[...], jnp.zeros((), BF))
    chosen[...] = dot(dot_nt(wide, act[...]).astype(BF), pick[...]).astype(BF)
    tab[...] = dot_nt(eye, pairs[...].astype(F32).astype(BF)).astype(jnp.int32)
    feats_t[...] = dot_nt(wide, feats[...]).astype(BF)


def prep(feats, pre, pairs, rows, parents, parent_rows):
    count, channels = feats.shape
    children, slots = rows.shape
    shapes = (
        ((channels, count), BF),
        ((count, channels), BF),
        ((pairs.shape[1], pairs.shape[0]), jnp.int32),
        ((count, children * slots), BF),
        ((children * slots, parent_rows), BF),
        ((channels, children * slots), BF),
    )
    return pl.pallas_call(
        prep_kernel,
        out_shape=tuple(jax.ShapeDtypeStruct(*shape) for shape in shapes),
        in_specs=[VMEM] * 5,
        out_specs=(VMEM,) * len(shapes),
        compiler_params=pltpu.CompilerParams(vmem_limit_bytes=16 << 20),
        cost_estimate=cost(1 << 30, 3 << 20),
        name="prep",
    )(feats, pre, pairs, rows, parents)


def down_grad_kernel(prev, cur, act, w, pick, parent_pick, gpre, head, tail, gath, contrib):
    count, channels = act.shape
    children = w.shape[0] // channels
    slots = gath.shape[0] // children
    ext = jnp.concatenate([prev[...], cur[...]], 0)
    for c in range(children):
        mine = pl.ds(c * slots, slots)
        got = dot(parent_pick[mine, :], ext).astype(BF)
        gath[mine, :] = got
        contrib[mine, :] = dot_nt(got, w[pl.ds(c * channels, channels), :]).astype(BF)
    grad = dot(pick[...], contrib[...])
    masked = jnp.where(act[...].astype(F32) > 0, grad, 0.0).astype(BF)
    gpre[...] = masked
    halo = head.shape[0]
    head[...] = masked[:halo]
    tail[...] = masked[count - halo :]


def down_grad(prev, cur, act, w, pick, parent_pick, halo):
    count, channels = act.shape
    listed = parent_pick.shape[0]
    shapes = ((count, channels), (halo, channels), (halo, channels), (listed, cur.shape[1]))
    return pl.pallas_call(
        down_grad_kernel,
        out_shape=tuple(jax.ShapeDtypeStruct(shape, BF) for shape in shapes),
        in_specs=[VMEM] * 6,
        out_specs=(VMEM,) * 4,
        scratch_shapes=[pltpu.VMEM((listed, channels), BF)],
        compiler_params=pltpu.CompilerParams(vmem_limit_bytes=16 << 20),
        cost_estimate=cost(1 << 30, 4 << 20),
        name="down_grad",
    )(prev, cur, act, w, pick, parent_pick)


def down_weight_kernel(core, chosen, gath, ahead, both, send):
    channels, listed = chosen.shape
    pairs, shard = send.shape[:2]
    children = 2 * pairs * shard // channels
    slots = listed // children
    for c in range(children):
        mine = pl.ds(c * slots, slots)
        place(both, dot(chosen[:, mine], gath[mine, :]), c * channels, core[0])
    send[...] = both[1].astype(BF)


def down_weight(core, chosen, gath, ahead, shard, total):
    return pl.pallas_call(
        down_weight_kernel,
        out_shape=halves(total, shard),
        in_specs=[SMEM, VMEM, VMEM, VMEM],
        out_specs=(VMEM, VMEM),
        compiler_params=pltpu.CompilerParams(vmem_limit_bytes=16 << 20),
        cost_estimate=cost(1 << 30, 6 << 20),
        name="down_weight",
    )(core, chosen, gath, ahead)


def conv_plan(kernel, channels, quarter):
    size = kernel * channels // 4
    plan, row = [], quarter * size
    while row < (quarter + 1) * size:
        k, first = divmod(row, channels)
        last = min(channels, (quarter + 1) * size - k * channels)
        plan.append((k, first, last, row - quarter * size))
        row += last - first
    return plan


def conv_kernel(plan, begun, *refs):
    core, src, tgt, tab, before, own, after, feats_t, w, *rest = refs
    if begun:
        partial, *rest = rest
    grad, both, send, ext, acc, col0, col1 = rest
    cols = (col0, col1)
    slots = src.shape[0]
    blocks, rows, channels = col0.shape
    count = feats_t.shape[1]
    at = 0
    for piece in (before, own, after):
        for b in range(piece.shape[0] // rows):
            ext[at] = piece[pl.ds(b * rows, rows), :]
            at += 1
    acc[...] = partial[...] if begun else jnp.zeros_like(acc)
    lanes = lax.broadcasted_iota(jnp.int32, (rows, rows), 1).astype(jnp.int16)
    one, zero = jnp.ones((), BF), jnp.zeros((), BF)

    def gather(k, col):
        col[...] = jnp.zeros_like(col)
        for p in range(slots):
            q = k * slots + p
            index = jnp.broadcast_to(tab[:, q : q + 1], (rows, rows)).astype(jnp.int16)
            pick = jnp.where(index == lanes, one, zero)
            piece = dot(pick, ext[tgt[p, k]]).astype(BF)
            owner = src[p, k]
            col[owner] = col[owner] + piece

    gather(plan[0][0], cols[0])
    for at, (k, first, last, out) in enumerate(plan):
        if at + 1 < len(plan):
            gather(plan[at + 1][0], cols[(at + 1) % 2])
        column = cols[at % 2][...].reshape(count, channels)
        place(both, dot(feats_t[pl.ds(first, last - first), :], column), out, core[0])
        if first == 0:
            acc[...] += dot_nt(column, w[pl.ds(k * channels, channels), :])
    grad[...] = acc[...].astype(grad.dtype)
    send[...] = both[1].astype(BF)


def conv(core, src, tgt, tab, before, own, after, feats_t, w, quarter, shard, partial, final):
    channels, count = feats_t.shape
    kernel = w.shape[0] // channels
    rows = tab.shape[0]
    begun = partial is not None
    total = (kernel * channels // 4, channels)
    ext_rows = count + before.shape[0] + after.shape[0]
    block = (rows, channels)
    grad = jax.ShapeDtypeStruct((count, channels), BF if final else F32)
    return pl.pallas_call(
        functools.partial(conv_kernel, conv_plan(kernel, channels, quarter), begun),
        out_shape=(grad,) + halves(total, shard),
        in_specs=[SMEM] * 3 + [VMEM] * (6 + begun),
        out_specs=(VMEM,) * 3,
        scratch_shapes=[
            pltpu.VMEM((ext_rows // rows,) + block, BF),
            pltpu.VMEM((count, channels), F32),
            pltpu.VMEM((count // rows,) + block, BF),
            pltpu.VMEM((count // rows,) + block, BF),
        ],
        compiler_params=pltpu.CompilerParams(vmem_limit_bytes=16 << 20),
        cost_estimate=cost(6 << 30, 5 << 20),
        name="conv",
    )(core, src, tgt, tab, before, own, after, feats_t, w, *([partial] if begun else []))


def moved(x, peers, to):
    pairs = [(i, to(i)) for i in range(peers)]
    return lax.ppermute(x, "space", [(i, j) for i, j in pairs if j is not None and 0 <= j < peers])


def taken(x, axis, digit):
    return lax.dynamic_index_in_dim(x, digit, axis=axis, keepdims=False)


def low_steps(bits):
    left = [list(range(bits - 1, -1, -1)) for core in range(2)]
    steps = []
    for j in range(bits):
        by = (j, (j + bits // 2) % bits)
        steps.append((by, [left[core].index(by[core]) for core in range(2)]))
        for core in range(2):
            left[core].remove(by[core])
    return steps


def fold_low(parts, me, step):
    core = me % 2
    by, axes = step
    bit = jnp.where(core == 0, me >> (1 + by[0]), me >> (1 + by[1])) % 2

    def half(x, digit):
        if axes[0] == axes[1]:
            return taken(x, 1 + axes[0], digit)
        return jnp.where(core == 0, taken(x, 1 + axes[0], digit), taken(x, 1 + axes[1], digit))

    def piece(digit):
        pieces = [half(kept, digit) + half(got, digit).astype(F32) for kept, got in parts]
        return jnp.concatenate(pieces, 0) if len(pieces) > 1 else pieces[0]

    return piece(bit), piece(1 - bit).astype(BF), lambda i: i ^ (2 << by[i % 2])


def fold_bit(keep, got, me, peers, stride, first):
    bit = me // stride % 2
    axis = keep.ndim - 3

    def piece(digit):
        return taken(keep, axis, digit) + taken(got, axis, digit).astype(F32)

    mine = bit ^ first
    sent = piece(1 - mine).astype(BF)
    return piece(mine), moved(sent, peers, lambda i: i ^ stride)


def per_device(
    feats,
    pre_act,
    coarse_grad,
    w_sub,
    w_down,
    pair_src,
    pair_tgt,
    pair_rows,
    down_rows,
    down_parent,
):
    peers = lax.axis_size("space")
    me = lax.axis_index("space")
    row_count, channels = feats.shape
    block_rows = pair_rows.shape[-1]
    out_width = coarse_grad.shape[1]
    kernel = pair_src.shape[1]
    children = down_rows.shape[1]
    scale = 1.0 / math.sqrt(peers * row_count)
    bits = (peers // 8).bit_length() - 1
    steps = low_steps(bits)
    near, far = peers // 4, peers // 2

    previous = moved(coarse_grad[-block_rows:], peers, lambda i: i + 1)
    feats_t, act, tab, pick, parent_pick, chosen = prep(
        feats,
        pre_act,
        pair_rows[0].reshape(-1, block_rows),
        down_rows[0],
        down_parent[0],
        block_rows + coarse_grad.shape[0],
    )
    grad_pre, head, tail, gathered = down_grad(
        previous, coarse_grad, act, w_down, pick, parent_pick, HB * block_rows
    )
    before = moved(tail, peers, lambda i: i + 1)
    after = moved(head, peers, lambda i: i - 1)
    src = pair_src[0].T
    tgt = pair_tgt[0].T
    core = (me % 2).reshape(1)
    pinned = lax.optimization_barrier

    def across(x):
        return moved(x, peers, lambda i: i ^ 1)

    def spread(both, got, high):
        shape = (high,) + (2,) * bits + got.shape[-2:]
        return both[0].reshape(shape), got.reshape(shape)

    def quarter(number, partial=None, final=False):
        return conv(
            core, src, tgt, tab, before, grad_pre, after, feats_t, w_sub,
            number, kernel * channels // peers, partial, final,
        )

    down, down_send = down_weight(
        core,
        chosen,
        gathered,
        w_sub,
        children * channels // peers,
        (children * channels, out_width),
    )
    before, after, down_send = pinned((before, after, down_send))
    down_got = across(down_send)
    partial, sub0, send0 = quarter(0)
    partial, sub0, send0, down_got = pinned((partial, sub0, send0, down_got))

    got0 = across(send0)
    down, down_send, to = fold_low([spread(down, down_got, 4)], me, steps[0])
    down_got = moved(down_send, peers, to)
    partial, sub3, send3 = quarter(3, partial)
    partial, sub3, send3, got0, down, down_got = pinned(
        (partial, sub3, send3, got0, down, down_got)
    )

    got3 = across(send3)
    for step in steps[1:]:
        down, down_send, to = fold_low([(down, down_got)], me, step)
        down_got = moved(down_send, peers, to)
    partial, sub1, send1 = quarter(1, partial)
    partial, sub1, send1, got3, down, down_got = pinned(
        (partial, sub1, send1, got3, down, down_got)
    )

    got1 = across(send1)
    outer, outer_send, to = fold_low([spread(sub0, got0, 1), spread(sub3, got3, 1)], me, steps[0])
    outer_got = moved(outer_send, peers, to)
    down, down_got = (x.reshape((2, 2) + x.shape[-2:]) for x in (down, down_got))
    down, down_got = fold_bit(down, down_got, me, peers, near, 0)
    grad_in, sub2, send2 = quarter(2, partial, True)
    grad_in, sub2, send2, got1, outer, outer_got, down, down_got = pinned(
        (grad_in, sub2, send2, got1, outer, outer_got, down, down_got)
    )

    got2 = across(send2)
    for step in steps[1:]:
        outer, outer_send, to = fold_low([(outer, outer_got)], me, step)
        outer_got = moved(outer_send, peers, to)
    down, down_got = fold_bit(down, down_got, me, peers, far, 0)
    got2, outer, outer_got, down, down_got = pinned((got2, outer, outer_got, down, down_got))

    inner, inner_send, to = fold_low([spread(sub1, got1, 1), spread(sub2, got2, 1)], me, steps[0])
    inner_got = moved(inner_send, peers, to)
    outer, outer_got = fold_bit(outer, outer_got, me, peers, near, 0)
    down_sum = (down + down_got.astype(F32)) * scale
    inner, inner_got, outer, outer_got, down_sum = pinned(
        (inner, inner_got, outer, outer_got, down_sum)
    )

    for step in steps[1:]:
        inner, inner_send, to = fold_low([(inner, inner_got)], me, step)
        inner_got = moved(inner_send, peers, to)
    inner, inner_got = fold_bit(inner, inner_got, me, peers, near, 1)

    digit = me // near
    is_outer = (digit == 0) | (digit == 3)
    outer_sum = outer + outer_got.astype(F32)
    inner_sum = inner + inner_got.astype(F32)
    sent = jnp.where(is_outer, inner_sum, outer_sum).astype(BF)
    sub_sum = jnp.where(is_outer, outer_sum, inner_sum)
    sub_sum = sub_sum + moved(sent, peers, lambda i: i ^ far).astype(F32)
    return (grad_in, sub_sum.reshape(-1) * scale, down_sum)


def solution(mesh):
    rows = ("scene", "space")
    placed = (
        P(rows, None),
        P(rows, None),
        P(rows, None),
        P(),
        P(),
        P(rows, None, None),
        P(rows, None, None),
        P(rows, None, None, None),
        P(rows, None, None),
        P(rows, None, None),
    )
    return jax.shard_map(
        per_device,
        mesh=mesh,
        in_specs=placed,
        out_specs=(P(rows, None), P(rows), P(rows, None)),
        check_vma=False,
    )
```

```python
import functools
import math

import jax
import jax.numpy as jnp
from jax import lax
from jax.experimental import pallas as pl
from jax.experimental.pallas import tpu as pltpu
from jax.sharding import PartitionSpec as P

HB = 2
BF = jnp.bfloat16
F32 = jnp.float32


def dot(a, b):
    return lax.dot_general(a, b, (((1,), (0,)), ((), ())), preferred_element_type=F32)


def dot_nt(a, b):
    return lax.dot_general(a, b, (((1,), (1,)), ((), ())), preferred_element_type=F32)


def one_hot(index, shape, axis):
    return jnp.where(index == lax.broadcasted_iota(jnp.int32, shape, axis), 1.0, 0.0).astype(BF)


def segments(first, count, shard):
    row, cuts = first, []
    while row < first + count:
        number, inside = divmod(row, shard)
        rows = min(shard - inside, first + count - row)
        cuts.append((row - first, number, inside, rows))
        row += rows
    return cuts


def place(both, value, first, core):
    for at, number, inside, rows in segments(first, value.shape[0], both.shape[2]):
        both[(number % 2) ^ core, number // 2, pl.ds(inside, rows), :] = value[at : at + rows]


def halves(total, shard):
    shape = (total[0] // (2 * shard), shard, total[1])
    kinds = (jax.ShapeDtypeStruct(shape, F32), jax.ShapeDtypeStruct(shape, BF))
    return kinds, pltpu.VMEM((2,) + shape, F32)


def part(both, keep, send):
    keep[...] = both[0]
    send[...] = both[1].astype(BF)


def identity(size):
    return one_hot(lax.broadcasted_iota(jnp.int32, (size, size), 0), (size, size), 1)


def turned(table):
    values = table.astype(F32).astype(BF)
    return dot_nt(identity(table.shape[1]), values).astype(jnp.int32)


VMEM = pl.BlockSpec(memory_space=pltpu.VMEM)
SMEM = pl.BlockSpec(memory_space=pltpu.SMEM)


SMALL = pl.CostEstimate(flops=1 << 20, bytes_accessed=1 << 10, transcendentals=0)


def prep_kernel(pre, rows, parents, w, cur, act, pick, parent_pick, chosen):
    children, slots = rows.shape
    count, channels = pre.shape
    for c in range(children):
        pick[:, pl.ds(c * slots, slots)] = one_hot(rows[c : c + 1, :], (count, slots), 0)
    columns = turned(parents[...])
    for c in range(children):
        parent_pick[pl.ds(c * slots, slots), :] = one_hot(
            columns[:, c : c + 1], (slots, parent_pick.shape[1]), 1
        )
    act[...] = jnp.maximum(pre[...], jnp.zeros((), BF))
    act_t = dot_nt(identity(channels), act[...]).astype(BF)
    chosen[...] = dot(act_t, pick[...]).astype(BF)


def prep(pre, rows, parents, w, cur, parent_rows):
    count, channels = pre.shape
    children, slots = rows.shape
    shapes = (
        (count, channels),
        (count, children * slots),
        (children * slots, parent_rows),
        (channels, children * slots),
    )
    return pl.pallas_call(
        prep_kernel,
        out_shape=tuple(jax.ShapeDtypeStruct(shape, BF) for shape in shapes),
        in_specs=[VMEM] * 5,
        out_specs=(VMEM,) * len(shapes),
        compiler_params=pltpu.CompilerParams(vmem_limit_bytes=16 << 20),
        cost_estimate=SMALL,
        name="prep",
    )(pre, rows, parents, w, cur)


def down_grad_kernel(prev, cur, act, w, pick, parent_pick, gpre, head, tail, gath, contrib):
    count, channels = act.shape
    children = w.shape[0] // channels
    slots = gath.shape[0] // children
    ext = jnp.concatenate([prev[...], cur[...]], 0)
    for c in range(children):
        mine = pl.ds(c * slots, slots)
        got = dot(parent_pick[mine, :], ext).astype(BF)
        gath[mine, :] = got
        contrib[mine, :] = dot_nt(got, w[pl.ds(c * channels, channels), :]).astype(BF)
    grad = dot(pick[...], contrib[...])
    masked = jnp.where(act[...].astype(F32) > 0, grad, 0.0).astype(BF)
    gpre[...] = masked
    halo = head.shape[0]
    head[...] = masked[:halo]
    tail[...] = masked[count - halo :]


def down_grad(prev, cur, act, w, pick, parent_pick, halo):
    count, channels = act.shape
    listed = parent_pick.shape[0]
    shapes = ((count, channels), (halo, channels), (halo, channels), (listed, cur.shape[1]))
    return pl.pallas_call(
        down_grad_kernel,
        out_shape=tuple(jax.ShapeDtypeStruct(shape, BF) for shape in shapes),
        in_specs=[VMEM] * 6,
        out_specs=(VMEM,) * 4,
        scratch_shapes=[pltpu.VMEM((listed, channels), BF)],
        compiler_params=pltpu.CompilerParams(vmem_limit_bytes=16 << 20),
        cost_estimate=SMALL,
        name="down_grad",
    )(prev, cur, act, w, pick, parent_pick)


def down_weight_kernel(core, chosen, gath, ahead, keep, send, both):
    channels, listed = chosen.shape
    pairs, shard = send.shape[:2]
    children = 2 * pairs * shard // channels
    slots = listed // children
    for c in range(children):
        mine = pl.ds(c * slots, slots)
        place(both, dot(chosen[:, mine], gath[mine, :]), c * channels, core[0])
    part(both, keep, send)


def down_weight(core, chosen, gath, ahead, shard, total):
    kinds, both = halves(total, shard)
    return pl.pallas_call(
        down_weight_kernel,
        out_shape=kinds,
        in_specs=[SMEM, VMEM, VMEM, VMEM],
        out_specs=(VMEM, VMEM),
        scratch_shapes=[both],
        compiler_params=pltpu.CompilerParams(vmem_limit_bytes=16 << 20),
        cost_estimate=SMALL,
        name="down_weight",
    )(core, chosen, gath, ahead)


def conv_plan(kernel, channels, quarters):
    size = kernel * channels // 4
    plan, out = [], 0
    for quarter in quarters:
        row = quarter * size
        while row < (quarter + 1) * size:
            k, first = divmod(row, channels)
            last = min(channels, (quarter + 1) * size - k * channels)
            plan.append((k, first, last, out))
            out += last - first
            row += last - first
    return plan


def conv_kernel(plan, begun, *refs):
    core, src, tgt, pairs, before, own, after, feats, w, *rest = refs
    if begun:
        partial, *rest = rest
    grad, keep, send, both, ext, acc, col0, col1, feats_t, tab = rest
    cols = (col0, col1)
    slots = src.shape[0]
    blocks, rows, channels = col0.shape
    count = feats.shape[0]
    at = 0
    for piece in (before, own, after):
        for b in range(piece.shape[0] // rows):
            ext[at] = piece[pl.ds(b * rows, rows), :]
            at += 1
    tab[...] = turned(pairs[...])
    feats_t[...] = dot_nt(identity(channels), feats[...]).astype(BF)
    acc[...] = partial[...] if begun else jnp.zeros_like(acc)
    lanes = lax.broadcasted_iota(jnp.int32, (rows, rows), 1).astype(jnp.int16)
    one, zero = jnp.ones((), BF), jnp.zeros((), BF)

    def gather(k, col):
        col[...] = jnp.zeros_like(col)
        for p in range(slots):
            q = k * slots + p
            index = jnp.broadcast_to(tab[:, q : q + 1], (rows, rows)).astype(jnp.int16)
            pick = jnp.where(index == lanes, one, zero)
            piece = dot(pick, ext[tgt[p, k]]).astype(BF)
            owner = src[p, k]
            col[owner] = col[owner] + piece

    gather(plan[0][0], cols[0])
    for at, (k, first, last, out) in enumerate(plan):
        if at + 1 < len(plan):
            gather(plan[at + 1][0], cols[(at + 1) % 2])
        column = cols[at % 2][...].reshape(count, channels)
        place(both, dot(feats_t[pl.ds(first, last - first), :], column), out, core[0])
        if first == 0:
            acc[...] += dot_nt(column, w[pl.ds(k * channels, channels), :])
    grad[...] = acc[...].astype(grad.dtype)
    part(both, keep, send)


def conv(core, src, tgt, pairs, before, own, after, feats, w, quarters, shard, partial, final):
    count, channels = feats.shape
    kernel = w.shape[0] // channels
    rows = pairs.shape[1]
    begun = partial is not None
    kinds, both = halves((len(quarters) * kernel * channels // 4, channels), shard)
    ext_rows = count + before.shape[0] + after.shape[0]
    block = (rows, channels)
    grad = jax.ShapeDtypeStruct((count, channels), BF if final else F32)
    return pl.pallas_call(
        functools.partial(conv_kernel, conv_plan(kernel, channels, quarters), begun),
        out_shape=(grad,) + kinds,
        in_specs=[SMEM] * 3 + [VMEM] * (6 + begun),
        out_specs=(VMEM,) * 3,
        scratch_shapes=[
            both,
            pltpu.VMEM((ext_rows // rows,) + block, BF),
            pltpu.VMEM((count, channels), F32),
            pltpu.VMEM((count // rows,) + block, BF),
            pltpu.VMEM((count // rows,) + block, BF),
            pltpu.VMEM((channels, count), BF),
            pltpu.VMEM((rows, pairs.shape[0]), jnp.int32),
        ],
        compiler_params=pltpu.CompilerParams(vmem_limit_bytes=20 << 20),
        cost_estimate=SMALL,
        name="conv",
    )(core, src, tgt, pairs, before, own, after, feats, w, *([partial] if begun else []))


def moved(x, peers, to):
    pairs = [(i, to(i)) for i in range(peers)]
    return lax.ppermute(x, "space", [(i, j) for i, j in pairs if j is not None and 0 <= j < peers])


def taken(x, axis, digit):
    return lax.dynamic_index_in_dim(x, digit, axis=axis, keepdims=False)


def low_steps(bits):
    left = [list(range(bits - 1, -1, -1)) for core in range(2)]
    steps = []
    for j in range(bits):
        by = (j, (j + bits // 2) % bits)
        steps.append((by, [left[core].index(by[core]) for core in range(2)]))
        for core in range(2):
            left[core].remove(by[core])
    return steps


def fold_low(parts, me, step):
    core = me % 2
    by, axes = step
    bit = jnp.where(core == 0, me >> (1 + by[0]), me >> (1 + by[1])) % 2

    def half(x, digit):
        if axes[0] == axes[1]:
            return taken(x, 1 + axes[0], digit)
        return jnp.where(core == 0, taken(x, 1 + axes[0], digit), taken(x, 1 + axes[1], digit))

    def piece(digit):
        pieces = [half(kept, digit) + half(got, digit).astype(F32) for kept, got in parts]
        return jnp.concatenate(pieces, 0) if len(pieces) > 1 else pieces[0]

    return piece(bit), piece(1 - bit).astype(BF), lambda i: i ^ (2 << by[i % 2])


def fold_bit(keep, got, me, peers, stride, first):
    bit = me // stride % 2
    axis = keep.ndim - 3

    def piece(digit):
        return taken(keep, axis, digit) + taken(got, axis, digit).astype(F32)

    mine = bit ^ first
    sent = piece(1 - mine).astype(BF)
    return piece(mine), moved(sent, peers, lambda i: i ^ stride)


def per_device(
    feats,
    pre_act,
    coarse_grad,
    w_sub,
    w_down,
    pair_src,
    pair_tgt,
    pair_rows,
    down_rows,
    down_parent,
):
    peers = lax.axis_size("space")
    me = lax.axis_index("space")
    row_count, channels = feats.shape
    block_rows = pair_rows.shape[-1]
    out_width = coarse_grad.shape[1]
    kernel = pair_src.shape[1]
    children = down_rows.shape[1]
    scale = 1.0 / math.sqrt(peers * row_count)
    bits = (peers // 8).bit_length() - 1
    steps = low_steps(bits)
    near, far = peers // 4, peers // 2

    previous = moved(coarse_grad[-block_rows:], peers, lambda i: i + 1)
    act, pick, parent_pick, chosen = prep(
        pre_act,
        down_rows[0],
        down_parent[0],
        w_down,
        coarse_grad,
        block_rows + coarse_grad.shape[0],
    )
    grad_pre, head, tail, gathered = down_grad(
        previous, coarse_grad, act, w_down, pick, parent_pick, HB * block_rows
    )
    before = moved(tail, peers, lambda i: i + 1)
    after = moved(head, peers, lambda i: i - 1)
    src = pair_src[0].T
    tgt = pair_tgt[0].T
    core = (me % 2).reshape(1)
    pinned = lax.optimization_barrier

    def across(x):
        return moved(x, peers, lambda i: i ^ 1)

    def spread(kept, got, high):
        shape = (high,) + (2,) * bits + got.shape[-2:]
        return kept.reshape(shape), got.reshape(shape)

    pairs = pair_rows[0].reshape(-1, block_rows)
    shard = kernel * channels // peers

    def quarters(numbers, partial=None, final=False):
        return conv(
            core, src, tgt, pairs, before, grad_pre, after, feats, w_sub,
            numbers, shard, partial, final,
        )

    down, down_send = down_weight(
        core,
        chosen,
        gathered,
        w_sub,
        children * channels // peers,
        (children * channels, out_width),
    )
    before, after, down_send = pinned((before, after, down_send))
    down_got = across(down_send)
    partial, outer, outer_send = quarters((0, 3))
    partial, outer, outer_send, down_got = pinned((partial, outer, outer_send, down_got))

    outer_got = across(outer_send)
    down, down_send, to = fold_low([spread(down, down_got, 4)], me, steps[0])
    down_got = moved(down_send, peers, to)
    partial, sub1, send1 = quarters((1,), partial)
    partial, sub1, send1, outer_got = pinned((partial, sub1, send1, outer_got))

    got1 = across(send1)
    outer, outer_send, to = fold_low([spread(outer, outer_got, 2)], me, steps[0])
    outer_got = moved(outer_send, peers, to)
    grad_in, sub2, send2 = quarters((2,), partial, True)
    grad_in, sub2, send2, got1, outer, outer_got, down, down_got = pinned(
        (grad_in, sub2, send2, got1, outer, outer_got, down, down_got)
    )

    got2 = across(send2)
    for step in steps[1:]:
        outer, outer_send, to = fold_low([(outer, outer_got)], me, step)
        outer_got = moved(outer_send, peers, to)
        down, down_send, to = fold_low([(down, down_got)], me, step)
        down_got = moved(down_send, peers, to)
    inner, inner_send, to = fold_low([spread(sub1, got1, 1), spread(sub2, got2, 1)], me, steps[0])
    inner_got = moved(inner_send, peers, to)
    for step in steps[1:]:
        inner, inner_send, to = fold_low([(inner, inner_got)], me, step)
        inner_got = moved(inner_send, peers, to)
    down, down_got = (x.reshape((2, 2) + x.shape[-2:]) for x in (down, down_got))
    down, down_got = fold_bit(down, down_got, me, peers, near, 0)
    outer, outer_got = fold_bit(outer, outer_got, me, peers, near, 0)
    down, down_got = fold_bit(down, down_got, me, peers, far, 0)
    inner, inner_got = fold_bit(inner, inner_got, me, peers, near, 1)

    def last_step(kept, got, wanted):
        total = kept + got.astype(F32)
        to = lambda i: i ^ far if (i ^ far) // near in wanted else None
        return total + moved(total.astype(BF), peers, to).astype(F32)

    digit = me // near
    is_outer = (digit == 0) | (digit == 3)
    outer_sum = last_step(outer, outer_got, (0, 3))
    inner_sum = last_step(inner, inner_got, (1, 2))
    sub_sum = jnp.where(is_outer, outer_sum, inner_sum)
    down_sum = down + down_got.astype(F32)
    return (grad_in, sub_sum.reshape(-1) * scale, down_sum * scale)


def solution(mesh):
    rows = ("scene", "space")
    placed = (
        P(rows, None),
        P(rows, None),
        P(rows, None),
        P(),
        P(),
        P(rows, None, None),
        P(rows, None, None),
        P(rows, None, None, None),
        P(rows, None, None),
        P(rows, None, None),
    )
    return jax.shard_map(
        per_device,
        mesh=mesh,
        in_specs=placed,
        out_specs=(P(rows, None), P(rows), P(rows, None)),
        check_vma=False,
    )
```

```python
import functools
import math

import jax
import jax.numpy as jnp
from jax import lax
from jax.experimental import pallas as pl
from jax.experimental.pallas import tpu as pltpu
from jax.sharding import PartitionSpec as P

HB = 2
BF = jnp.bfloat16
F32 = jnp.float32


def dot(a, b):
    return lax.dot_general(a, b, (((1,), (0,)), ((), ())), preferred_element_type=F32)


def dot_nt(a, b):
    return lax.dot_general(a, b, (((1,), (1,)), ((), ())), preferred_element_type=F32)


def one_hot(index, shape, axis):
    return jnp.where(index == lax.broadcasted_iota(jnp.int32, shape, axis), 1.0, 0.0).astype(BF)


def segments(first, count, shard):
    row, cuts = first, []
    while row < first + count:
        number, inside = divmod(row, shard)
        rows = min(shard - inside, first + count - row)
        cuts.append((row - first, number, inside, rows))
        row += rows
    return cuts


def place(both, value, first, core):
    for at, number, inside, rows in segments(first, value.shape[0], both.shape[2]):
        both[(number % 2) ^ core, number // 2, pl.ds(inside, rows), :] = value[at : at + rows]


def halves(total, shard):
    shape = (total[0] // (2 * shard), shard, total[1])
    return (jax.ShapeDtypeStruct(shape, BF),) * 2, pltpu.VMEM((2,) + shape, F32)


def part(both, keep, send):
    keep[...] = both[0].astype(BF)
    send[...] = both[1].astype(BF)


def identity(size):
    return one_hot(lax.broadcasted_iota(jnp.int32, (size, size), 0), (size, size), 1)


def turned(table):
    values = table.astype(F32).astype(BF)
    return dot_nt(identity(table.shape[1]), values).astype(jnp.int32)


VMEM = pl.BlockSpec(memory_space=pltpu.VMEM)
SMEM = pl.BlockSpec(memory_space=pltpu.SMEM)


SMALL = pl.CostEstimate(flops=1 << 20, bytes_accessed=1 << 10, transcendentals=0)


def prep_kernel(pre, rows, parents, w_in, cur_in, act, pick, parent_pick, chosen, w, cur):
    children, slots = rows.shape
    count, channels = pre.shape
    columns = turned(parents[...])
    for c in range(children):
        mine = pl.ds(c * slots, slots)
        pick[:, mine] = one_hot(rows[c : c + 1, :], (count, slots), 0)
        parent_pick[mine, :] = one_hot(columns[:, c : c + 1], (slots, parent_pick.shape[1]), 1)
    act[...] = jnp.maximum(pre[...], jnp.zeros((), BF))
    turned_act = dot_nt(identity(channels), act[...]).astype(BF)
    chosen[...] = dot(turned_act, pick[...]).astype(BF)
    w[...] = w_in[...]
    cur[...] = cur_in[...]


def prep(pre, rows, parents, w, cur, parent_rows):
    count, channels = pre.shape
    children, slots = rows.shape
    shapes = (
        (count, channels),
        (count, children * slots),
        (children * slots, parent_rows),
        (channels, children * slots),
        w.shape,
        cur.shape,
    )
    return pl.pallas_call(
        prep_kernel,
        out_shape=tuple(jax.ShapeDtypeStruct(shape, BF) for shape in shapes),
        in_specs=[VMEM] * 5,
        out_specs=(VMEM,) * len(shapes),
        compiler_params=pltpu.CompilerParams(vmem_limit_bytes=16 << 20),
        cost_estimate=SMALL,
        name="prep",
    )(pre, rows, parents, w, cur)


def down_kernel(
    core, prev, act, pick, parent_pick, chosen, w, cur, head, tail, keep, send, both, gath, contrib
):
    count, channels = act.shape
    children = w.shape[0] // channels
    slots = pick.shape[1] // children
    halo = head.shape[0]
    ext = jnp.concatenate([prev[...], cur[...]], 0)
    own = [pl.ds(c * slots, slots) for c in range(children)]
    for c in range(children):
        got = dot(parent_pick[own[c], :], ext).astype(BF)
        gath[own[c], :] = got
        contrib[own[c], :] = dot_nt(got, w[pl.ds(c * channels, channels), :]).astype(BF)
    grad = dot(pick[...], contrib[...])
    masked = jnp.where(act[...].astype(F32) > 0, grad, 0.0).astype(BF)
    head[...] = masked[:halo]
    tail[...] = masked[count - halo :]
    for c in range(children):
        place(both, dot(chosen[:, own[c]], gath[own[c], :]), c * channels, core[0])
    part(both, keep, send)


def down(core, prev, prepared, halo, shard):
    act, pick, parent_pick, chosen, w, cur = prepared
    channels = act.shape[1]
    listed, width = pick.shape[1], cur.shape[1]
    kinds, both = halves(w.shape, shard)
    side = jax.ShapeDtypeStruct((halo, channels), BF)
    return pl.pallas_call(
        down_kernel,
        out_shape=(side, side) + kinds,
        in_specs=[SMEM] + [VMEM] * 7,
        out_specs=(VMEM,) * 4,
        scratch_shapes=[
            both,
            pltpu.VMEM((listed, width), BF),
            pltpu.VMEM((listed, channels), BF),
        ],
        compiler_params=pltpu.CompilerParams(vmem_limit_bytes=20 << 20),
        cost_estimate=SMALL,
        name="down",
    )(core, prev, *prepared)


def conv_plan(kernel, channels, quarters):
    size = kernel * channels // 4
    plan, out = [], 0
    for quarter in quarters:
        row = quarter * size
        while row < (quarter + 1) * size:
            k, first = divmod(row, channels)
            last = min(channels, (quarter + 1) * size - k * channels)
            plan.append((k, first, last, out))
            out += last - first
            row += last - first
    return plan


def turn_kernel(pairs, feats, w, tab, feats_t):
    tab[...] = turned(pairs[...])
    feats_t[...] = dot_nt(identity(feats.shape[1]), feats[...]).astype(BF)


def turn(pairs, feats, w):
    return pl.pallas_call(
        turn_kernel,
        out_shape=(
            jax.ShapeDtypeStruct(pairs.shape[::-1], jnp.int32),
            jax.ShapeDtypeStruct(feats.shape[::-1], BF),
        ),
        in_specs=[VMEM] * 3,
        out_specs=(VMEM,) * 2,
        compiler_params=pltpu.CompilerParams(vmem_limit_bytes=20 << 20),
        cost_estimate=SMALL,
        name="turn",
    )(pairs, feats, w)


def conv_kernel(plan, begun, *refs):
    core, src, tgt, before, head, tail, after, w, *rest = refs
    if begun:
        pairs, feats, partial, grad, keep, send, both, ext, acc, col0, col1, tab, feats_t = rest
        turn_kernel(pairs, feats, w, tab, feats_t)
    else:
        tab, feats_t, grad, keep, send, both, ext, acc, col0, col1 = rest
    cols = (col0, col1)
    slots = src.shape[0]
    blocks, rows, channels = col0.shape
    count = feats_t.shape[1]
    at = 0
    for piece in (before, head, tail, after):
        for b in range(piece.shape[0] // rows):
            ext[at] = piece[pl.ds(b * rows, rows), :]
            at += 1
    acc[...] = partial[...] if begun else jnp.zeros_like(acc)
    lanes = lax.broadcasted_iota(jnp.int32, (rows, rows), 1).astype(jnp.int16)
    one, zero = jnp.ones((), BF), jnp.zeros((), BF)

    def gather(k, col):
        col[...] = jnp.zeros_like(col)
        for p in range(slots):
            q = k * slots + p
            index = jnp.broadcast_to(tab[:, q : q + 1], (rows, rows)).astype(jnp.int16)
            pick = jnp.where(index == lanes, one, zero)
            piece = dot(pick, ext[tgt[p, k]]).astype(BF)
            owner = src[p, k]
            col[owner] = col[owner] + piece

    gather(plan[0][0], cols[0])
    for at, (k, first, last, out) in enumerate(plan):
        if at + 1 < len(plan):
            gather(plan[at + 1][0], cols[(at + 1) % 2])
        column = cols[at % 2][...].reshape(count, channels)
        place(both, dot(feats_t[pl.ds(first, last - first), :], column), out, core[0])
        if first == 0:
            acc[...] += dot_nt(column, w[pl.ds(k * channels, channels), :])
    grad[...] = acc[...].astype(grad.dtype)
    part(both, keep, send)


def conv(core, src, tgt, sides, w, tables, quarters, shard, partial):
    begun = partial is not None
    shapes = [x.shape if begun else x.shape[::-1] for x in tables]
    (listed, rows), (count, channels) = shapes
    kernel = w.shape[0] // channels
    kinds, both = halves((len(quarters) * kernel * channels // 4, channels), shard)
    ext_rows = sum(side.shape[0] for side in sides)
    block = (rows, channels)
    grad = jax.ShapeDtypeStruct((count, channels), BF if begun else F32)
    operands = (core, src, tgt, *sides, w, *tables) + ((partial,) if begun else ())
    return pl.pallas_call(
        functools.partial(conv_kernel, conv_plan(kernel, channels, quarters), begun),
        out_shape=(grad,) + kinds,
        in_specs=[SMEM] * 3 + [VMEM] * (len(operands) - 3),
        out_specs=(VMEM,) * 3,
        scratch_shapes=[
            both,
            pltpu.VMEM((ext_rows // rows,) + block, BF),
            pltpu.VMEM((count, channels), F32),
            pltpu.VMEM((count // rows,) + block, BF),
            pltpu.VMEM((count // rows,) + block, BF),
        ]
        + [
            pltpu.VMEM((rows, listed), jnp.int32),
            pltpu.VMEM((channels, count), BF),
        ]
        * begun,
        compiler_params=pltpu.CompilerParams(vmem_limit_bytes=24 << 20),
        cost_estimate=SMALL,
        name="conv",
    )(*operands)


def moved(x, peers, to):
    pairs = [(i, to(i)) for i in range(peers)]
    return lax.ppermute(x, "space", [(i, j) for i, j in pairs if j is not None and 0 <= j < peers])


def moved_together(x, to_x, y, to_y, peers):
    if any(to_x(i) != to_y(i) for i in range(peers)):
        return moved(x, peers, to_x), moved(y, peers, to_y)
    rows = x.shape[-2:]
    flat = [z.reshape((-1,) + rows) for z in (x, y)]
    got = moved(jnp.concatenate(flat, 0), peers, to_x)
    cut = flat[0].shape[0]
    return got[:cut].reshape(x.shape), got[cut:].reshape(y.shape)


def taken(x, axis, digit):
    return lax.dynamic_index_in_dim(x, digit, axis=axis, keepdims=False)


def low_steps(bits):
    left = [list(range(bits - 1, -1, -1)) for core in range(2)]
    steps = []
    for j in range(bits):
        by = (j, (j + bits // 2) % bits)
        steps.append((by, [left[core].index(by[core]) for core in range(2)]))
        for core in range(2):
            left[core].remove(by[core])
    return steps


def fold_low(parts, me, step):
    core = me % 2
    by, axes = step
    bit = jnp.where(core == 0, me >> (1 + by[0]), me >> (1 + by[1])) % 2

    def half(x, digit):
        if axes[0] == axes[1]:
            return taken(x, 1 + axes[0], digit)
        return jnp.where(core == 0, taken(x, 1 + axes[0], digit), taken(x, 1 + axes[1], digit))

    def piece(digit):
        pieces = [half(kept, digit).astype(F32) + half(got, digit).astype(F32) for kept, got in parts]
        return jnp.concatenate(pieces, 0) if len(pieces) > 1 else pieces[0]

    return piece(bit), piece(1 - bit).astype(BF), lambda i: i ^ (2 << by[i % 2])


def fold_bit(keep, got, me, peers, stride, first):
    bit = me // stride % 2
    axis = keep.ndim - 3

    def piece(digit):
        return taken(keep, axis, digit) + taken(got, axis, digit).astype(F32)

    mine = bit ^ first
    sent = piece(1 - mine).astype(BF)
    return piece(mine), moved(sent, peers, lambda i: i ^ stride)


def per_device(
    feats,
    pre_act,
    coarse_grad,
    w_sub,
    w_down,
    pair_src,
    pair_tgt,
    pair_rows,
    down_rows,
    down_parent,
):
    peers = lax.axis_size("space")
    me = lax.axis_index("space")
    row_count, channels = feats.shape
    block_rows = pair_rows.shape[-1]
    out_width = coarse_grad.shape[1]
    kernel = pair_src.shape[1]
    children = down_rows.shape[1]
    scale = 1.0 / math.sqrt(peers * row_count)
    bits = (peers // 8).bit_length() - 1
    steps = low_steps(bits)
    near, far = peers // 4, peers // 2

    halo = HB * block_rows
    core = (me % 2).reshape(1)
    pinned = lax.optimization_barrier
    other_way = [((b, a), [y, x]) for (a, b), (x, y) in steps]

    def across(x):
        return moved(x, peers, lambda i: i ^ 1)

    def spread(kept, got, high):
        shape = (high,) + (2,) * bits + got.shape[-2:]
        return kept.reshape(shape), got.reshape(shape)

    previous = moved(coarse_grad[-block_rows:], peers, lambda i: i + 1)
    prepared = prep(
        pre_act,
        down_rows[0],
        down_parent[0],
        w_down,
        coarse_grad,
        block_rows + coarse_grad.shape[0],
    )
    head, tail, low, low_send = down(
        core, previous, prepared, halo, children * channels // peers
    )

    before = moved(tail, peers, lambda i: i + 1)
    after = moved(head, peers, lambda i: i - 1)
    low_got = across(low_send)
    pairs = pair_rows[0].reshape(-1, block_rows)
    tables = turn(pairs, feats, w_sub)
    before, after, tables, low, low_got = pinned((before, after, tables, low, low_got))
    sides = (before, head, tail, after)
    shard = kernel * channels // peers

    def quarters(numbers, tables, partial=None):
        src, tgt = pair_src[0].T, pair_tgt[0].T
        return conv(core, src, tgt, sides, w_sub, tables, numbers, shard, partial)

    low, low_send, to = fold_low([spread(low, low_got, 4)], me, steps[0])
    low_got = moved(low_send, peers, to)
    partial, outer, outer_send = quarters((0, 3), tables)
    partial, outer, outer_send, low, low_got = pinned((partial, outer, outer_send, low, low_got))

    outer_got = across(outer_send)
    for step in steps[1:]:
        low, low_send, to = fold_low([(low, low_got)], me, step)
        low_got = moved(low_send, peers, to)
    grad_in, inner, inner_send = quarters((1, 2), (pairs, feats), partial)
    grad_in, inner, inner_send, outer, outer_got, low, low_got = pinned(
        (grad_in, inner, inner_send, outer, outer_got, low, low_got)
    )

    inner_got = across(inner_send)
    outer, outer_send, outer_to = fold_low([spread(outer, outer_got, 2)], me, other_way[0])
    for step in other_way[1:]:
        outer_got = moved(outer_send, peers, outer_to)
        outer, outer_send, outer_to = fold_low([(outer, outer_got)], me, step)
    low, low_got = (x.reshape((2, 2) + x.shape[-2:]) for x in (low, low_got))
    low, low_got = fold_bit(low, low_got, me, peers, near, 0)

    inner, inner_send, inner_to = fold_low([spread(inner, inner_got, 2)], me, steps[0])
    outer_got, inner_got = moved_together(outer_send, outer_to, inner_send, inner_to, peers)
    low, low_got = fold_bit(low, low_got, me, peers, far, 0)

    for step in steps[1:]:
        inner, inner_send, to = fold_low([(inner, inner_got)], me, step)
        inner_got = moved(inner_send, peers, to)
    outer, outer_got = fold_bit(outer, outer_got, me, peers, near, 0)
    inner, inner_got = fold_bit(inner, inner_got, me, peers, near, 1)

    def last_step(kept, got, wanted):
        total = kept + got.astype(F32)
        to = lambda i: i ^ far if (i ^ far) // near in wanted else None
        return total + moved(total.astype(BF), peers, to).astype(F32)

    digit = me // near
    is_outer = (digit == 0) | (digit == 3)
    outer_sum = last_step(outer, outer_got, (0, 3))
    inner_sum = last_step(inner, inner_got, (1, 2))
    sub_sum = jnp.where(is_outer, outer_sum, inner_sum)
    low_sum = low + low_got.astype(F32)
    return (grad_in, sub_sum.reshape(-1) * scale, low_sum * scale)


def solution(mesh):
    rows = ("scene", "space")
    placed = (
        P(rows, None),
        P(rows, None),
        P(rows, None),
        P(),
        P(),
        P(rows, None, None),
        P(rows, None, None),
        P(rows, None, None, None),
        P(rows, None, None),
        P(rows, None, None),
    )
    return jax.shard_map(
        per_device,
        mesh=mesh,
        in_specs=placed,
        out_specs=(P(rows, None), P(rows), P(rows, None)),
        check_vma=False,
    )
```

```python
import functools
import math

import jax
import jax.numpy as jnp
from jax import lax
from jax.experimental import pallas as pl
from jax.experimental.pallas import tpu as pltpu
from jax.sharding import PartitionSpec as P

HB = 2
BF = jnp.bfloat16
F32 = jnp.float32


def dot(a, b):
    return lax.dot_general(a, b, (((1,), (0,)), ((), ())), preferred_element_type=F32)


def dot_nt(a, b):
    return lax.dot_general(a, b, (((1,), (1,)), ((), ())), preferred_element_type=F32)


def one_hot(index, shape, axis):
    return jnp.where(index == lax.broadcasted_iota(jnp.int32, shape, axis), 1.0, 0.0).astype(BF)


def segments(first, count, shard):
    row, cuts = first, []
    while row < first + count:
        number, inside = divmod(row, shard)
        rows = min(shard - inside, first + count - row)
        cuts.append((row - first, number, inside, rows))
        row += rows
    return cuts


def low_order(bits):
    return [[(j + core * (bits // 2)) % bits for j in range(bits)] for core in range(2)]


def position(number, me, bits, quarters):
    part, low = divmod(number, 2 << bits)
    core = low % 2
    at = core ^ (me & 1)
    for bit in low_order(bits)[core]:
        at = at * 2 + ((low >> (1 + bit) & 1) ^ (me >> (1 + bit) & 1))
    z = me >> (1 + bits)
    if len(quarters) == 4:
        at = at * 2 + ((part & 1) ^ (z & 1))
        return at * 2 + ((part >> 1) ^ (z >> 1))
    return at * 2 + (part ^ (z & 1) ^ (quarters[0] & 1))


def place(both, value, first, me, bits, quarters):
    for at, number, inside, rows in segments(first, value.shape[0], both.shape[1]):
        both[position(number, me, bits, quarters), pl.ds(inside, rows), :] = value[at : at + rows]


def halves(total, shard):
    count = total[0] // shard
    half = jax.ShapeDtypeStruct((count // 2, shard, total[1]), BF)
    return (half, half), pltpu.VMEM((count, shard, total[1]), F32)


def part(both, keep, send):
    half = keep.shape[0]
    keep[...] = both[:half].astype(BF)
    send[...] = both[half:].astype(BF)


def identity(size):
    return one_hot(lax.broadcasted_iota(jnp.int32, (size, size), 0), (size, size), 1)


def turned(table):
    values = table.astype(F32).astype(BF)
    return dot_nt(identity(table.shape[1]), values).astype(jnp.int32)


VMEM = pl.BlockSpec(memory_space=pltpu.VMEM)
SMEM = pl.BlockSpec(memory_space=pltpu.SMEM)


SMALL = pl.CostEstimate(flops=1 << 20, bytes_accessed=1 << 10, transcendentals=0)


def prep_kernel(pre, rows, parents, w_in, cur_in, act, pick, parent_pick, chosen, w, cur):
    children, slots = rows.shape
    count, channels = pre.shape
    columns = turned(parents[...])
    for c in range(children):
        mine = pl.ds(c * slots, slots)
        pick[:, mine] = one_hot(rows[c : c + 1, :], (count, slots), 0)
        parent_pick[mine, :] = one_hot(columns[:, c : c + 1], (slots, parent_pick.shape[1]), 1)
    act[...] = jnp.maximum(pre[...], jnp.zeros((), BF))
    turned_act = dot_nt(identity(channels), act[...]).astype(BF)
    chosen[...] = dot(turned_act, pick[...]).astype(BF)
    w[...] = w_in[...]
    cur[...] = cur_in[...]


def prep(pre, rows, parents, w, cur, parent_rows):
    count, channels = pre.shape
    children, slots = rows.shape
    shapes = (
        (count, channels),
        (count, children * slots),
        (children * slots, parent_rows),
        (channels, children * slots),
        w.shape,
        cur.shape,
    )
    return pl.pallas_call(
        prep_kernel,
        out_shape=tuple(jax.ShapeDtypeStruct(shape, BF) for shape in shapes),
        in_specs=[VMEM] * 5,
        out_specs=(VMEM,) * len(shapes),
        compiler_params=pltpu.CompilerParams(vmem_limit_bytes=16 << 20),
        cost_estimate=SMALL,
        name="prep",
    )(pre, rows, parents, w, cur)


def down_kernel(
    bits, me, prev, act, pick, parent_pick, chosen, w, cur, head, tail, keep, send, both, gath, contrib
):
    count, channels = act.shape
    children = w.shape[0] // channels
    slots = pick.shape[1] // children
    halo = head.shape[0]
    ext = jnp.concatenate([prev[...], cur[...]], 0)
    own = [pl.ds(c * slots, slots) for c in range(children)]
    for c in range(children):
        got = dot(parent_pick[own[c], :], ext).astype(BF)
        gath[own[c], :] = got
        contrib[own[c], :] = dot_nt(got, w[pl.ds(c * channels, channels), :]).astype(BF)
    grad = dot(pick[...], contrib[...])
    masked = jnp.where(act[...].astype(F32) > 0, grad, 0.0).astype(BF)
    head[...] = masked[:halo]
    tail[...] = masked[count - halo :]
    for c in range(children):
        value = dot(chosen[:, own[c]], gath[own[c], :])
        place(both, value, c * channels, me[0], bits, range(4))
    part(both, keep, send)


def down(bits, me, prev, prepared, halo, shard):
    act, pick, parent_pick, chosen, w, cur = prepared
    channels = act.shape[1]
    listed, width = pick.shape[1], cur.shape[1]
    kinds, both = halves(w.shape, shard)
    side = jax.ShapeDtypeStruct((halo, channels), BF)
    return pl.pallas_call(
        functools.partial(down_kernel, bits),
        out_shape=(side, side) + kinds,
        in_specs=[SMEM] + [VMEM] * 7,
        out_specs=(VMEM,) * 4,
        scratch_shapes=[
            both,
            pltpu.VMEM((listed, width), BF),
            pltpu.VMEM((listed, channels), BF),
        ],
        compiler_params=pltpu.CompilerParams(vmem_limit_bytes=20 << 20),
        cost_estimate=SMALL,
        name="down",
    )(me, prev, *prepared)


def conv_plan(kernel, channels, quarters):
    size = kernel * channels // 4
    plan, out = [], 0
    for quarter in quarters:
        row = quarter * size
        while row < (quarter + 1) * size:
            k, first = divmod(row, channels)
            last = min(channels, (quarter + 1) * size - k * channels)
            plan.append((k, first, last, out))
            out += last - first
            row += last - first
    return plan


def turn_kernel(pairs, feats, w, tab, feats_t):
    tab[...] = turned(pairs[...])
    feats_t[...] = dot_nt(identity(feats.shape[1]), feats[...]).astype(BF)


def turn(pairs, feats, w):
    return pl.pallas_call(
        turn_kernel,
        out_shape=(
            jax.ShapeDtypeStruct(pairs.shape[::-1], jnp.int32),
            jax.ShapeDtypeStruct(feats.shape[::-1], BF),
        ),
        in_specs=[VMEM] * 3,
        out_specs=(VMEM,) * 2,
        compiler_params=pltpu.CompilerParams(vmem_limit_bytes=20 << 20),
        cost_estimate=SMALL,
        name="turn",
    )(pairs, feats, w)


def conv_kernel(plan, bits, quarters, begun, *refs):
    me, src, tgt, before, head, tail, after, w, *rest = refs
    if begun:
        pairs, feats, partial, grad, keep, send, both, ext, acc, col0, col1, tab, feats_t = rest
        turn_kernel(pairs, feats, w, tab, feats_t)
    else:
        tab, feats_t, grad, keep, send, both, ext, acc, col0, col1 = rest
    cols = (col0, col1)
    slots = src.shape[0]
    blocks, rows, channels = col0.shape
    count = feats_t.shape[1]
    at = 0
    for piece in (before, head, tail, after):
        for b in range(piece.shape[0] // rows):
            ext[at] = piece[pl.ds(b * rows, rows), :]
            at += 1
    acc[...] = partial[...] if begun else jnp.zeros_like(acc)
    lanes = lax.broadcasted_iota(jnp.int32, (rows, rows), 1).astype(jnp.int16)
    one, zero = jnp.ones((), BF), jnp.zeros((), BF)

    def gather(k, col):
        col[...] = jnp.zeros_like(col)
        for p in range(slots):
            q = k * slots + p
            index = jnp.broadcast_to(tab[:, q : q + 1], (rows, rows)).astype(jnp.int16)
            pick = jnp.where(index == lanes, one, zero)
            piece = dot(pick, ext[tgt[p, k]]).astype(BF)
            owner = src[p, k]
            col[owner] = col[owner] + piece

    gather(plan[0][0], cols[0])
    for at, (k, first, last, out) in enumerate(plan):
        if at + 1 < len(plan):
            gather(plan[at + 1][0], cols[(at + 1) % 2])
        column = cols[at % 2][...].reshape(count, channels)
        value = dot(feats_t[pl.ds(first, last - first), :], column)
        place(both, value, out, me[0], bits, quarters)
        if first == 0:
            acc[...] += dot_nt(column, w[pl.ds(k * channels, channels), :])
    grad[...] = acc[...].astype(grad.dtype)
    part(both, keep, send)


def conv(bits, me, src, tgt, sides, w, tables, quarters, shard, partial):
    begun = partial is not None
    shapes = [x.shape if begun else x.shape[::-1] for x in tables]
    (listed, rows), (count, channels) = shapes
    kernel = w.shape[0] // channels
    kinds, both = halves((len(quarters) * kernel * channels // 4, channels), shard)
    ext_rows = sum(side.shape[0] for side in sides)
    block = (rows, channels)
    grad = jax.ShapeDtypeStruct((count, channels), BF if begun else F32)
    operands = (me, src, tgt, *sides, w, *tables) + ((partial,) if begun else ())
    return pl.pallas_call(
        functools.partial(
            conv_kernel, conv_plan(kernel, channels, quarters), bits, quarters, begun
        ),
        out_shape=(grad,) + kinds,
        in_specs=[SMEM] * 3 + [VMEM] * (len(operands) - 3),
        out_specs=(VMEM,) * 3,
        scratch_shapes=[
            both,
            pltpu.VMEM((ext_rows // rows,) + block, BF),
            pltpu.VMEM((count, channels), F32),
            pltpu.VMEM((count // rows,) + block, BF),
            pltpu.VMEM((count // rows,) + block, BF),
        ]
        + [
            pltpu.VMEM((rows, listed), jnp.int32),
            pltpu.VMEM((channels, count), BF),
        ]
        * begun,
        compiler_params=pltpu.CompilerParams(vmem_limit_bytes=24 << 20),
        cost_estimate=SMALL,
        name="conv",
    )(*operands)


def moved(x, peers, to):
    pairs = [(i, to(i)) for i in range(peers)]
    return lax.ppermute(x, "space", [(i, j) for i, j in pairs if j is not None and 0 <= j < peers])


def fold(kept, got):
    half = kept.shape[0] // 2
    total = kept.astype(F32) + got.astype(F32)
    return total[:half], total[half:].astype(BF)


def per_device(
    feats,
    pre_act,
    coarse_grad,
    w_sub,
    w_down,
    pair_src,
    pair_tgt,
    pair_rows,
    down_rows,
    down_parent,
):
    peers = lax.axis_size("space")
    me = lax.axis_index("space")
    row_count, channels = feats.shape
    block_rows = pair_rows.shape[-1]
    out_width = coarse_grad.shape[1]
    kernel = pair_src.shape[1]
    children = down_rows.shape[1]
    scale = 1.0 / math.sqrt(peers * row_count)
    bits = (peers // 8).bit_length() - 1
    near, far = peers // 4, peers // 2

    halo = HB * block_rows
    ident = me.reshape(1)
    pinned = lax.optimization_barrier
    low_bits = list(zip(*low_order(bits)))

    def across(x):
        return moved(x, peers, lambda i: i ^ 1)

    def xy(x, step):
        return moved(x, peers, lambda i: i ^ (2 << low_bits[step][i % 2]))

    def z_near(x):
        return moved(x, peers, lambda i: i ^ near)

    def z_far(x, wanted=(0, 1, 2, 3)):
        return moved(x, peers, lambda i: i ^ far if (i ^ far) // near in wanted else None)

    def middle(kept, got):
        kept, send = fold(kept, got)
        for step in range(1, bits - 1):
            kept, send = fold(kept, xy(send, step))
        return kept, send

    previous = moved(coarse_grad[-block_rows:], peers, lambda i: i + 1)
    prepared = prep(
        pre_act,
        down_rows[0],
        down_parent[0],
        w_down,
        coarse_grad,
        block_rows + coarse_grad.shape[0],
    )
    head, tail, low, low_send = down(
        bits, ident, previous, prepared, halo, children * channels // peers
    )

    before = moved(tail, peers, lambda i: i + 1)
    after = moved(head, peers, lambda i: i - 1)
    low_got = across(low_send)
    pairs = pair_rows[0].reshape(-1, block_rows)
    tables = turn(pairs, feats, w_sub)
    before, after, tables, low, low_got = pinned((before, after, tables, low, low_got))
    sides = (before, head, tail, after)
    shard = kernel * channels // peers

    def quarters(numbers, tables, partial=None):
        src, tgt = pair_src[0].T, pair_tgt[0].T
        return conv(bits, ident, src, tgt, sides, w_sub, tables, numbers, shard, partial)

    low, low_send = fold(low, low_got)
    low_got = xy(low_send, 0)
    partial, outer, outer_send = quarters((0, 3), tables)
    partial, outer, outer_send, low, low_got = pinned((partial, outer, outer_send, low, low_got))

    outer_got = across(outer_send)
    low, low_send = middle(low, low_got)
    low_got = xy(low_send, bits - 1)
    outer, outer_send = fold(outer, outer_got)
    partial, outer_send = pinned((partial, outer_send))
    outer_got = xy(outer_send, 0)
    grad_in, inner, inner_send = quarters((1, 2), (pairs, feats), partial)
    grad_in, inner, inner_send, outer, outer_got, low, low_got = pinned(
        (grad_in, inner, inner_send, outer, outer_got, low, low_got)
    )

    inner_got = across(inner_send)
    outer, outer_send = middle(outer, outer_got)
    outer_got = xy(outer_send, bits - 1)
    low, low_send = fold(low, low_got)
    low_got = z_near(low_send)
    inner, inner_send = fold(inner, inner_got)
    inner_got = xy(inner_send, 0)

    outer, outer_send = fold(outer, outer_got)
    outer_got = z_near(outer_send)
    low, low_send = fold(low, low_got)
    low_got = z_far(low_send)
    inner, inner_send = middle(inner, inner_got)
    inner_got = xy(inner_send, bits - 1)

    inner, inner_send = fold(inner, inner_got)
    inner_got = z_near(inner_send)

    def last_step(kept, got, wanted):
        total = kept + got.astype(F32)
        return total + z_far(total.astype(BF), wanted).astype(F32)

    digit = me // near
    is_outer = (digit == 0) | (digit == 3)
    outer_sum = last_step(outer, outer_got, (0, 3))
    inner_sum = last_step(inner, inner_got, (1, 2))
    sub_sum = jnp.where(is_outer, outer_sum, inner_sum)
    low_sum = (low + low_got.astype(F32)).reshape(-1, out_width)
    return (grad_in, sub_sum.reshape(-1) * scale, low_sum * scale)


def solution(mesh):
    rows = ("scene", "space")
    placed = (
        P(rows, None),
        P(rows, None),
        P(rows, None),
        P(),
        P(),
        P(rows, None, None),
        P(rows, None, None),
        P(rows, None, None, None),
        P(rows, None, None),
        P(rows, None, None),
    )
    return jax.shard_map(
        per_device,
        mesh=mesh,
        in_specs=placed,
        out_specs=(P(rows, None), P(rows), P(rows, None)),
        check_vma=False,
    )
```

```python
import functools
import math

import jax
import jax.numpy as jnp
from jax import lax
from jax.experimental import pallas as pl
from jax.experimental.pallas import tpu as pltpu
from jax.sharding import PartitionSpec as P

HB = 2
BF = jnp.bfloat16
F32 = jnp.float32


def dot(a, b):
    return lax.dot_general(a, b, (((1,), (0,)), ((), ())), preferred_element_type=F32)


def dot_nt(a, b):
    return lax.dot_general(a, b, (((1,), (1,)), ((), ())), preferred_element_type=F32)


def one_hot(index, shape, axis):
    return jnp.where(index == lax.broadcasted_iota(jnp.int32, shape, axis), 1.0, 0.0).astype(BF)


def segments(first, count, shard):
    row, cuts = first, []
    while row < first + count:
        number, inside = divmod(row, shard)
        rows = min(shard - inside, first + count - row)
        cuts.append((row - first, number, inside, rows))
        row += rows
    return cuts


def low_order(bits):
    return [[(j + core * (bits // 2)) % bits for j in range(bits)] for core in range(2)]


def position(number, me, bits, quarters):
    part, low = divmod(number, 2 << bits)
    core = low % 2
    at = core ^ (me & 1)
    for bit in low_order(bits)[core]:
        at = at * 2 + ((low >> (1 + bit) & 1) ^ (me >> (1 + bit) & 1))
    z = me >> (1 + bits)
    if len(quarters) == 4:
        at = at * 2 + ((part & 1) ^ (z & 1))
        return at * 2 + ((part >> 1) ^ (z >> 1))
    return at * 2 + (part ^ (z & 1) ^ (quarters[0] & 1))


def place(both, value, first, me, bits, quarters):
    for at, number, inside, rows in segments(first, value.shape[0], both.shape[1]):
        both[position(number, me, bits, quarters), pl.ds(inside, rows), :] = value[at : at + rows]


def halves(total, shard):
    count = total[0] // shard
    half = jax.ShapeDtypeStruct((count // 2, shard, total[1]), BF)
    return (half, half), pltpu.VMEM((count, shard, total[1]), F32)


def part(both, keep, send):
    half = keep.shape[0]
    keep[...] = both[:half].astype(BF)
    send[...] = both[half:].astype(BF)


def identity(size):
    return one_hot(lax.broadcasted_iota(jnp.int32, (size, size), 0), (size, size), 1)


def turned(table):
    values = table.astype(F32).astype(BF)
    return dot_nt(identity(table.shape[1]), values).astype(jnp.int32)


VMEM = pl.BlockSpec(memory_space=pltpu.VMEM)
SMEM = pl.BlockSpec(memory_space=pltpu.SMEM)


SMALL = pl.CostEstimate(flops=1 << 20, bytes_accessed=1 << 10, transcendentals=0)


def prep_kernel(pre, rows, parents, w_in, cur_in, act, pick, parent_pick, chosen, w, cur):
    children, slots = rows.shape
    count, channels = pre.shape
    columns = turned(parents[...])
    for c in range(children):
        mine = pl.ds(c * slots, slots)
        pick[:, mine] = one_hot(rows[c : c + 1, :], (count, slots), 0)
        parent_pick[mine, :] = one_hot(columns[:, c : c + 1], (slots, parent_pick.shape[1]), 1)
    act[...] = jnp.maximum(pre[...], jnp.zeros((), BF))
    turned_act = dot_nt(identity(channels), act[...]).astype(BF)
    chosen[...] = dot(turned_act, pick[...]).astype(BF)
    w[...] = w_in[...]
    cur[...] = cur_in[...]


def prep(pre, rows, parents, w, cur, parent_rows):
    count, channels = pre.shape
    children, slots = rows.shape
    shapes = (
        (count, channels),
        (count, children * slots),
        (children * slots, parent_rows),
        (channels, children * slots),
        w.shape,
        cur.shape,
    )
    return pl.pallas_call(
        prep_kernel,
        out_shape=tuple(jax.ShapeDtypeStruct(shape, BF) for shape in shapes),
        in_specs=[VMEM] * 5,
        out_specs=(VMEM,) * len(shapes),
        compiler_params=pltpu.CompilerParams(vmem_limit_bytes=16 << 20),
        cost_estimate=SMALL,
        name="prep",
    )(pre, rows, parents, w, cur)


def down_kernel(
    bits, me, prev, act, pick, parent_pick, chosen, w, cur, head, tail, keep, send, both, gath, contrib
):
    count, channels = act.shape
    children = w.shape[0] // channels
    slots = pick.shape[1] // children
    halo = head.shape[0]
    ext = jnp.concatenate([prev[...], cur[...]], 0)
    own = [pl.ds(c * slots, slots) for c in range(children)]
    for c in range(children):
        got = dot(parent_pick[own[c], :], ext).astype(BF)
        gath[own[c], :] = got
        contrib[own[c], :] = dot_nt(got, w[pl.ds(c * channels, channels), :]).astype(BF)
    grad = dot(pick[...], contrib[...])
    masked = jnp.where(act[...].astype(F32) > 0, grad, 0.0).astype(BF)
    head[...] = masked[:halo]
    tail[...] = masked[count - halo :]
    for c in range(children):
        value = dot(chosen[:, own[c]], gath[own[c], :])
        place(both, value, c * channels, me[0], bits, range(4))
    part(both, keep, send)


def down(bits, me, prev, prepared, halo, shard):
    act, pick, parent_pick, chosen, w, cur = prepared
    channels = act.shape[1]
    listed, width = pick.shape[1], cur.shape[1]
    kinds, both = halves(w.shape, shard)
    side = jax.ShapeDtypeStruct((halo, channels), BF)
    return pl.pallas_call(
        functools.partial(down_kernel, bits),
        out_shape=(side, side) + kinds,
        in_specs=[SMEM] + [VMEM] * 7,
        out_specs=(VMEM,) * 4,
        scratch_shapes=[
            both,
            pltpu.VMEM((listed, width), BF),
            pltpu.VMEM((listed, channels), BF),
        ],
        compiler_params=pltpu.CompilerParams(vmem_limit_bytes=20 << 20),
        cost_estimate=SMALL,
        name="down",
    )(me, prev, *prepared)


def conv_plan(kernel, channels, quarters):
    size = kernel * channels // 4
    plan, out = [], 0
    for quarter in quarters:
        row = quarter * size
        while row < (quarter + 1) * size:
            k, first = divmod(row, channels)
            last = min(channels, (quarter + 1) * size - k * channels)
            plan.append((k, first, last, out))
            out += last - first
            row += last - first
    return plan


def turn_kernel(pairs, feats, w, tab, feats_t):
    tab[...] = turned(pairs[...])
    feats_t[...] = dot_nt(identity(feats.shape[1]), feats[...]).astype(BF)


def turn(pairs, feats, w):
    return pl.pallas_call(
        turn_kernel,
        out_shape=(
            jax.ShapeDtypeStruct(pairs.shape[::-1], jnp.int32),
            jax.ShapeDtypeStruct(feats.shape[::-1], BF),
        ),
        in_specs=[VMEM] * 3,
        out_specs=(VMEM,) * 2,
        compiler_params=pltpu.CompilerParams(vmem_limit_bytes=20 << 20),
        cost_estimate=SMALL,
        name="turn",
    )(pairs, feats, w)


def conv_kernel(plan, bits, quarters, begun, *refs):
    me, src, tgt, before, head, tail, after, w, *rest = refs
    if begun:
        pairs, feats, partial, grad, keep, send, both, ext, acc, col0, col1, tab, feats_t = rest
        turn_kernel(pairs, feats, w, tab, feats_t)
    else:
        tab, feats_t, grad, keep, send, both, ext, acc, col0, col1 = rest
    cols = (col0, col1)
    slots = src.shape[0]
    blocks, rows, channels = col0.shape
    count = feats_t.shape[1]
    at = 0
    for piece in (before, head, tail, after):
        for b in range(piece.shape[0] // rows):
            ext[at] = piece[pl.ds(b * rows, rows), :]
            at += 1
    acc[...] = partial[...] if begun else jnp.zeros_like(acc)
    lanes = lax.broadcasted_iota(jnp.int32, (rows, rows), 1).astype(jnp.int16)
    one, zero = jnp.ones((), BF), jnp.zeros((), BF)

    def gather(k, col):
        col[...] = jnp.zeros_like(col)
        for p in range(slots):
            q = k * slots + p
            index = jnp.broadcast_to(tab[:, q : q + 1], (rows, rows)).astype(jnp.int16)
            pick = jnp.where(index == lanes, one, zero)
            piece = dot(pick, ext[tgt[p, k]]).astype(BF)
            owner = src[p, k]
            col[owner] = col[owner] + piece

    gather(plan[0][0], cols[0])
    for at, (k, first, last, out) in enumerate(plan):
        if at + 1 < len(plan):
            gather(plan[at + 1][0], cols[(at + 1) % 2])
        column = cols[at % 2][...].reshape(count, channels)
        value = dot(feats_t[pl.ds(first, last - first), :], column)
        place(both, value, out, me[0], bits, quarters)
        if first == 0:
            acc[...] += dot_nt(column, w[pl.ds(k * channels, channels), :])
    grad[...] = acc[...].astype(grad.dtype)
    part(both, keep, send)


def conv(bits, me, src, tgt, sides, w, tables, quarters, shard, partial):
    begun = partial is not None
    shapes = [x.shape if begun else x.shape[::-1] for x in tables]
    (listed, rows), (count, channels) = shapes
    kernel = w.shape[0] // channels
    kinds, both = halves((len(quarters) * kernel * channels // 4, channels), shard)
    ext_rows = sum(side.shape[0] for side in sides)
    block = (rows, channels)
    grad = jax.ShapeDtypeStruct((count, channels), BF if begun else F32)
    operands = (me, src, tgt, *sides, w, *tables) + ((partial,) if begun else ())
    return pl.pallas_call(
        functools.partial(
            conv_kernel, conv_plan(kernel, channels, quarters), bits, quarters, begun
        ),
        out_shape=(grad,) + kinds,
        in_specs=[SMEM] * 3 + [VMEM] * (len(operands) - 3),
        out_specs=(VMEM,) * 3,
        scratch_shapes=[
            both,
            pltpu.VMEM((ext_rows // rows,) + block, BF),
            pltpu.VMEM((count, channels), F32),
            pltpu.VMEM((count // rows,) + block, BF),
            pltpu.VMEM((count // rows,) + block, BF),
        ]
        + [
            pltpu.VMEM((rows, listed), jnp.int32),
            pltpu.VMEM((channels, count), BF),
        ]
        * begun,
        compiler_params=pltpu.CompilerParams(vmem_limit_bytes=24 << 20),
        cost_estimate=SMALL,
        name="conv",
    )(*operands)


def moved(x, peers, to):
    pairs = [(i, to(i)) for i in range(peers)]
    return lax.ppermute(x, "space", [(i, j) for i, j in pairs if j is not None and 0 <= j < peers])


def fold(kept, got):
    half = kept.shape[0] // 2
    total = kept.astype(F32) + got.astype(F32)
    return total[:half], total[half:].astype(BF)


def fold_kernel(kept, got, keep, send):
    half = keep.shape[0]
    keep[...] = kept[:half].astype(F32) + got[:half].astype(F32)
    send[...] = (kept[half:].astype(F32) + got[half:].astype(F32)).astype(BF)


def fold_long(kept, got):
    shape = (kept.shape[0] // 2,) + kept.shape[1:]
    return pl.pallas_call(
        fold_kernel,
        out_shape=(jax.ShapeDtypeStruct(shape, F32), jax.ShapeDtypeStruct(shape, BF)),
        in_specs=[VMEM] * 2,
        out_specs=(VMEM,) * 2,
        compiler_params=pltpu.CompilerParams(vmem_limit_bytes=16 << 20),
        cost_estimate=pl.CostEstimate(flops=12 << 30, bytes_accessed=1 << 10, transcendentals=0),
        name="fold",
    )(kept, got)


def per_device(
    feats,
    pre_act,
    coarse_grad,
    w_sub,
    w_down,
    pair_src,
    pair_tgt,
    pair_rows,
    down_rows,
    down_parent,
):
    peers = lax.axis_size("space")
    me = lax.axis_index("space")
    row_count, channels = feats.shape
    block_rows = pair_rows.shape[-1]
    out_width = coarse_grad.shape[1]
    kernel = pair_src.shape[1]
    children = down_rows.shape[1]
    scale = 1.0 / math.sqrt(peers * row_count)
    bits = (peers // 8).bit_length() - 1
    near, far = peers // 4, peers // 2

    halo = HB * block_rows
    ident = me.reshape(1)
    pinned = lax.optimization_barrier
    low_bits = list(zip(*low_order(bits)))

    def across(x):
        return moved(x, peers, lambda i: i ^ 1)

    def xy(x, step):
        return moved(x, peers, lambda i: i ^ (2 << low_bits[step][i % 2]))

    def z_near(x):
        return moved(x, peers, lambda i: i ^ near)

    def z_far(x, wanted=(0, 1, 2, 3)):
        return moved(x, peers, lambda i: i ^ far if (i ^ far) // near in wanted else None)

    def middle(kept, got):
        kept, send = fold_long(kept, got)
        for step in range(1, bits - 1):
            kept, send = fold(kept, xy(send, step))
        return kept, send

    previous = moved(coarse_grad[-block_rows:], peers, lambda i: i + 1)
    prepared = prep(
        pre_act,
        down_rows[0],
        down_parent[0],
        w_down,
        coarse_grad,
        block_rows + coarse_grad.shape[0],
    )
    head, tail, low, low_send = down(
        bits, ident, previous, prepared, halo, children * channels // peers
    )

    before = moved(tail, peers, lambda i: i + 1)
    after = moved(head, peers, lambda i: i - 1)
    low_got = across(low_send)
    pairs = pair_rows[0].reshape(-1, block_rows)
    tables = turn(pairs, feats, w_sub)
    before, after, tables, low, low_got = pinned((before, after, tables, low, low_got))
    sides = (before, head, tail, after)
    shard = kernel * channels // peers

    def quarters(numbers, tables, partial=None):
        src, tgt = pair_src[0].T, pair_tgt[0].T
        return conv(bits, ident, src, tgt, sides, w_sub, tables, numbers, shard, partial)

    low, low_send = fold(low, low_got)
    low_got = xy(low_send, 0)
    partial, outer, outer_send = quarters((0, 3), tables)
    partial, low, low_got = pinned((partial, low, low_got))

    outer_got = across(outer_send)
    low, low_send = middle(low, low_got)
    outer_got, low, low_send = pinned((outer_got, low, low_send))
    low_got = xy(low_send, bits - 1)
    outer, outer_send = fold(outer, outer_got)
    partial, outer_send = pinned((partial, outer_send))
    outer_got = xy(outer_send, 0)
    grad_in, inner, inner_send = quarters((1, 2), (pairs, feats), partial)
    grad_in, outer, outer_got, low, low_got = pinned((grad_in, outer, outer_got, low, low_got))

    inner_got = across(inner_send)
    outer, outer_send = middle(outer, outer_got)
    outer_got = xy(outer_send, bits - 1)
    inner, inner_send = fold(inner, inner_got)
    inner_send, low, low_got = pinned((inner_send, low, low_got))
    inner_got = xy(inner_send, 0)
    low, low_send = fold(low, low_got)
    low_got = z_near(low_send)

    outer, outer_send = fold(outer, outer_got)
    outer_got = z_near(outer_send)
    low, low_send = fold(low, low_got)
    low_got = z_far(low_send)
    inner, inner_send = middle(inner, inner_got)
    inner_got = xy(inner_send, bits - 1)

    inner, inner_send = fold(inner, inner_got)
    inner_got = z_near(inner_send)

    def last_step(kept, got, wanted):
        total = kept + got.astype(F32)
        return total + z_far(total.astype(BF), wanted).astype(F32)

    digit = me // near
    is_outer = (digit == 0) | (digit == 3)
    outer_sum = last_step(outer, outer_got, (0, 3))
    inner_sum = last_step(inner, inner_got, (1, 2))
    sub_sum = jnp.where(is_outer, outer_sum, inner_sum)
    low_sum = (low + low_got.astype(F32)).reshape(-1, out_width)
    return (grad_in, sub_sum.reshape(-1) * scale, low_sum * scale)


def solution(mesh):
    rows = ("scene", "space")
    placed = (
        P(rows, None),
        P(rows, None),
        P(rows, None),
        P(),
        P(),
        P(rows, None, None),
        P(rows, None, None),
        P(rows, None, None, None),
        P(rows, None, None),
        P(rows, None, None),
    )
    return jax.shard_map(
        per_device,
        mesh=mesh,
        in_specs=placed,
        out_specs=(P(rows, None), P(rows), P(rows, None)),
        check_vma=False,
    )
```

```python
import functools
import math

import jax
import jax.numpy as jnp
from jax import lax
from jax.experimental import pallas as pl
from jax.experimental.pallas import tpu as pltpu
from jax.sharding import PartitionSpec as P

HB = 2
BF = jnp.bfloat16
F32 = jnp.float32


def dot(a, b):
    return lax.dot_general(a, b, (((1,), (0,)), ((), ())), preferred_element_type=F32)


def dot_nt(a, b):
    return lax.dot_general(a, b, (((1,), (1,)), ((), ())), preferred_element_type=F32)


def one_hot(index, shape, axis):
    return jnp.where(index == lax.broadcasted_iota(jnp.int32, shape, axis), 1.0, 0.0).astype(BF)


def segments(first, count, shard):
    row, cuts = first, []
    while row < first + count:
        number, inside = divmod(row, shard)
        rows = min(shard - inside, first + count - row)
        cuts.append((row - first, number, inside, rows))
        row += rows
    return cuts


def low_order(bits):
    return [[(j + core * (bits // 2)) % bits for j in range(bits)] for core in range(2)]


def position(number, me, bits, quarters):
    part, low = divmod(number, 2 << bits)
    core = low % 2
    at = core ^ (me & 1)
    for bit in low_order(bits)[core]:
        at = at * 2 + ((low >> (1 + bit) & 1) ^ (me >> (1 + bit) & 1))
    z = me >> (1 + bits)
    if len(quarters) == 4:
        at = at * 2 + ((part & 1) ^ (z & 1))
        return at * 2 + ((part >> 1) ^ (z >> 1))
    return at * 2 + (part ^ (z & 1) ^ (quarters[0] & 1))


def place(both, value, first, me, bits, quarters):
    for at, number, inside, rows in segments(first, value.shape[0], both.shape[1]):
        both[position(number, me, bits, quarters), pl.ds(inside, rows), :] = value[at : at + rows]


def halves(total, shard):
    count = total[0] // shard
    half = jax.ShapeDtypeStruct((count // 2, shard, total[1]), BF)
    return (half, half), pltpu.VMEM((count, shard, total[1]), F32)


def part(both, keep, send):
    half = keep.shape[0]
    keep[...] = both[:half].astype(BF)
    send[...] = both[half:].astype(BF)


def identity(size):
    return one_hot(lax.broadcasted_iota(jnp.int32, (size, size), 0), (size, size), 1)


def turned(table):
    values = table.astype(F32).astype(BF)
    return dot_nt(identity(table.shape[1]), values).astype(jnp.int32)


VMEM = pl.BlockSpec(memory_space=pltpu.VMEM)
SMEM = pl.BlockSpec(memory_space=pltpu.SMEM)


SMALL = pl.CostEstimate(flops=1 << 20, bytes_accessed=1 << 10, transcendentals=0)


def prep_kernel(pre, rows, parents, w_in, cur_in, act, pick, parent_pick, chosen, w, cur):
    children, slots = rows.shape
    count, channels = pre.shape
    columns = turned(parents[...])
    for c in range(children):
        mine = pl.ds(c * slots, slots)
        pick[:, mine] = one_hot(rows[c : c + 1, :], (count, slots), 0)
        parent_pick[mine, :] = one_hot(columns[:, c : c + 1], (slots, parent_pick.shape[1]), 1)
    act[...] = jnp.maximum(pre[...], jnp.zeros((), BF))
    turned_act = dot_nt(identity(channels), act[...]).astype(BF)
    chosen[...] = dot(turned_act, pick[...]).astype(BF)
    w[...] = w_in[...]
    cur[...] = cur_in[...]


def prep(pre, rows, parents, w, cur, parent_rows):
    count, channels = pre.shape
    children, slots = rows.shape
    shapes = (
        (count, channels),
        (count, children * slots),
        (children * slots, parent_rows),
        (channels, children * slots),
        w.shape,
        cur.shape,
    )
    return pl.pallas_call(
        prep_kernel,
        out_shape=tuple(jax.ShapeDtypeStruct(shape, BF) for shape in shapes),
        in_specs=[VMEM] * 5,
        out_specs=(VMEM,) * len(shapes),
        compiler_params=pltpu.CompilerParams(vmem_limit_bytes=16 << 20),
        cost_estimate=SMALL,
        name="prep",
    )(pre, rows, parents, w, cur)


def down_kernel(
    bits, me, prev, act, pick, parent_pick, chosen, w, cur, head, tail, keep, send, both, gath, contrib
):
    count, channels = act.shape
    children = w.shape[0] // channels
    slots = pick.shape[1] // children
    halo = head.shape[0]
    ext = jnp.concatenate([prev[...], cur[...]], 0)
    own = [pl.ds(c * slots, slots) for c in range(children)]
    for c in range(children):
        got = dot(parent_pick[own[c], :], ext).astype(BF)
        gath[own[c], :] = got
        contrib[own[c], :] = dot_nt(got, w[pl.ds(c * channels, channels), :]).astype(BF)
    grad = dot(pick[...], contrib[...])
    masked = jnp.where(act[...].astype(F32) > 0, grad, 0.0).astype(BF)
    head[...] = masked[:halo]
    tail[...] = masked[count - halo :]
    for c in range(children):
        value = dot(chosen[:, own[c]], gath[own[c], :])
        place(both, value, c * channels, me[0], bits, range(4))
    part(both, keep, send)


def down(bits, me, prev, prepared, halo, shard):
    act, pick, parent_pick, chosen, w, cur = prepared
    channels = act.shape[1]
    listed, width = pick.shape[1], cur.shape[1]
    kinds, both = halves(w.shape, shard)
    side = jax.ShapeDtypeStruct((halo, channels), BF)
    return pl.pallas_call(
        functools.partial(down_kernel, bits),
        out_shape=(side, side) + kinds,
        in_specs=[SMEM] + [VMEM] * 7,
        out_specs=(VMEM,) * 4,
        scratch_shapes=[
            both,
            pltpu.VMEM((listed, width), BF),
            pltpu.VMEM((listed, channels), BF),
        ],
        compiler_params=pltpu.CompilerParams(vmem_limit_bytes=20 << 20),
        cost_estimate=SMALL,
        name="down",
    )(me, prev, *prepared)


def conv_plan(kernel, channels, quarters):
    size = kernel * channels // 4
    plan, out = [], 0
    for quarter in quarters:
        row = quarter * size
        while row < (quarter + 1) * size:
            k, first = divmod(row, channels)
            last = min(channels, (quarter + 1) * size - k * channels)
            plan.append((k, first, last, out))
            out += last - first
            row += last - first
    return plan


def turn_kernel(pairs, feats, w, tab, feats_t):
    tab[...] = turned(pairs[...])
    feats_t[...] = dot_nt(identity(feats.shape[1]), feats[...]).astype(BF)


def turn(pairs, feats, w):
    return pl.pallas_call(
        turn_kernel,
        out_shape=(
            jax.ShapeDtypeStruct(pairs.shape[::-1], jnp.int32),
            jax.ShapeDtypeStruct(feats.shape[::-1], BF),
        ),
        in_specs=[VMEM] * 3,
        out_specs=(VMEM,) * 2,
        compiler_params=pltpu.CompilerParams(vmem_limit_bytes=20 << 20),
        cost_estimate=SMALL,
        name="turn",
    )(pairs, feats, w)


def conv_kernel(plan, bits, quarters, begun, *refs):
    me, src, tgt, before, head, tail, after, w, *rest = refs
    if begun:
        pairs, feats, partial, grad, keep, send, both, ext, acc, col0, col1, tab, feats_t = rest
        turn_kernel(pairs, feats, w, tab, feats_t)
    else:
        tab, feats_t, grad, keep, send, both, ext, acc, col0, col1 = rest
    cols = (col0, col1)
    slots = src.shape[0]
    blocks, rows, channels = col0.shape
    count = feats_t.shape[1]
    at = 0
    for piece in (before, head, tail, after):
        for b in range(piece.shape[0] // rows):
            ext[at] = piece[pl.ds(b * rows, rows), :]
            at += 1
    acc[...] = partial[...] if begun else jnp.zeros_like(acc)
    lanes = lax.broadcasted_iota(jnp.int32, (rows, rows), 1).astype(jnp.int16)
    one, zero = jnp.ones((), BF), jnp.zeros((), BF)

    def gather(k, col):
        col[...] = jnp.zeros_like(col)
        for p in range(slots):
            q = k * slots + p
            index = jnp.broadcast_to(tab[:, q : q + 1], (rows, rows)).astype(jnp.int16)
            pick = jnp.where(index == lanes, one, zero)
            piece = dot(pick, ext[tgt[p, k]]).astype(BF)
            owner = src[p, k]
            col[owner] = col[owner] + piece

    gather(plan[0][0], cols[0])
    for at, (k, first, last, out) in enumerate(plan):
        if at + 1 < len(plan):
            gather(plan[at + 1][0], cols[(at + 1) % 2])
        column = cols[at % 2][...].reshape(count, channels)
        value = dot(feats_t[pl.ds(first, last - first), :], column)
        place(both, value, out, me[0], bits, quarters)
        if first == 0:
            acc[...] += dot_nt(column, w[pl.ds(k * channels, channels), :])
    grad[...] = acc[...].astype(grad.dtype)
    part(both, keep, send)


def conv(bits, me, src, tgt, sides, w, tables, quarters, shard, partial):
    begun = partial is not None
    shapes = [x.shape if begun else x.shape[::-1] for x in tables]
    (listed, rows), (count, channels) = shapes
    kernel = w.shape[0] // channels
    kinds, both = halves((len(quarters) * kernel * channels // 4, channels), shard)
    ext_rows = sum(side.shape[0] for side in sides)
    block = (rows, channels)
    grad = jax.ShapeDtypeStruct((count, channels), BF if begun else F32)
    operands = (me, src, tgt, *sides, w, *tables) + ((partial,) if begun else ())
    return pl.pallas_call(
        functools.partial(
            conv_kernel, conv_plan(kernel, channels, quarters), bits, quarters, begun
        ),
        out_shape=(grad,) + kinds,
        in_specs=[SMEM] * 3 + [VMEM] * (len(operands) - 3),
        out_specs=(VMEM,) * 3,
        scratch_shapes=[
            both,
            pltpu.VMEM((ext_rows // rows,) + block, BF),
            pltpu.VMEM((count, channels), F32),
            pltpu.VMEM((count // rows,) + block, BF),
            pltpu.VMEM((count // rows,) + block, BF),
        ]
        + [
            pltpu.VMEM((rows, listed), jnp.int32),
            pltpu.VMEM((channels, count), BF),
        ]
        * begun,
        compiler_params=pltpu.CompilerParams(vmem_limit_bytes=24 << 20),
        cost_estimate=SMALL,
        name="conv",
    )(*operands)


def moved(x, peers, to):
    pairs = [(i, to(i)) for i in range(peers)]
    return lax.ppermute(x, "space", [(i, j) for i, j in pairs if j is not None and 0 <= j < peers])


def fold(kept, got):
    half = kept.shape[0] // 2
    total = kept.astype(F32) + got.astype(F32)
    return total[:half], total[half:].astype(BF)


def fold_kernel(kept, got, keep, send):
    half = keep.shape[0]
    keep[...] = kept[:half].astype(F32) + got[:half].astype(F32)
    send[...] = (kept[half:].astype(F32) + got[half:].astype(F32)).astype(BF)


def fold_long(kept, got):
    shape = (kept.shape[0] // 2,) + kept.shape[1:]
    return pl.pallas_call(
        fold_kernel,
        out_shape=(jax.ShapeDtypeStruct(shape, F32), jax.ShapeDtypeStruct(shape, BF)),
        in_specs=[VMEM] * 2,
        out_specs=(VMEM,) * 2,
        compiler_params=pltpu.CompilerParams(vmem_limit_bytes=16 << 20),
        cost_estimate=pl.CostEstimate(flops=12 << 30, bytes_accessed=1 << 10, transcendentals=0),
        name="fold",
    )(kept, got)


def per_device(
    feats,
    pre_act,
    coarse_grad,
    w_sub,
    w_down,
    pair_src,
    pair_tgt,
    pair_rows,
    down_rows,
    down_parent,
):
    peers = lax.axis_size("space")
    me = lax.axis_index("space")
    row_count, channels = feats.shape
    block_rows = pair_rows.shape[-1]
    out_width = coarse_grad.shape[1]
    kernel = pair_src.shape[1]
    children = down_rows.shape[1]
    scale = 1.0 / math.sqrt(peers * row_count)
    bits = (peers // 8).bit_length() - 1
    near, far = peers // 4, peers // 2

    halo = HB * block_rows
    ident = me.reshape(1)
    pinned = lax.optimization_barrier
    low_bits = list(zip(*low_order(bits)))

    def across(x):
        return moved(x, peers, lambda i: i ^ 1)

    def xy(x, step):
        return moved(x, peers, lambda i: i ^ (2 << low_bits[step][i % 2]))

    def z_near(x):
        return moved(x, peers, lambda i: i ^ near)

    def z_far(x, wanted=(0, 1, 2, 3)):
        return moved(x, peers, lambda i: i ^ far if (i ^ far) // near in wanted else None)

    def middle(kept, got):
        kept, send = fold_long(kept, got)
        for step in range(1, bits - 1):
            kept, send = fold(kept, xy(send, step))
        return kept, send

    previous = moved(coarse_grad[-block_rows:], peers, lambda i: i + 1)
    prepared = prep(
        pre_act,
        down_rows[0],
        down_parent[0],
        w_down,
        coarse_grad,
        block_rows + coarse_grad.shape[0],
    )
    head, tail, low, low_send = down(
        bits, ident, previous, prepared, halo, children * channels // peers
    )

    before = moved(tail, peers, lambda i: i + 1)
    after = moved(head, peers, lambda i: i - 1)
    low_got = across(low_send)
    pairs = pair_rows[0].reshape(-1, block_rows)
    tables = turn(pairs, feats, w_sub)
    before, after, tables, low, low_got = pinned((before, after, tables, low, low_got))
    sides = (before, head, tail, after)
    shard = kernel * channels // peers

    def quarters(numbers, tables, partial=None):
        src, tgt = pair_src[0].T, pair_tgt[0].T
        return conv(bits, ident, src, tgt, sides, w_sub, tables, numbers, shard, partial)

    low, low_send = fold(low, low_got)
    low_got = xy(low_send, 0)
    partial, outer, outer_send = quarters((0, 3), tables)
    partial, low, low_got = pinned((partial, low, low_got))

    outer_got = across(outer_send)
    low, low_send = middle(low, low_got)
    outer_got, low, low_send = pinned((outer_got, low, low_send))
    low_got = xy(low_send, bits - 1)
    outer, outer_send = fold(outer, outer_got)
    partial, outer_send = pinned((partial, outer_send))
    outer_got = xy(outer_send, 0)
    grad_in, inner, inner_send = quarters((1, 2), (pairs, feats), partial)
    grad_in, outer, outer_got, low, low_got = pinned((grad_in, outer, outer_got, low, low_got))

    inner_got = across(inner_send)
    outer, outer_send = middle(outer, outer_got)
    outer_got = xy(outer_send, bits - 1)
    low, low_send = fold_long(low, low_got)
    low_got = z_near(low_send)
    inner_got, outer, low = pinned((inner_got, outer, low))
    inner, inner_send = fold(inner, inner_got)
    inner_got = xy(inner_send, 0)

    outer, outer_send = fold_long(outer, outer_got)
    outer_got = z_near(outer_send)
    inner_got, outer, low_got = pinned((inner_got, outer, low_got))
    inner, inner_send = middle(inner, inner_got)
    inner_got = xy(inner_send, bits - 1)

    low, low_send = fold(low, low_got)
    low_got = z_far(low_send)
    outer = outer + outer_got.astype(F32)
    outer_got = z_far(outer.astype(BF), (0, 3))
    inner_got, outer, low_got = pinned((inner_got, outer, low_got))
    inner, inner_send = fold(inner, inner_got)
    inner_got = z_near(inner_send)
    inner = inner + inner_got.astype(F32)
    low_sum = (low + low_got.astype(F32)).reshape(-1, out_width) * scale

    outer_sum = outer + outer_got.astype(F32)
    inner, outer_sum = pinned((inner, outer_sum))
    inner_sum = inner + z_far(inner.astype(BF), (1, 2)).astype(F32)

    digit = me // near
    is_outer = (digit == 0) | (digit == 3)
    sub_sum = jnp.where(is_outer, outer_sum, inner_sum)
    return (grad_in, sub_sum.reshape(-1) * scale, low_sum)


def solution(mesh):
    rows = ("scene", "space")
    placed = (
        P(rows, None),
        P(rows, None),
        P(rows, None),
        P(),
        P(),
        P(rows, None, None),
        P(rows, None, None),
        P(rows, None, None, None),
        P(rows, None, None),
        P(rows, None, None),
    )
    return jax.shard_map(
        per_device,
        mesh=mesh,
        in_specs=placed,
        out_specs=(P(rows, None), P(rows), P(rows, None)),
        check_vma=False,
    )
```

```python
import functools
import math

import jax
import jax.numpy as jnp
from jax import lax
from jax.experimental import pallas as pl
from jax.experimental.pallas import tpu as pltpu
from jax.sharding import PartitionSpec as P

HB = 2
BF = jnp.bfloat16
F32 = jnp.float32


def dot(a, b):
    return lax.dot_general(a, b, (((1,), (0,)), ((), ())), preferred_element_type=F32)


def dot_nt(a, b):
    return lax.dot_general(a, b, (((1,), (1,)), ((), ())), preferred_element_type=F32)


def one_hot(index, shape, axis):
    return jnp.where(index == lax.broadcasted_iota(jnp.int32, shape, axis), 1.0, 0.0).astype(BF)


def segments(first, count, shard):
    row, cuts = first, []
    while row < first + count:
        number, inside = divmod(row, shard)
        rows = min(shard - inside, first + count - row)
        cuts.append((row - first, number, inside, rows))
        row += rows
    return cuts


def low_order(bits):
    return [[(j + core * (bits // 2)) % bits for j in range(bits)] for core in range(2)]


def position(number, me, bits, quarters):
    part, low = divmod(number, 2 << bits)
    core = low % 2
    at = core ^ (me & 1)
    for bit in low_order(bits)[core]:
        at = at * 2 + ((low >> (1 + bit) & 1) ^ (me >> (1 + bit) & 1))
    z = me >> (1 + bits)
    if len(quarters) == 4:
        at = at * 2 + ((part & 1) ^ (z & 1))
        return at * 2 + ((part >> 1) ^ (z >> 1))
    return at * 2 + (part ^ (z & 1) ^ (quarters[0] & 1))


def place(both, value, first, me, bits, quarters):
    for at, number, inside, rows in segments(first, value.shape[0], both.shape[1]):
        both[position(number, me, bits, quarters), pl.ds(inside, rows), :] = value[at : at + rows]


def halves(total, shard):
    count = total[0] // shard
    half = jax.ShapeDtypeStruct((count // 2, shard, total[1]), BF)
    return (half, half), pltpu.VMEM((count, shard, total[1]), F32)


def part(both, keep, send):
    half = keep.shape[0]
    keep[...] = both[:half].astype(BF)
    send[...] = both[half:].astype(BF)


def identity(size):
    return one_hot(lax.broadcasted_iota(jnp.int32, (size, size), 0), (size, size), 1)


def turned(table):
    values = table.astype(F32).astype(BF)
    return dot_nt(identity(table.shape[1]), values).astype(jnp.int32)


VMEM = pl.BlockSpec(memory_space=pltpu.VMEM)
SMEM = pl.BlockSpec(memory_space=pltpu.SMEM)


SMALL = pl.CostEstimate(flops=1 << 20, bytes_accessed=1 << 10, transcendentals=0)


def prep_kernel(pre, rows, parents, w_in, cur_in, act, pick, parent_pick, chosen, w, cur):
    children, slots = rows.shape
    count, channels = pre.shape
    columns = turned(parents[...])
    for c in range(children):
        mine = pl.ds(c * slots, slots)
        pick[:, mine] = one_hot(rows[c : c + 1, :], (count, slots), 0)
        parent_pick[mine, :] = one_hot(columns[:, c : c + 1], (slots, parent_pick.shape[1]), 1)
    act[...] = jnp.maximum(pre[...], jnp.zeros((), BF))
    turned_act = dot_nt(identity(channels), act[...]).astype(BF)
    chosen[...] = dot(turned_act, pick[...]).astype(BF)
    w[...] = w_in[...]
    cur[...] = cur_in[...]


def prep(pre, rows, parents, w, cur, parent_rows):
    count, channels = pre.shape
    children, slots = rows.shape
    shapes = (
        (count, channels),
        (count, children * slots),
        (children * slots, parent_rows),
        (channels, children * slots),
        w.shape,
        cur.shape,
    )
    return pl.pallas_call(
        prep_kernel,
        out_shape=tuple(jax.ShapeDtypeStruct(shape, BF) for shape in shapes),
        in_specs=[VMEM] * 5,
        out_specs=(VMEM,) * len(shapes),
        compiler_params=pltpu.CompilerParams(vmem_limit_bytes=16 << 20),
        cost_estimate=SMALL,
        name="prep",
    )(pre, rows, parents, w, cur)


def down_kernel(
    bits, me, prev, act, pick, parent_pick, chosen, w, cur, head, tail, keep, send, both, gath, contrib
):
    count, channels = act.shape
    children = w.shape[0] // channels
    slots = pick.shape[1] // children
    halo = head.shape[0]
    ext = jnp.concatenate([prev[...], cur[...]], 0)
    own = [pl.ds(c * slots, slots) for c in range(children)]
    for c in range(children):
        got = dot(parent_pick[own[c], :], ext).astype(BF)
        gath[own[c], :] = got
        contrib[own[c], :] = dot_nt(got, w[pl.ds(c * channels, channels), :]).astype(BF)
    grad = dot(pick[...], contrib[...])
    masked = jnp.where(act[...].astype(F32) > 0, grad, 0.0).astype(BF)
    head[...] = masked[:halo]
    tail[...] = masked[count - halo :]
    for c in range(children):
        value = dot(chosen[:, own[c]], gath[own[c], :])
        place(both, value, c * channels, me[0], bits, range(4))
    part(both, keep, send)


def down(bits, me, prev, prepared, halo, shard):
    act, pick, parent_pick, chosen, w, cur = prepared
    channels = act.shape[1]
    listed, width = pick.shape[1], cur.shape[1]
    kinds, both = halves(w.shape, shard)
    side = jax.ShapeDtypeStruct((halo, channels), BF)
    return pl.pallas_call(
        functools.partial(down_kernel, bits),
        out_shape=(side, side) + kinds,
        in_specs=[SMEM] + [VMEM] * 7,
        out_specs=(VMEM,) * 4,
        scratch_shapes=[
            both,
            pltpu.VMEM((listed, width), BF),
            pltpu.VMEM((listed, channels), BF),
        ],
        compiler_params=pltpu.CompilerParams(vmem_limit_bytes=20 << 20),
        cost_estimate=SMALL,
        name="down",
    )(me, prev, *prepared)


def conv_plan(kernel, channels, quarters):
    size = kernel * channels // 4
    plan, out = [], 0
    for quarter in quarters:
        row = quarter * size
        while row < (quarter + 1) * size:
            k, first = divmod(row, channels)
            last = min(channels, (quarter + 1) * size - k * channels)
            plan.append((k, first, last, out))
            out += last - first
            row += last - first
    return plan


def turn_kernel(pairs, feats, w, tab, feats_t):
    tab[...] = turned(pairs[...])
    feats_t[...] = dot_nt(identity(feats.shape[1]), feats[...]).astype(BF)


def turn(pairs, feats, w):
    return pl.pallas_call(
        turn_kernel,
        out_shape=(
            jax.ShapeDtypeStruct(pairs.shape[::-1], jnp.int32),
            jax.ShapeDtypeStruct(feats.shape[::-1], BF),
        ),
        in_specs=[VMEM] * 3,
        out_specs=(VMEM,) * 2,
        compiler_params=pltpu.CompilerParams(vmem_limit_bytes=20 << 20),
        cost_estimate=SMALL,
        name="turn",
    )(pairs, feats, w)


def conv_kernel(plan, bits, quarters, begun, *refs):
    me, src, tgt, before, head, tail, after, w, *rest = refs
    if begun:
        pairs, feats, partial, grad, keep, send, both, ext, acc, col0, col1, tab, feats_t = rest
        turn_kernel(pairs, feats, w, tab, feats_t)
    else:
        tab, feats_t, grad, keep, send, both, ext, acc, col0, col1 = rest
    cols = (col0, col1)
    slots = src.shape[0]
    blocks, rows, channels = col0.shape
    count = feats_t.shape[1]
    at = 0
    for piece in (before, head, tail, after):
        for b in range(piece.shape[0] // rows):
            ext[at] = piece[pl.ds(b * rows, rows), :]
            at += 1
    acc[...] = partial[...] if begun else jnp.zeros_like(acc)
    lanes = lax.broadcasted_iota(jnp.int32, (rows, rows), 1).astype(jnp.int16)
    one, zero = jnp.ones((), BF), jnp.zeros((), BF)

    def gather(k, col):
        col[...] = jnp.zeros_like(col)
        for p in range(slots):
            q = k * slots + p
            index = jnp.broadcast_to(tab[:, q : q + 1], (rows, rows)).astype(jnp.int16)
            pick = jnp.where(index == lanes, one, zero)
            piece = dot(pick, ext[tgt[p, k]]).astype(BF)
            owner = src[p, k]
            col[owner] = col[owner] + piece

    gather(plan[0][0], cols[0])
    for at, (k, first, last, out) in enumerate(plan):
        if at + 1 < len(plan):
            gather(plan[at + 1][0], cols[(at + 1) % 2])
        column = cols[at % 2][...].reshape(count, channels)
        value = dot(feats_t[pl.ds(first, last - first), :], column)
        place(both, value, out, me[0], bits, quarters)
        if first == 0:
            acc[...] += dot_nt(column, w[pl.ds(k * channels, channels), :])
    grad[...] = acc[...].astype(grad.dtype)
    part(both, keep, send)


def conv(bits, me, src, tgt, sides, w, tables, quarters, shard, partial):
    begun = partial is not None
    shapes = [x.shape if begun else x.shape[::-1] for x in tables]
    (listed, rows), (count, channels) = shapes
    kernel = w.shape[0] // channels
    kinds, both = halves((len(quarters) * kernel * channels // 4, channels), shard)
    ext_rows = sum(side.shape[0] for side in sides)
    block = (rows, channels)
    grad = jax.ShapeDtypeStruct((count, channels), BF if begun else F32)
    operands = (me, src, tgt, *sides, w, *tables) + ((partial,) if begun else ())
    return pl.pallas_call(
        functools.partial(
            conv_kernel, conv_plan(kernel, channels, quarters), bits, quarters, begun
        ),
        out_shape=(grad,) + kinds,
        in_specs=[SMEM] * 3 + [VMEM] * (len(operands) - 3),
        out_specs=(VMEM,) * 3,
        scratch_shapes=[
            both,
            pltpu.VMEM((ext_rows // rows,) + block, BF),
            pltpu.VMEM((count, channels), F32),
            pltpu.VMEM((count // rows,) + block, BF),
            pltpu.VMEM((count // rows,) + block, BF),
        ]
        + [
            pltpu.VMEM((rows, listed), jnp.int32),
            pltpu.VMEM((channels, count), BF),
        ]
        * begun,
        compiler_params=pltpu.CompilerParams(vmem_limit_bytes=24 << 20),
        cost_estimate=SMALL,
        name="conv",
    )(*operands)


def moved(x, peers, to):
    pairs = [(i, to(i)) for i in range(peers)]
    return lax.ppermute(x, "space", [(i, j) for i, j in pairs if j is not None and 0 <= j < peers])


def fold(kept, got):
    half = kept.shape[0] // 2
    total = kept.astype(F32) + got.astype(F32)
    return total[:half], total[half:].astype(BF)


def fold_kernel(kept, got, keep, send):
    half = keep.shape[0]
    keep[...] = kept[:half].astype(F32) + got[:half].astype(F32)
    send[...] = (kept[half:].astype(F32) + got[half:].astype(F32)).astype(BF)


def fold_long(kept, got):
    shape = (kept.shape[0] // 2,) + kept.shape[1:]
    return pl.pallas_call(
        fold_kernel,
        out_shape=(jax.ShapeDtypeStruct(shape, F32), jax.ShapeDtypeStruct(shape, BF)),
        in_specs=[VMEM] * 2,
        out_specs=(VMEM,) * 2,
        compiler_params=pltpu.CompilerParams(vmem_limit_bytes=16 << 20),
        cost_estimate=pl.CostEstimate(flops=6 << 30, bytes_accessed=1 << 10, transcendentals=0),
        name="fold",
    )(kept, got)


def per_device(
    feats,
    pre_act,
    coarse_grad,
    w_sub,
    w_down,
    pair_src,
    pair_tgt,
    pair_rows,
    down_rows,
    down_parent,
):
    peers = lax.axis_size("space")
    me = lax.axis_index("space")
    row_count, channels = feats.shape
    block_rows = pair_rows.shape[-1]
    out_width = coarse_grad.shape[1]
    kernel = pair_src.shape[1]
    children = down_rows.shape[1]
    scale = 1.0 / math.sqrt(peers * row_count)
    bits = (peers // 8).bit_length() - 1
    near, far = peers // 4, peers // 2

    halo = HB * block_rows
    ident = me.reshape(1)
    pinned = lax.optimization_barrier
    low_bits = list(zip(*low_order(bits)))

    def across(x):
        return moved(x, peers, lambda i: i ^ 1)

    def xy(x, step):
        return moved(x, peers, lambda i: i ^ (2 << low_bits[step][i % 2]))

    def z_near(x):
        return moved(x, peers, lambda i: i ^ near)

    def z_far(x, wanted=(0, 1, 2, 3)):
        return moved(x, peers, lambda i: i ^ far if (i ^ far) // near in wanted else None)

    def middle(kept, got):
        kept, send = fold_long(kept, got)
        for step in range(1, bits - 1):
            kept, send = fold(kept, xy(send, step))
        return kept, send

    previous = moved(coarse_grad[-block_rows:], peers, lambda i: i + 1)
    prepared = prep(
        pre_act,
        down_rows[0],
        down_parent[0],
        w_down,
        coarse_grad,
        block_rows + coarse_grad.shape[0],
    )
    head, tail, low, low_send = down(
        bits, ident, previous, prepared, halo, children * channels // peers
    )

    before = moved(tail, peers, lambda i: i + 1)
    after = moved(head, peers, lambda i: i - 1)
    low_got = across(low_send)
    pairs = pair_rows[0].reshape(-1, block_rows)
    tables = turn(pairs, feats, w_sub)
    before, after, tables, low, low_got = pinned((before, after, tables, low, low_got))
    sides = (before, head, tail, after)
    shard = kernel * channels // peers

    def quarters(numbers, tables, partial=None):
        src, tgt = pair_src[0].T, pair_tgt[0].T
        return conv(bits, ident, src, tgt, sides, w_sub, tables, numbers, shard, partial)

    low, low_send = fold(low, low_got)
    low_got = xy(low_send, 0)
    partial, outer, outer_send = quarters((0, 3), tables)
    partial, low, low_got = pinned((partial, low, low_got))

    outer_got = across(outer_send)
    low, low_send = middle(low, low_got)
    outer_got, low, low_send = pinned((outer_got, low, low_send))
    low_got = xy(low_send, bits - 1)
    outer, outer_send = fold(outer, outer_got)
    partial, outer_send = pinned((partial, outer_send))
    outer_got = xy(outer_send, 0)
    grad_in, inner, inner_send = quarters((1, 2), (pairs, feats), partial)
    grad_in, outer, outer_got, low, low_got = pinned((grad_in, outer, outer_got, low, low_got))

    inner_got = across(inner_send)
    outer, outer_send = middle(outer, outer_got)
    outer_got = xy(outer_send, bits - 1)
    low, low_send = fold_long(low, low_got)
    low_got = z_near(low_send)
    inner_got, outer, low = pinned((inner_got, outer, low))
    inner, inner_send = fold(inner, inner_got)
    inner_got = xy(inner_send, 0)

    outer, outer_send = fold_long(outer, outer_got)
    outer_got = z_near(outer_send)
    inner_got, outer, low_got = pinned((inner_got, outer, low_got))
    inner, inner_send = middle(inner, inner_got)
    inner_got = xy(inner_send, bits - 1)

    low, low_send = fold(low, low_got)
    low_got = z_far(low_send)
    outer = outer + outer_got.astype(F32)
    outer_got = z_far(outer.astype(BF), (0, 3))
    inner_got, outer, low_got = pinned((inner_got, outer, low_got))
    inner, inner_send = fold(inner, inner_got)
    inner_got = z_near(inner_send)
    inner = inner + inner_got.astype(F32)
    low_sum = (low + low_got.astype(F32)).reshape(-1, out_width) * scale

    outer_sum = outer + outer_got.astype(F32)
    inner, outer_sum = pinned((inner, outer_sum))
    inner_sum = inner + z_far(inner.astype(BF), (1, 2)).astype(F32)

    digit = me // near
    is_outer = (digit == 0) | (digit == 3)
    sub_sum = jnp.where(is_outer, outer_sum, inner_sum)
    return (grad_in, sub_sum.reshape(-1) * scale, low_sum)


def solution(mesh):
    rows = ("scene", "space")
    placed = (
        P(rows, None),
        P(rows, None),
        P(rows, None),
        P(),
        P(),
        P(rows, None, None),
        P(rows, None, None),
        P(rows, None, None, None),
        P(rows, None, None),
        P(rows, None, None),
    )
    return jax.shard_map(
        per_device,
        mesh=mesh,
        in_specs=placed,
        out_specs=(P(rows, None), P(rows), P(rows, None)),
        check_vma=False,
    )
```

```python
import functools
import math

import jax
import jax.numpy as jnp
from jax import lax
from jax.experimental import pallas as pl
from jax.experimental.pallas import tpu as pltpu
from jax.sharding import PartitionSpec as P

HB = 2
BF = jnp.bfloat16
F32 = jnp.float32


def dot(a, b):
    return lax.dot_general(a, b, (((1,), (0,)), ((), ())), preferred_element_type=F32)


def dot_nt(a, b):
    return lax.dot_general(a, b, (((1,), (1,)), ((), ())), preferred_element_type=F32)


def one_hot(index, shape, axis):
    return jnp.where(index == lax.broadcasted_iota(jnp.int32, shape, axis), 1.0, 0.0).astype(BF)


def segments(first, count, shard):
    row, cuts = first, []
    while row < first + count:
        number, inside = divmod(row, shard)
        rows = min(shard - inside, first + count - row)
        cuts.append((row - first, number, inside, rows))
        row += rows
    return cuts


def low_order(bits):
    return [[(j + core * (bits // 2)) % bits for j in range(bits)] for core in range(2)]


def position(number, me, bits, quarters):
    part, low = divmod(number, 2 << bits)
    core = low % 2
    at = core ^ (me & 1)
    for bit in low_order(bits)[core]:
        at = at * 2 + ((low >> (1 + bit) & 1) ^ (me >> (1 + bit) & 1))
    z = me >> (1 + bits)
    if len(quarters) == 4:
        at = at * 2 + ((part & 1) ^ (z & 1))
        return at * 2 + ((part >> 1) ^ (z >> 1))
    return at * 2 + (part ^ (z & 1) ^ (quarters[0] & 1))


def place(both, value, first, me, bits, quarters):
    for at, number, inside, rows in segments(first, value.shape[0], both.shape[1]):
        both[position(number, me, bits, quarters), pl.ds(inside, rows), :] = value[at : at + rows]


def halves(total, shard):
    count = total[0] // shard
    half = jax.ShapeDtypeStruct((count // 2, shard, total[1]), BF)
    return (half, half), pltpu.VMEM((count, shard, total[1]), F32)


def part(both, keep, send):
    half = keep.shape[0]
    keep[...] = both[:half].astype(BF)
    send[...] = both[half:].astype(BF)


def identity(size):
    return one_hot(lax.broadcasted_iota(jnp.int32, (size, size), 0), (size, size), 1)


def turned(table):
    values = table.astype(F32).astype(BF)
    return dot_nt(identity(table.shape[1]), values).astype(jnp.int32)


VMEM = pl.BlockSpec(memory_space=pltpu.VMEM)
SMEM = pl.BlockSpec(memory_space=pltpu.SMEM)


SMALL = pl.CostEstimate(flops=1 << 20, bytes_accessed=1 << 10, transcendentals=0)


def prep_kernel(pre, rows, parents, w_in, cur_in, act, pick, parent_pick, chosen, w, cur):
    children, slots = rows.shape
    count, channels = pre.shape
    columns = turned(parents[...])
    for c in range(children):
        mine = pl.ds(c * slots, slots)
        pick[:, mine] = one_hot(rows[c : c + 1, :], (count, slots), 0)
        parent_pick[mine, :] = one_hot(columns[:, c : c + 1], (slots, parent_pick.shape[1]), 1)
    act[...] = jnp.maximum(pre[...], jnp.zeros((), BF))
    turned_act = dot_nt(identity(channels), act[...]).astype(BF)
    chosen[...] = dot(turned_act, pick[...]).astype(BF)
    w[...] = w_in[...]
    cur[...] = cur_in[...]


def prep(pre, rows, parents, w, cur, parent_rows):
    count, channels = pre.shape
    children, slots = rows.shape
    shapes = (
        (count, channels),
        (count, children * slots),
        (children * slots, parent_rows),
        (channels, children * slots),
        w.shape,
        cur.shape,
    )
    return pl.pallas_call(
        prep_kernel,
        out_shape=tuple(jax.ShapeDtypeStruct(shape, BF) for shape in shapes),
        in_specs=[VMEM] * 5,
        out_specs=(VMEM,) * len(shapes),
        compiler_params=pltpu.CompilerParams(vmem_limit_bytes=16 << 20),
        cost_estimate=SMALL,
        name="prep",
    )(pre, rows, parents, w, cur)


def down_kernel(
    bits, me, prev, act, pick, parent_pick, chosen, w, cur, head, tail, keep, send, both, gath, contrib
):
    count, channels = act.shape
    children = w.shape[0] // channels
    slots = pick.shape[1] // children
    halo = head.shape[0]
    ext = jnp.concatenate([prev[...], cur[...]], 0)
    own = [pl.ds(c * slots, slots) for c in range(children)]
    for c in range(children):
        got = dot(parent_pick[own[c], :], ext).astype(BF)
        gath[own[c], :] = got
        contrib[own[c], :] = dot_nt(got, w[pl.ds(c * channels, channels), :]).astype(BF)
    grad = dot(pick[...], contrib[...])
    masked = jnp.where(act[...].astype(F32) > 0, grad, 0.0).astype(BF)
    head[...] = masked[:halo]
    tail[...] = masked[count - halo :]
    for c in range(children):
        value = dot(chosen[:, own[c]], gath[own[c], :])
        place(both, value, c * channels, me[0], bits, range(4))
    part(both, keep, send)


def down(bits, me, prev, prepared, halo, shard):
    act, pick, parent_pick, chosen, w, cur = prepared
    channels = act.shape[1]
    listed, width = pick.shape[1], cur.shape[1]
    kinds, both = halves(w.shape, shard)
    side = jax.ShapeDtypeStruct((halo, channels), BF)
    return pl.pallas_call(
        functools.partial(down_kernel, bits),
        out_shape=(side, side) + kinds,
        in_specs=[SMEM] + [VMEM] * 7,
        out_specs=(VMEM,) * 4,
        scratch_shapes=[
            both,
            pltpu.VMEM((listed, width), BF),
            pltpu.VMEM((listed, channels), BF),
        ],
        compiler_params=pltpu.CompilerParams(vmem_limit_bytes=20 << 20),
        cost_estimate=SMALL,
        name="down",
    )(me, prev, *prepared)


def conv_plan(kernel, channels, quarters):
    size = kernel * channels // 4
    plan, out = [], 0
    for quarter in quarters:
        row = quarter * size
        while row < (quarter + 1) * size:
            k, first = divmod(row, channels)
            last = min(channels, (quarter + 1) * size - k * channels)
            plan.append((k, first, last, out))
            out += last - first
            row += last - first
    return plan


def turn_kernel(pairs, feats, w, tab, feats_t):
    tab[...] = turned(pairs[...])
    feats_t[...] = dot_nt(identity(feats.shape[1]), feats[...]).astype(BF)


def turn(pairs, feats, w):
    return pl.pallas_call(
        turn_kernel,
        out_shape=(
            jax.ShapeDtypeStruct(pairs.shape[::-1], jnp.int32),
            jax.ShapeDtypeStruct(feats.shape[::-1], BF),
        ),
        in_specs=[VMEM] * 3,
        out_specs=(VMEM,) * 2,
        compiler_params=pltpu.CompilerParams(vmem_limit_bytes=20 << 20),
        cost_estimate=SMALL,
        name="turn",
    )(pairs, feats, w)


def conv_kernel(plan, bits, quarters, begun, *refs):
    me, src, tgt, before, head, tail, after, w, *rest = refs
    if begun:
        pairs, feats, partial, grad, keep, send, both, ext, acc, col0, col1, tab, feats_t = rest
        turn_kernel(pairs, feats, w, tab, feats_t)
    else:
        tab, feats_t, grad, keep, send, both, ext, acc, col0, col1 = rest
    cols = (col0, col1)
    slots = src.shape[0]
    blocks, rows, channels = col0.shape
    count = feats_t.shape[1]
    at = 0
    for piece in (before, head, tail, after):
        for b in range(piece.shape[0] // rows):
            ext[at] = piece[pl.ds(b * rows, rows), :]
            at += 1
    acc[...] = partial[...] if begun else jnp.zeros_like(acc)
    lanes = lax.broadcasted_iota(jnp.int32, (rows, rows), 1).astype(jnp.int16)
    one, zero = jnp.ones((), BF), jnp.zeros((), BF)

    def gather(k, col):
        col[...] = jnp.zeros_like(col)
        for p in range(slots):
            q = k * slots + p
            index = jnp.broadcast_to(tab[:, q : q + 1], (rows, rows)).astype(jnp.int16)
            pick = jnp.where(index == lanes, one, zero)
            piece = dot(pick, ext[tgt[p, k]]).astype(BF)
            owner = src[p, k]
            col[owner] = col[owner] + piece

    gather(plan[0][0], cols[0])
    for at, (k, first, last, out) in enumerate(plan):
        if at + 1 < len(plan):
            gather(plan[at + 1][0], cols[(at + 1) % 2])
        column = cols[at % 2][...].reshape(count, channels)
        value = dot(feats_t[pl.ds(first, last - first), :], column)
        place(both, value, out, me[0], bits, quarters)
        if first == 0:
            acc[...] += dot_nt(column, w[pl.ds(k * channels, channels), :])
    grad[...] = acc[...].astype(grad.dtype)
    part(both, keep, send)


def conv(bits, me, src, tgt, sides, w, tables, quarters, shard, partial):
    begun = partial is not None
    shapes = [x.shape if begun else x.shape[::-1] for x in tables]
    (listed, rows), (count, channels) = shapes
    kernel = w.shape[0] // channels
    kinds, both = halves((len(quarters) * kernel * channels // 4, channels), shard)
    ext_rows = sum(side.shape[0] for side in sides)
    block = (rows, channels)
    grad = jax.ShapeDtypeStruct((count, channels), BF if begun else F32)
    operands = (me, src, tgt, *sides, w, *tables) + ((partial,) if begun else ())
    return pl.pallas_call(
        functools.partial(
            conv_kernel, conv_plan(kernel, channels, quarters), bits, quarters, begun
        ),
        out_shape=(grad,) + kinds,
        in_specs=[SMEM] * 3 + [VMEM] * (len(operands) - 3),
        out_specs=(VMEM,) * 3,
        scratch_shapes=[
            both,
            pltpu.VMEM((ext_rows // rows,) + block, BF),
            pltpu.VMEM((count, channels), F32),
            pltpu.VMEM((count // rows,) + block, BF),
            pltpu.VMEM((count // rows,) + block, BF),
        ]
        + [
            pltpu.VMEM((rows, listed), jnp.int32),
            pltpu.VMEM((channels, count), BF),
        ]
        * begun,
        compiler_params=pltpu.CompilerParams(vmem_limit_bytes=24 << 20),
        cost_estimate=SMALL,
        name="conv",
    )(*operands)


def moved(x, peers, to):
    pairs = [(i, to(i)) for i in range(peers)]
    return lax.ppermute(x, "space", [(i, j) for i, j in pairs if j is not None and 0 <= j < peers])


def fold(kept, got):
    half = kept.shape[0] // 2
    total = kept.astype(F32) + got.astype(F32)
    return total[:half], total[half:].astype(BF)


def fold_kernel(kept, got, keep, send):
    half = keep.shape[0]
    keep[...] = kept[:half].astype(F32) + got[:half].astype(F32)
    send[...] = (kept[half:].astype(F32) + got[half:].astype(F32)).astype(BF)


def fold_long(kept, got):
    shape = (kept.shape[0] // 2,) + kept.shape[1:]
    return pl.pallas_call(
        fold_kernel,
        out_shape=(jax.ShapeDtypeStruct(shape, F32), jax.ShapeDtypeStruct(shape, BF)),
        in_specs=[VMEM] * 2,
        out_specs=(VMEM,) * 2,
        compiler_params=pltpu.CompilerParams(vmem_limit_bytes=16 << 20),
        cost_estimate=pl.CostEstimate(flops=6 << 30, bytes_accessed=1 << 10, transcendentals=0),
        name="fold",
    )(kept, got)


def per_device(
    feats,
    pre_act,
    coarse_grad,
    w_sub,
    w_down,
    pair_src,
    pair_tgt,
    pair_rows,
    down_rows,
    down_parent,
):
    peers = lax.axis_size("space")
    me = lax.axis_index("space")
    row_count, channels = feats.shape
    block_rows = pair_rows.shape[-1]
    out_width = coarse_grad.shape[1]
    kernel = pair_src.shape[1]
    children = down_rows.shape[1]
    scale = 1.0 / math.sqrt(peers * row_count)
    bits = (peers // 8).bit_length() - 1
    near, far = peers // 4, peers // 2

    halo = HB * block_rows
    ident = me.reshape(1)
    pinned = lax.optimization_barrier
    low_bits = list(zip(*low_order(bits)))

    def across(x):
        return moved(x, peers, lambda i: i ^ 1)

    def xy(x, step):
        return moved(x, peers, lambda i: i ^ (2 << low_bits[step][i % 2]))

    def z_near(x):
        return moved(x, peers, lambda i: i ^ near)

    def z_far(x, wanted=(0, 1, 2, 3)):
        return moved(x, peers, lambda i: i ^ far if (i ^ far) // near in wanted else None)

    def middle(kept, got):
        kept, send = fold_long(kept, got)
        for step in range(1, bits - 1):
            kept, send = fold(kept, xy(send, step))
        return kept, send

    previous = moved(coarse_grad[-block_rows:], peers, lambda i: i + 1)
    prepared = prep(
        pre_act,
        down_rows[0],
        down_parent[0],
        w_down,
        coarse_grad,
        block_rows + coarse_grad.shape[0],
    )
    head, tail, low, low_send = down(
        bits, ident, previous, prepared, halo, children * channels // peers
    )

    before = moved(tail, peers, lambda i: i + 1)
    after = moved(head, peers, lambda i: i - 1)
    low_got = across(low_send)
    pairs = pair_rows[0].reshape(-1, block_rows)
    tables = turn(pairs, feats, w_sub)
    before, after, tables, low, low_got = pinned((before, after, tables, low, low_got))
    sides = (before, head, tail, after)
    shard = kernel * channels // peers

    def quarters(numbers, tables, partial=None):
        src, tgt = pair_src[0].T, pair_tgt[0].T
        return conv(bits, ident, src, tgt, sides, w_sub, tables, numbers, shard, partial)

    low, low_send = fold(low, low_got)
    low_got = xy(low_send, 0)
    partial, outer, outer_send = quarters((0, 3), tables)
    partial, low, low_got = pinned((partial, low, low_got))

    outer_got = across(outer_send)
    low, low_send = middle(low, low_got)
    outer_got, low, low_send = pinned((outer_got, low, low_send))
    low_got = xy(low_send, bits - 1)
    outer, outer_send = fold(outer, outer_got)
    partial, outer_send = pinned((partial, outer_send))
    outer_got = xy(outer_send, 0)
    grad_in, inner, inner_send = quarters((1, 2), (pairs, feats), partial)
    grad_in, outer, outer_got, low, low_got = pinned((grad_in, outer, outer_got, low, low_got))

    inner_got = across(inner_send)
    outer, outer_send = middle(outer, outer_got)
    outer_got = xy(outer_send, bits - 1)
    low, low_send = fold(low, low_got)
    low_got = z_near(low_send)
    inner_got, outer, low = pinned((inner_got, outer, low))
    inner, inner_send = fold(inner, inner_got)
    inner_got = xy(inner_send, 0)

    outer, outer_send = fold(outer, outer_got)
    outer_got = z_near(outer_send)
    inner_got, outer, low_got = pinned((inner_got, outer, low_got))
    inner, inner_send = middle(inner, inner_got)
    inner_got = xy(inner_send, bits - 1)

    low, low_send = fold(low, low_got)
    low_got = z_far(low_send)
    outer = outer + outer_got.astype(F32)
    outer_got = z_far(outer.astype(BF), (0, 3))
    inner_got, outer, low_got = pinned((inner_got, outer, low_got))
    inner, inner_send = fold(inner, inner_got)
    inner_got = z_near(inner_send)
    inner = inner + inner_got.astype(F32)
    low_sum = (low + low_got.astype(F32)).reshape(-1, out_width) * scale

    outer_sum = outer + outer_got.astype(F32)
    inner, outer_sum = pinned((inner, outer_sum))
    inner_sum = inner + z_far(inner.astype(BF), (1, 2)).astype(F32)

    digit = me // near
    is_outer = (digit == 0) | (digit == 3)
    sub_sum = jnp.where(is_outer, outer_sum, inner_sum)
    return (grad_in, sub_sum.reshape(-1) * scale, low_sum)


def solution(mesh):
    rows = ("scene", "space")
    placed = (
        P(rows, None),
        P(rows, None),
        P(rows, None),
        P(),
        P(),
        P(rows, None, None),
        P(rows, None, None),
        P(rows, None, None, None),
        P(rows, None, None),
        P(rows, None, None),
    )
    return jax.shard_map(
        per_device,
        mesh=mesh,
        in_specs=placed,
        out_specs=(P(rows, None), P(rows), P(rows, None)),
        check_vma=False,
    )
```

```python
import functools
import math

import jax
import jax.numpy as jnp
from jax import lax
from jax.experimental import pallas as pl
from jax.experimental.pallas import tpu as pltpu
from jax.sharding import PartitionSpec as P

HB = 2
BF = jnp.bfloat16
F32 = jnp.float32


def dot(a, b):
    return lax.dot_general(a, b, (((1,), (0,)), ((), ())), preferred_element_type=F32)


def dot_nt(a, b):
    return lax.dot_general(a, b, (((1,), (1,)), ((), ())), preferred_element_type=F32)


def one_hot(index, shape, axis):
    return jnp.where(index == lax.broadcasted_iota(jnp.int32, shape, axis), 1.0, 0.0).astype(BF)


def segments(first, count, shard):
    row, cuts = first, []
    while row < first + count:
        number, inside = divmod(row, shard)
        rows = min(shard - inside, first + count - row)
        cuts.append((row - first, number, inside, rows))
        row += rows
    return cuts


def low_order(bits):
    return [[(j + core * (bits // 2)) % bits for j in range(bits)] for core in range(2)]


def position(number, me, bits, quarters):
    part, low = divmod(number, 2 << bits)
    core = low % 2
    at = core ^ (me & 1)
    for bit in low_order(bits)[core]:
        at = at * 2 + ((low >> (1 + bit) & 1) ^ (me >> (1 + bit) & 1))
    z = me >> (1 + bits)
    if len(quarters) == 4:
        at = at * 2 + ((part & 1) ^ (z & 1))
        return at * 2 + ((part >> 1) ^ (z >> 1))
    return at * 2 + (part ^ (z & 1) ^ (quarters[0] & 1))


def place(both, value, first, me, bits, quarters):
    for at, number, inside, rows in segments(first, value.shape[0], both.shape[1]):
        both[position(number, me, bits, quarters), pl.ds(inside, rows), :] = value[at : at + rows]


def halves(total, shard):
    count = total[0] // shard
    half = jax.ShapeDtypeStruct((count // 2, shard, total[1]), BF)
    return (half, half), pltpu.VMEM((count, shard, total[1]), F32)


def part(both, keep, send):
    half = keep.shape[0]
    keep[...] = both[:half].astype(BF)
    send[...] = both[half:].astype(BF)


def identity(size):
    return one_hot(lax.broadcasted_iota(jnp.int32, (size, size), 0), (size, size), 1)


def turned(table):
    values = table.astype(F32).astype(BF)
    return dot_nt(identity(table.shape[1]), values).astype(jnp.int32)


VMEM = pl.BlockSpec(memory_space=pltpu.VMEM)
SMEM = pl.BlockSpec(memory_space=pltpu.SMEM)


SMALL = pl.CostEstimate(flops=1 << 20, bytes_accessed=1 << 10, transcendentals=0)


def prep_kernel(pre, lists, w_in, cur_in, act, pick, parent_pick, chosen, w, cur):
    children, slots = lists.shape[0] // 2, lists.shape[1]
    rows, parents = lists[:children], lists[children:]
    count, channels = pre.shape
    columns = turned(parents)
    for c in range(children):
        mine = pl.ds(c * slots, slots)
        pick[:, mine] = one_hot(rows[c : c + 1, :], (count, slots), 0)
        parent_pick[mine, :] = one_hot(columns[:, c : c + 1], (slots, parent_pick.shape[1]), 1)
    act[...] = jnp.maximum(pre[...], jnp.zeros((), BF))
    turned_act = dot_nt(identity(channels), act[...]).astype(BF)
    chosen[...] = dot(turned_act, pick[...]).astype(BF)
    w[...] = w_in[...]
    cur[...] = cur_in[...]


def prep(pre, lists, w, cur, parent_rows):
    count, channels = pre.shape
    children, slots = lists.shape[0] // 2, lists.shape[1]
    shapes = (
        (count, channels),
        (count, children * slots),
        (children * slots, parent_rows),
        (channels, children * slots),
        w.shape,
        cur.shape,
    )
    return pl.pallas_call(
        prep_kernel,
        out_shape=tuple(jax.ShapeDtypeStruct(shape, BF) for shape in shapes),
        in_specs=[VMEM] * 4,
        out_specs=(VMEM,) * len(shapes),
        compiler_params=pltpu.CompilerParams(vmem_limit_bytes=16 << 20),
        cost_estimate=SMALL,
        name="prep",
    )(pre, lists, w, cur)


def down_kernel(
    bits, me, prev, act, pick, parent_pick, chosen, w, cur, head, tail, keep, send, both, gath, contrib
):
    count, channels = act.shape
    children = w.shape[0] // channels
    slots = pick.shape[1] // children
    halo = head.shape[0]
    ext = jnp.concatenate([prev[...], cur[...]], 0)
    own = [pl.ds(c * slots, slots) for c in range(children)]
    for c in range(children):
        got = dot(parent_pick[own[c], :], ext).astype(BF)
        gath[own[c], :] = got
        contrib[own[c], :] = dot_nt(got, w[pl.ds(c * channels, channels), :]).astype(BF)
    grad = dot(pick[...], contrib[...])
    masked = jnp.where(act[...].astype(F32) > 0, grad, 0.0).astype(BF)
    head[...] = masked[:halo]
    tail[...] = masked[count - halo :]
    for c in range(children):
        value = dot(chosen[:, own[c]], gath[own[c], :])
        place(both, value, c * channels, me[0], bits, range(4))
    part(both, keep, send)


def down(bits, me, prev, prepared, halo, shard):
    act, pick, parent_pick, chosen, w, cur = prepared
    channels = act.shape[1]
    listed, width = pick.shape[1], cur.shape[1]
    kinds, both = halves(w.shape, shard)
    side = jax.ShapeDtypeStruct((halo, channels), BF)
    return pl.pallas_call(
        functools.partial(down_kernel, bits),
        out_shape=(side, side) + kinds,
        in_specs=[SMEM] + [VMEM] * 7,
        out_specs=(VMEM,) * 4,
        scratch_shapes=[
            both,
            pltpu.VMEM((listed, width), BF),
            pltpu.VMEM((listed, channels), BF),
        ],
        compiler_params=pltpu.CompilerParams(vmem_limit_bytes=20 << 20),
        cost_estimate=SMALL,
        name="down",
    )(me, prev, *prepared)


def conv_plan(kernel, channels, quarters):
    size = kernel * channels // 4
    plan, out = [], 0
    for quarter in quarters:
        row = quarter * size
        while row < (quarter + 1) * size:
            k, first = divmod(row, channels)
            last = min(channels, (quarter + 1) * size - k * channels)
            plan.append((k, first, last, out))
            out += last - first
            row += last - first
    return plan


def turn_kernel(pairs, feats, w, tab, feats_t):
    tab[...] = turned(pairs[...])
    feats_t[...] = dot_nt(identity(feats.shape[1]), feats[...]).astype(BF)


def turn(pairs, feats, w):
    return pl.pallas_call(
        turn_kernel,
        out_shape=(
            jax.ShapeDtypeStruct(pairs.shape[::-1], jnp.int32),
            jax.ShapeDtypeStruct(feats.shape[::-1], BF),
        ),
        in_specs=[VMEM] * 3,
        out_specs=(VMEM,) * 2,
        compiler_params=pltpu.CompilerParams(vmem_limit_bytes=20 << 20),
        cost_estimate=SMALL,
        name="turn",
    )(pairs, feats, w)


def conv_kernel(plan, bits, quarters, begun, *refs):
    me, src, tgt, before, head, tail, after, w, *rest = refs
    if begun:
        pairs, feats, partial, grad, keep, send, both, ext, acc, col0, col1, tab, feats_t = rest
        turn_kernel(pairs, feats, w, tab, feats_t)
    else:
        tab, feats_t, grad, keep, send, both, ext, acc, col0, col1 = rest
    cols = (col0, col1)
    slots = src.shape[0]
    blocks, rows, channels = col0.shape
    count = feats_t.shape[1]
    at = 0
    for piece in (before, head, tail, after):
        for b in range(piece.shape[0] // rows):
            ext[at] = piece[pl.ds(b * rows, rows), :]
            at += 1
    acc[...] = partial[...] if begun else jnp.zeros_like(acc)
    lanes = lax.broadcasted_iota(jnp.int32, (rows, rows), 1).astype(jnp.int16)
    one, zero = jnp.ones((), BF), jnp.zeros((), BF)

    def gather(k, col):
        col[...] = jnp.zeros_like(col)
        for p in range(slots):
            q = k * slots + p
            index = jnp.broadcast_to(tab[:, q : q + 1], (rows, rows)).astype(jnp.int16)
            pick = jnp.where(index == lanes, one, zero)
            piece = dot(pick, ext[tgt[p, k]]).astype(BF)
            owner = src[p, k]
            col[owner] = col[owner] + piece

    gather(plan[0][0], cols[0])
    for at, (k, first, last, out) in enumerate(plan):
        if at + 1 < len(plan):
            gather(plan[at + 1][0], cols[(at + 1) % 2])
        column = cols[at % 2][...].reshape(count, channels)
        value = dot(feats_t[pl.ds(first, last - first), :], column)
        place(both, value, out, me[0], bits, quarters)
        if first == 0:
            acc[...] += dot_nt(column, w[pl.ds(k * channels, channels), :])
    grad[...] = acc[...].astype(grad.dtype)
    part(both, keep, send)


def conv(bits, me, src, tgt, sides, w, tables, quarters, shard, partial):
    begun = partial is not None
    shapes = [x.shape if begun else x.shape[::-1] for x in tables]
    (listed, rows), (count, channels) = shapes
    kernel = w.shape[0] // channels
    kinds, both = halves((len(quarters) * kernel * channels // 4, channels), shard)
    ext_rows = sum(side.shape[0] for side in sides)
    block = (rows, channels)
    grad = jax.ShapeDtypeStruct((count, channels), BF if begun else F32)
    operands = (me, src, tgt, *sides, w, *tables) + ((partial,) if begun else ())
    return pl.pallas_call(
        functools.partial(
            conv_kernel, conv_plan(kernel, channels, quarters), bits, quarters, begun
        ),
        out_shape=(grad,) + kinds,
        in_specs=[SMEM] * 3 + [VMEM] * (len(operands) - 3),
        out_specs=(VMEM,) * 3,
        scratch_shapes=[
            both,
            pltpu.VMEM((ext_rows // rows,) + block, BF),
            pltpu.VMEM((count, channels), F32),
            pltpu.VMEM((count // rows,) + block, BF),
            pltpu.VMEM((count // rows,) + block, BF),
        ]
        + [
            pltpu.VMEM((rows, listed), jnp.int32),
            pltpu.VMEM((channels, count), BF),
        ]
        * begun,
        compiler_params=pltpu.CompilerParams(vmem_limit_bytes=24 << 20),
        cost_estimate=SMALL,
        name="conv",
    )(*operands)


def moved(x, peers, to):
    pairs = [(i, to(i)) for i in range(peers)]
    return lax.ppermute(x, "space", [(i, j) for i, j in pairs if j is not None and 0 <= j < peers])


def fold(kept, got):
    half = kept.shape[0] // 2
    keep = kept[:half].astype(F32) + got[:half].astype(F32)
    send = kept[half:].astype(F32) + got[half:].astype(F32)
    return keep, send.astype(BF)


def fold_kernel(kept, got, keep, send):
    half = keep.shape[0]
    keep[...] = kept[:half].astype(F32) + got[:half].astype(F32)
    send[...] = (kept[half:].astype(F32) + got[half:].astype(F32)).astype(BF)


def fold_long(kept, got):
    shape = (kept.shape[0] // 2,) + kept.shape[1:]
    return pl.pallas_call(
        fold_kernel,
        out_shape=(jax.ShapeDtypeStruct(shape, F32), jax.ShapeDtypeStruct(shape, BF)),
        in_specs=[VMEM] * 2,
        out_specs=(VMEM,) * 2,
        compiler_params=pltpu.CompilerParams(vmem_limit_bytes=16 << 20),
        cost_estimate=pl.CostEstimate(flops=6 << 30, bytes_accessed=1 << 10, transcendentals=0),
        name="fold",
    )(kept, got)


def per_device(
    feats,
    pre_act,
    coarse_grad,
    w_sub,
    w_down,
    pair_src,
    pair_tgt,
    pair_rows,
    down_rows,
    down_parent,
):
    peers = lax.axis_size("space")
    me = lax.axis_index("space")
    row_count, channels = feats.shape
    block_rows = pair_rows.shape[-1]
    out_width = coarse_grad.shape[1]
    kernel = pair_src.shape[1]
    children = down_rows.shape[1]
    scale = 1.0 / math.sqrt(peers * row_count)
    bits = (peers // 8).bit_length() - 1
    near, far = peers // 4, peers // 2

    halo = HB * block_rows
    ident = me.reshape(1)
    pinned = lax.optimization_barrier
    low_bits = list(zip(*low_order(bits)))

    def across(x):
        return moved(x, peers, lambda i: i ^ 1)

    def xy(x, step):
        return moved(x, peers, lambda i: i ^ (2 << low_bits[step][i % 2]))

    def z_near(x):
        return moved(x, peers, lambda i: i ^ near)

    def z_far(x, wanted=(0, 1, 2, 3)):
        return moved(x, peers, lambda i: i ^ far if (i ^ far) // near in wanted else None)

    def middle(kept, got):
        kept, send = fold_long(kept, got)
        for step in range(1, bits - 1):
            kept, send = fold(kept, xy(send, step))
        return kept, send

    previous = moved(coarse_grad[-block_rows:], peers, lambda i: i + 1)
    prepared = prep(
        pre_act,
        jnp.concatenate([down_rows[0], down_parent[0]], 0),
        w_down,
        coarse_grad,
        block_rows + coarse_grad.shape[0],
    )
    head, tail, low, low_send = down(
        bits, ident, previous, prepared, halo, children * channels // peers
    )

    before = moved(tail, peers, lambda i: i + 1)
    after = moved(head, peers, lambda i: i - 1)
    low_got = across(low_send)
    pairs = pair_rows[0].reshape(-1, block_rows)
    tables = turn(pairs, feats, w_sub)
    before, after, tables, low, low_got = pinned((before, after, tables, low, low_got))
    sides = (before, head, tail, after)
    shard = kernel * channels // peers

    def quarters(numbers, tables, partial=None):
        src, tgt = pair_src[0].T, pair_tgt[0].T
        return conv(bits, ident, src, tgt, sides, w_sub, tables, numbers, shard, partial)

    low, low_send = fold(low, low_got)
    low_got = xy(low_send, 0)
    partial, outer, outer_send = quarters((0, 3), tables)
    partial, low, low_got = pinned((partial, low, low_got))

    outer_got = across(outer_send)
    low, low_send = middle(low, low_got)
    outer_got, low, low_send = pinned((outer_got, low, low_send))
    low_got = xy(low_send, bits - 1)
    outer, outer_send = fold(outer, outer_got)
    partial, outer_send = pinned((partial, outer_send))
    outer_got = xy(outer_send, 0)
    grad_in, inner, inner_send = quarters((1, 2), (pairs, feats), partial)
    grad_in, outer, outer_got, low, low_got = pinned((grad_in, outer, outer_got, low, low_got))

    inner_got = across(inner_send)
    outer, outer_send = middle(outer, outer_got)
    outer_got = xy(outer_send, bits - 1)
    low, low_send = fold(low, low_got)
    low_got = z_near(low_send)
    inner_got, outer, low = pinned((inner_got, outer, low))
    inner, inner_send = fold(inner, inner_got)
    inner_got = xy(inner_send, 0)

    outer, outer_send = fold(outer, outer_got)
    outer_got = z_near(outer_send)
    inner_got, outer, low_got = pinned((inner_got, outer, low_got))
    inner, inner_send = middle(inner, inner_got)
    inner_got = xy(inner_send, bits - 1)
    inner, low_got = pinned((inner, low_got))

    low, low_send = fold(low, low_got)
    low_got = z_far(low_send)
    outer = outer + outer_got.astype(F32)
    outer_got = z_far(outer.astype(BF), (0, 3))
    inner_got, outer, low_got = pinned((inner_got, outer, low_got))
    inner, inner_send = fold(inner, inner_got)
    inner_got = z_near(inner_send)
    inner = inner + inner_got.astype(F32)
    low_sum = (low + low_got.astype(F32)).reshape(-1, out_width) * scale

    outer_sum = outer + outer_got.astype(F32)
    inner, outer_sum = pinned((inner, outer_sum))
    inner_sum = inner + z_far(inner.astype(BF), (1, 2)).astype(F32)

    digit = me // near
    is_outer = (digit == 0) | (digit == 3)
    sub_sum = jnp.where(is_outer, outer_sum, inner_sum)
    return (grad_in, sub_sum.reshape(-1) * scale, low_sum)


def solution(mesh):
    rows = ("scene", "space")
    placed = (
        P(rows, None),
        P(rows, None),
        P(rows, None),
        P(),
        P(),
        P(rows, None, None),
        P(rows, None, None),
        P(rows, None, None, None),
        P(rows, None, None),
        P(rows, None, None),
    )
    return jax.shard_map(
        per_device,
        mesh=mesh,
        in_specs=placed,
        out_specs=(P(rows, None), P(rows), P(rows, None)),
        check_vma=False,
    )
```

```python
import functools
import math

import jax
import jax.numpy as jnp
from jax import lax
from jax.experimental import pallas as pl
from jax.experimental.pallas import tpu as pltpu
from jax.sharding import PartitionSpec as P

HB = 2
BF = jnp.bfloat16
F32 = jnp.float32


def dot(a, b):
    return lax.dot_general(a, b, (((1,), (0,)), ((), ())), preferred_element_type=F32)


def dot_nt(a, b):
    return lax.dot_general(a, b, (((1,), (1,)), ((), ())), preferred_element_type=F32)


def one_hot(index, shape, axis):
    return jnp.where(index == lax.broadcasted_iota(jnp.int32, shape, axis), 1.0, 0.0).astype(BF)


def segments(first, count, shard):
    row, cuts = first, []
    while row < first + count:
        number, inside = divmod(row, shard)
        rows = min(shard - inside, first + count - row)
        cuts.append((row - first, number, inside, rows))
        row += rows
    return cuts


def low_order(bits):
    return [[(j + core * (bits // 2)) % bits for j in range(bits)] for core in range(2)]


def position(number, me, bits, quarters):
    part, low = divmod(number, 2 << bits)
    core = low % 2
    at = core ^ (me & 1)
    for bit in low_order(bits)[core]:
        at = at * 2 + ((low >> (1 + bit) & 1) ^ (me >> (1 + bit) & 1))
    z = me >> (1 + bits)
    if len(quarters) == 4:
        at = at * 2 + ((part & 1) ^ (z & 1))
        return at * 2 + ((part >> 1) ^ (z >> 1))
    return at * 2 + (part ^ (z & 1) ^ (quarters[0] & 1))


def place(both, value, first, me, bits, quarters):
    for at, number, inside, rows in segments(first, value.shape[0], both.shape[1]):
        both[position(number, me, bits, quarters), pl.ds(inside, rows), :] = value[at : at + rows]


def halves(total, shard):
    count = total[0] // shard
    half = jax.ShapeDtypeStruct((count // 2, shard, total[1]), BF)
    return (half, half), pltpu.VMEM((count, shard, total[1]), F32)


def part(both, keep, send):
    half = keep.shape[0]
    keep[...] = both[:half].astype(BF)
    send[...] = both[half:].astype(BF)


def identity(size):
    return one_hot(lax.broadcasted_iota(jnp.int32, (size, size), 0), (size, size), 1)


def turned(table):
    values = table.astype(F32).astype(BF)
    return dot_nt(identity(table.shape[1]), values).astype(jnp.int32)


VMEM = pl.BlockSpec(memory_space=pltpu.VMEM)
SMEM = pl.BlockSpec(memory_space=pltpu.SMEM)


SMALL = pl.CostEstimate(flops=1 << 20, bytes_accessed=1 << 10, transcendentals=0)


def prep_kernel(pre, lists, w_in, cur_in, act, pick, parent_pick, chosen, w, cur):
    children, slots = lists.shape[0] // 2, lists.shape[1]
    rows, parents = lists[:children], lists[children:]
    count, channels = pre.shape
    columns = turned(parents)
    for c in range(children):
        mine = pl.ds(c * slots, slots)
        pick[:, mine] = one_hot(rows[c : c + 1, :], (count, slots), 0)
        parent_pick[mine, :] = one_hot(columns[:, c : c + 1], (slots, parent_pick.shape[1]), 1)
    act[...] = jnp.maximum(pre[...], jnp.zeros((), BF))
    turned_act = dot_nt(identity(channels), act[...]).astype(BF)
    chosen[...] = dot(turned_act, pick[...]).astype(BF)
    w[...] = w_in[...]
    cur[...] = cur_in[...]


def prep(pre, lists, w, cur, parent_rows):
    count, channels = pre.shape
    children, slots = lists.shape[0] // 2, lists.shape[1]
    shapes = (
        (count, channels),
        (count, children * slots),
        (children * slots, parent_rows),
        (channels, children * slots),
        w.shape,
        cur.shape,
    )
    return pl.pallas_call(
        prep_kernel,
        out_shape=tuple(jax.ShapeDtypeStruct(shape, BF) for shape in shapes),
        in_specs=[VMEM] * 4,
        out_specs=(VMEM,) * len(shapes),
        compiler_params=pltpu.CompilerParams(vmem_limit_bytes=16 << 20),
        cost_estimate=SMALL,
        name="prep",
    )(pre, lists, w, cur)


def down_kernel(
    bits, me, prev, act, pick, parent_pick, chosen, w, cur, head, tail, keep, send, both, gath, contrib
):
    count, channels = act.shape
    children = w.shape[0] // channels
    slots = pick.shape[1] // children
    halo = head.shape[0]
    ext = jnp.concatenate([prev[...], cur[...]], 0)
    own = [pl.ds(c * slots, slots) for c in range(children)]
    for c in range(children):
        got = dot(parent_pick[own[c], :], ext).astype(BF)
        gath[own[c], :] = got
        contrib[own[c], :] = dot_nt(got, w[pl.ds(c * channels, channels), :]).astype(BF)
    grad = dot(pick[...], contrib[...])
    masked = jnp.where(act[...].astype(F32) > 0, grad, 0.0).astype(BF)
    head[...] = masked[:halo]
    tail[...] = masked[count - halo :]
    for c in range(children):
        value = dot(chosen[:, own[c]], gath[own[c], :])
        place(both, value, c * channels, me[0], bits, range(4))
    part(both, keep, send)


def down(bits, me, prev, prepared, halo, shard):
    act, pick, parent_pick, chosen, w, cur = prepared
    channels = act.shape[1]
    listed, width = pick.shape[1], cur.shape[1]
    kinds, both = halves(w.shape, shard)
    side = jax.ShapeDtypeStruct((halo, channels), BF)
    return pl.pallas_call(
        functools.partial(down_kernel, bits),
        out_shape=(side, side) + kinds,
        in_specs=[SMEM] + [VMEM] * 7,
        out_specs=(VMEM,) * 4,
        scratch_shapes=[
            both,
            pltpu.VMEM((listed, width), BF),
            pltpu.VMEM((listed, channels), BF),
        ],
        compiler_params=pltpu.CompilerParams(vmem_limit_bytes=20 << 20),
        cost_estimate=SMALL,
        name="down",
    )(me, prev, *prepared)


def conv_plan(kernel, channels, quarters):
    size = kernel * channels // 4
    plan, out = [], 0
    for quarter in quarters:
        row = quarter * size
        while row < (quarter + 1) * size:
            k, first = divmod(row, channels)
            last = min(channels, (quarter + 1) * size - k * channels)
            plan.append((k, first, last, out))
            out += last - first
            row += last - first
    return plan


def turn_kernel(pairs, feats, w, tab, feats_t):
    tab[...] = turned(pairs[...])
    feats_t[...] = dot_nt(identity(feats.shape[1]), feats[...]).astype(BF)


def turn(pairs, feats, w):
    return pl.pallas_call(
        turn_kernel,
        out_shape=(
            jax.ShapeDtypeStruct(pairs.shape[::-1], jnp.int32),
            jax.ShapeDtypeStruct(feats.shape[::-1], BF),
        ),
        in_specs=[VMEM] * 3,
        out_specs=(VMEM,) * 2,
        compiler_params=pltpu.CompilerParams(vmem_limit_bytes=20 << 20),
        cost_estimate=SMALL,
        name="turn",
    )(pairs, feats, w)


def conv_kernel(plan, bits, quarters, begun, *refs):
    me, src, tgt, before, head, tail, after, w, *rest = refs
    if begun:
        pairs, feats, partial, grad, keep, send, both, ext, acc, col0, col1, col2, tab, feats_t = rest
        turn_kernel(pairs, feats, w, tab, feats_t)
    else:
        tab, feats_t, grad, keep, send, both, ext, acc, col0, col1, col2 = rest
    cols = (col0, col1, col2)
    slots = src.shape[0]
    blocks, rows, channels = col0.shape
    count = feats_t.shape[1]
    at = 0
    for piece in (before, head, tail, after):
        for b in range(piece.shape[0] // rows):
            ext[at] = piece[pl.ds(b * rows, rows), :]
            at += 1
    acc[...] = partial[...] if begun else jnp.zeros_like(acc)
    lanes = lax.broadcasted_iota(jnp.int32, (rows, rows), 1).astype(jnp.int16)
    one, zero = jnp.ones((), BF), jnp.zeros((), BF)

    def gather(k, col):
        col[...] = jnp.zeros_like(col)
        for p in range(slots):
            q = k * slots + p
            index = jnp.broadcast_to(tab[:, q : q + 1], (rows, rows)).astype(jnp.int16)
            pick = jnp.where(index == lanes, one, zero)
            piece = dot(pick, ext[tgt[p, k]]).astype(BF)
            owner = src[p, k]
            col[owner] = col[owner] + piece

    gather(plan[0][0], cols[0])
    waiting = []
    for at, (k, first, last, out) in enumerate(plan):
        if at + 1 < len(plan):
            gather(plan[at + 1][0], cols[(at + 1) % 3])
        column = cols[at % 3][...].reshape(count, channels)
        value = dot(feats_t[pl.ds(first, last - first), :], column)
        place(both, value, out, me[0], bits, quarters)
        if first == 0:
            waiting.append((cols[at % 3], k))
        if len(waiting) == 2 or (waiting and (first > 0 or at + 1 == len(plan))):
            terms = [
                dot_nt(col[...].reshape(count, channels), w[pl.ds(j * channels, channels), :])
                for col, j in waiting
            ]
            acc[...] += sum(terms[1:], terms[0])
            waiting = []
    grad[...] = acc[...].astype(grad.dtype)
    part(both, keep, send)


def conv(bits, me, src, tgt, sides, w, tables, quarters, shard, partial):
    begun = partial is not None
    shapes = [x.shape if begun else x.shape[::-1] for x in tables]
    (listed, rows), (count, channels) = shapes
    kernel = w.shape[0] // channels
    kinds, both = halves((len(quarters) * kernel * channels // 4, channels), shard)
    ext_rows = sum(side.shape[0] for side in sides)
    block = (rows, channels)
    grad = jax.ShapeDtypeStruct((count, channels), BF if begun else F32)
    operands = (me, src, tgt, *sides, w, *tables) + ((partial,) if begun else ())
    return pl.pallas_call(
        functools.partial(
            conv_kernel, conv_plan(kernel, channels, quarters), bits, quarters, begun
        ),
        out_shape=(grad,) + kinds,
        in_specs=[SMEM] * 3 + [VMEM] * (len(operands) - 3),
        out_specs=(VMEM,) * 3,
        scratch_shapes=[
            both,
            pltpu.VMEM((ext_rows // rows,) + block, BF),
            pltpu.VMEM((count, channels), F32),
            pltpu.VMEM((count // rows,) + block, BF),
            pltpu.VMEM((count // rows,) + block, BF),
            pltpu.VMEM((count // rows,) + block, BF),
        ]
        + [
            pltpu.VMEM((rows, listed), jnp.int32),
            pltpu.VMEM((channels, count), BF),
        ]
        * begun,
        compiler_params=pltpu.CompilerParams(vmem_limit_bytes=24 << 20),
        cost_estimate=SMALL,
        name="conv",
    )(*operands)


def moved(x, peers, to):
    pairs = [(i, to(i)) for i in range(peers)]
    return lax.ppermute(x, "space", [(i, j) for i, j in pairs if j is not None and 0 <= j < peers])


def fold(kept, got):
    half = kept.shape[0] // 2
    keep = kept[:half].astype(F32) + got[:half].astype(F32)
    send = kept[half:].astype(F32) + got[half:].astype(F32)
    return keep, send.astype(BF)


def fold_kernel(kept, got, keep, send):
    half = keep.shape[0]
    keep[...] = kept[:half].astype(F32) + got[:half].astype(F32)
    send[...] = (kept[half:].astype(F32) + got[half:].astype(F32)).astype(BF)


def fold_long(kept, got):
    shape = (kept.shape[0] // 2,) + kept.shape[1:]
    return pl.pallas_call(
        fold_kernel,
        out_shape=(jax.ShapeDtypeStruct(shape, F32), jax.ShapeDtypeStruct(shape, BF)),
        in_specs=[VMEM] * 2,
        out_specs=(VMEM,) * 2,
        compiler_params=pltpu.CompilerParams(vmem_limit_bytes=16 << 20),
        cost_estimate=pl.CostEstimate(flops=6 << 30, bytes_accessed=1 << 10, transcendentals=0),
        name="fold",
    )(kept, got)


def per_device(
    feats,
    pre_act,
    coarse_grad,
    w_sub,
    w_down,
    pair_src,
    pair_tgt,
    pair_rows,
    down_rows,
    down_parent,
):
    peers = lax.axis_size("space")
    me = lax.axis_index("space")
    row_count, channels = feats.shape
    block_rows = pair_rows.shape[-1]
    out_width = coarse_grad.shape[1]
    kernel = pair_src.shape[1]
    children = down_rows.shape[1]
    scale = 1.0 / math.sqrt(peers * row_count)
    bits = (peers // 8).bit_length() - 1
    near, far = peers // 4, peers // 2

    halo = HB * block_rows
    ident = me.reshape(1)
    pinned = lax.optimization_barrier
    low_bits = list(zip(*low_order(bits)))

    def across(x):
        return moved(x, peers, lambda i: i ^ 1)

    def xy(x, step):
        return moved(x, peers, lambda i: i ^ (2 << low_bits[step][i % 2]))

    def z_near(x):
        return moved(x, peers, lambda i: i ^ near)

    def z_far(x, wanted=(0, 1, 2, 3)):
        return moved(x, peers, lambda i: i ^ far if (i ^ far) // near in wanted else None)

    def middle(kept, got):
        kept, send = fold_long(kept, got)
        for step in range(1, bits - 1):
            kept, send = fold(kept, xy(send, step))
        return kept, send

    previous = moved(coarse_grad[-block_rows:], peers, lambda i: i + 1)
    prepared = prep(
        pre_act,
        jnp.concatenate([down_rows[0], down_parent[0]], 0),
        w_down,
        coarse_grad,
        block_rows + coarse_grad.shape[0],
    )
    head, tail, low, low_send = down(
        bits, ident, previous, prepared, halo, children * channels // peers
    )

    before = moved(tail, peers, lambda i: i + 1)
    after = moved(head, peers, lambda i: i - 1)
    low_got = across(low_send)
    pairs = pair_rows[0].reshape(-1, block_rows)
    tables = turn(pairs, feats, w_sub)
    before, after, tables, low, low_got = pinned((before, after, tables, low, low_got))
    sides = (before, head, tail, after)
    shard = kernel * channels // peers

    def quarters(numbers, tables, partial=None):
        src, tgt = pair_src[0].T, pair_tgt[0].T
        return conv(bits, ident, src, tgt, sides, w_sub, tables, numbers, shard, partial)

    low, low_send = fold(low, low_got)
    low_got = xy(low_send, 0)
    partial, outer, outer_send = quarters((0, 3), tables)
    partial, low, low_got = pinned((partial, low, low_got))

    outer_got = across(outer_send)
    low, low_send = middle(low, low_got)
    outer_got, low, low_send = pinned((outer_got, low, low_send))
    low_got = xy(low_send, bits - 1)
    outer, outer_send = fold(outer, outer_got)
    partial, outer_send = pinned((partial, outer_send))
    outer_got = xy(outer_send, 0)
    grad_in, inner, inner_send = quarters((1, 2), (pairs, feats), partial)
    grad_in, outer, outer_got, low, low_got = pinned((grad_in, outer, outer_got, low, low_got))

    inner_got = across(inner_send)
    outer, outer_send = middle(outer, outer_got)
    outer_got = xy(outer_send, bits - 1)
    low, low_send = fold(low, low_got)
    low_got = z_near(low_send)
    inner_got, outer, low = pinned((inner_got, outer, low))
    inner, inner_send = fold(inner, inner_got)
    inner_got = xy(inner_send, 0)

    outer, outer_send = fold(outer, outer_got)
    outer_got = z_near(outer_send)
    inner_got, outer, low_got = pinned((inner_got, outer, low_got))
    inner, inner_send = middle(inner, inner_got)
    inner_got = xy(inner_send, bits - 1)
    inner, low_got = pinned((inner, low_got))

    low, low_send = fold(low, low_got)
    low_got = z_far(low_send)
    outer = outer + outer_got.astype(F32)
    outer_got = z_far(outer.astype(BF), (0, 3))
    inner_got, outer, low_got = pinned((inner_got, outer, low_got))
    inner, inner_send = fold(inner, inner_got)
    inner_got = z_near(inner_send)
    inner = inner + inner_got.astype(F32)
    low_sum = (low + low_got.astype(F32)).reshape(-1, out_width) * scale

    outer_sum = outer + outer_got.astype(F32)
    inner, outer_sum = pinned((inner, outer_sum))
    inner_sum = inner + z_far(inner.astype(BF), (1, 2)).astype(F32)

    digit = me // near
    is_outer = (digit == 0) | (digit == 3)
    sub_sum = jnp.where(is_outer, outer_sum, inner_sum)
    return (grad_in, sub_sum.reshape(-1) * scale, low_sum)


def solution(mesh):
    rows = ("scene", "space")
    placed = (
        P(rows, None),
        P(rows, None),
        P(rows, None),
        P(),
        P(),
        P(rows, None, None),
        P(rows, None, None),
        P(rows, None, None, None),
        P(rows, None, None),
        P(rows, None, None),
    )
    return jax.shard_map(
        per_device,
        mesh=mesh,
        in_specs=placed,
        out_specs=(P(rows, None), P(rows), P(rows, None)),
        check_vma=False,
    )
```

```python
import functools
import math

import jax
import jax.numpy as jnp
from jax import lax
from jax.experimental import pallas as pl
from jax.experimental.pallas import tpu as pltpu
from jax.sharding import PartitionSpec as P

HB = 2
BF = jnp.bfloat16
F32 = jnp.float32


def dot(a, b):
    return lax.dot_general(a, b, (((1,), (0,)), ((), ())), preferred_element_type=F32)


def dot_nt(a, b):
    return lax.dot_general(a, b, (((1,), (1,)), ((), ())), preferred_element_type=F32)


def one_hot(index, shape, axis):
    return jnp.where(index == lax.broadcasted_iota(jnp.int32, shape, axis), 1.0, 0.0).astype(BF)


def segments(first, count, shard):
    row, cuts = first, []
    while row < first + count:
        number, inside = divmod(row, shard)
        rows = min(shard - inside, first + count - row)
        cuts.append((row - first, number, inside, rows))
        row += rows
    return cuts


def low_order(bits):
    return [[(j + core * (bits // 2)) % bits for j in range(bits)] for core in range(2)]


def position(number, me, bits, quarters):
    part, low = divmod(number, 2 << bits)
    core = low % 2
    at = core ^ (me & 1)
    for bit in low_order(bits)[core]:
        at = at * 2 + ((low >> (1 + bit) & 1) ^ (me >> (1 + bit) & 1))
    z = me >> (1 + bits)
    if len(quarters) == 4:
        at = at * 2 + ((part & 1) ^ (z & 1))
        return at * 2 + ((part >> 1) ^ (z >> 1))
    return at * 2 + (part ^ (z & 1) ^ (quarters[0] & 1))


def place(both, value, first, me, bits, quarters):
    for at, number, inside, rows in segments(first, value.shape[0], both.shape[1]):
        both[position(number, me, bits, quarters), pl.ds(inside, rows), :] = value[at : at + rows]


def halves(total, shard):
    count = total[0] // shard
    half = jax.ShapeDtypeStruct((count // 2, shard, total[1]), BF)
    return (half, half), pltpu.VMEM((count, shard, total[1]), F32)


def part(both, keep, send):
    half = keep.shape[0]
    keep[...] = both[:half].astype(BF)
    send[...] = both[half:].astype(BF)


def identity(size):
    return one_hot(lax.broadcasted_iota(jnp.int32, (size, size), 0), (size, size), 1)


def turned(table):
    values = table.astype(F32).astype(BF)
    return dot_nt(identity(table.shape[1]), values).astype(jnp.int32)


VMEM = pl.BlockSpec(memory_space=pltpu.VMEM)
SMEM = pl.BlockSpec(memory_space=pltpu.SMEM)


SMALL = pl.CostEstimate(flops=1 << 20, bytes_accessed=1 << 10, transcendentals=0)


def prep_kernel(pre, lists, w_in, cur_in, act, pick, parent_pick, chosen, w, cur):
    children, slots = lists.shape[0] // 2, lists.shape[1]
    rows, parents = lists[:children], lists[children:]
    count, channels = pre.shape
    columns = turned(parents)
    for c in range(children):
        mine = pl.ds(c * slots, slots)
        pick[:, mine] = one_hot(rows[c : c + 1, :], (count, slots), 0)
        parent_pick[mine, :] = one_hot(columns[:, c : c + 1], (slots, parent_pick.shape[1]), 1)
    act[...] = jnp.maximum(pre[...], jnp.zeros((), BF))
    turned_act = dot_nt(identity(channels), act[...]).astype(BF)
    chosen[...] = dot(turned_act, pick[...]).astype(BF)
    w[...] = w_in[...]
    cur[...] = cur_in[...]


def prep(pre, lists, w, cur, parent_rows):
    count, channels = pre.shape
    children, slots = lists.shape[0] // 2, lists.shape[1]
    shapes = (
        (count, channels),
        (count, children * slots),
        (children * slots, parent_rows),
        (channels, children * slots),
        w.shape,
        cur.shape,
    )
    return pl.pallas_call(
        prep_kernel,
        out_shape=tuple(jax.ShapeDtypeStruct(shape, BF) for shape in shapes),
        in_specs=[VMEM] * 4,
        out_specs=(VMEM,) * len(shapes),
        compiler_params=pltpu.CompilerParams(vmem_limit_bytes=16 << 20),
        cost_estimate=SMALL,
        name="prep",
    )(pre, lists, w, cur)


def down_kernel(
    bits, me, prev, act, pick, parent_pick, chosen, w, cur, head, tail, keep, send, both, gath, contrib
):
    count, channels = act.shape
    children = w.shape[0] // channels
    slots = pick.shape[1] // children
    halo = head.shape[0]
    ext = jnp.concatenate([prev[...], cur[...]], 0)
    own = [pl.ds(c * slots, slots) for c in range(children)]
    for c in range(children):
        got = dot(parent_pick[own[c], :], ext).astype(BF)
        gath[own[c], :] = got
        contrib[own[c], :] = dot_nt(got, w[pl.ds(c * channels, channels), :]).astype(BF)
    grad = dot(pick[...], contrib[...])
    masked = jnp.where(act[...].astype(F32) > 0, grad, 0.0).astype(BF)
    head[...] = masked[:halo]
    tail[...] = masked[count - halo :]
    for c in range(children):
        value = dot(chosen[:, own[c]], gath[own[c], :])
        place(both, value, c * channels, me[0], bits, range(4))
    part(both, keep, send)


def down(bits, me, prev, prepared, halo, shard):
    act, pick, parent_pick, chosen, w, cur = prepared
    channels = act.shape[1]
    listed, width = pick.shape[1], cur.shape[1]
    kinds, both = halves(w.shape, shard)
    side = jax.ShapeDtypeStruct((halo, channels), BF)
    return pl.pallas_call(
        functools.partial(down_kernel, bits),
        out_shape=(side, side) + kinds,
        in_specs=[SMEM] + [VMEM] * 7,
        out_specs=(VMEM,) * 4,
        scratch_shapes=[
            both,
            pltpu.VMEM((listed, width), BF),
            pltpu.VMEM((listed, channels), BF),
        ],
        compiler_params=pltpu.CompilerParams(vmem_limit_bytes=20 << 20),
        cost_estimate=SMALL,
        name="down",
    )(me, prev, *prepared)


def conv_plan(kernel, channels, quarters):
    size = kernel * channels // 4
    plan, out = [], 0
    for quarter in quarters:
        row = quarter * size
        while row < (quarter + 1) * size:
            k, first = divmod(row, channels)
            last = min(channels, (quarter + 1) * size - k * channels)
            plan.append((k, first, last, out))
            out += last - first
            row += last - first
    return plan


def turn_kernel(pairs, feats, w, tab, feats_t):
    tab[...] = turned(pairs[...])
    feats_t[...] = dot_nt(identity(feats.shape[1]), feats[...]).astype(BF)


def turn(pairs, feats, w):
    return pl.pallas_call(
        turn_kernel,
        out_shape=(
            jax.ShapeDtypeStruct(pairs.shape[::-1], jnp.int32),
            jax.ShapeDtypeStruct(feats.shape[::-1], BF),
        ),
        in_specs=[VMEM] * 3,
        out_specs=(VMEM,) * 2,
        compiler_params=pltpu.CompilerParams(vmem_limit_bytes=20 << 20),
        cost_estimate=SMALL,
        name="turn",
    )(pairs, feats, w)


def conv_kernel(plan, bits, quarters, begun, *refs):
    me, src, tgt, before, head, tail, after, w, *rest = refs
    if begun:
        pairs, feats, partial, grad, keep, send, both, ext, acc, col0, col1, tab, feats_t = rest
        turn_kernel(pairs, feats, w, tab, feats_t)
    else:
        tab, feats_t, grad, keep, send, both, ext, acc, col0, col1 = rest
    cols = (col0, col1)
    slots = src.shape[0]
    blocks, rows, channels = col0.shape
    count = feats_t.shape[1]
    at = 0
    for piece in (before, head, tail, after):
        for b in range(piece.shape[0] // rows):
            ext[at] = piece[pl.ds(b * rows, rows), :]
            at += 1
    acc[...] = partial[...] if begun else jnp.zeros_like(acc)
    lanes = lax.broadcasted_iota(jnp.int32, (rows, rows), 1).astype(jnp.int16)
    one, zero = jnp.ones((), BF), jnp.zeros((), BF)

    def gather(k, col):
        col[...] = jnp.zeros_like(col)
        for p in range(slots):
            q = k * slots + p
            index = jnp.broadcast_to(tab[:, q : q + 1], (rows, rows)).astype(jnp.int16)
            pick = jnp.where(index == lanes, one, zero)
            piece = dot(pick, ext[tgt[p, k]]).astype(BF)
            owner = src[p, k]
            col[owner] = col[owner] + piece

    gather(plan[0][0], cols[0])
    for at, (k, first, last, out) in enumerate(plan):
        column = cols[at % 2][...].reshape(count, channels)
        value = dot(feats_t[pl.ds(first, last - first), :], column)
        place(both, value, out, me[0], bits, quarters)
        if at + 1 < len(plan):
            gather(plan[at + 1][0], cols[(at + 1) % 2])
        if first == 0:
            acc[...] += dot_nt(column, w[pl.ds(k * channels, channels), :])
    grad[...] = acc[...].astype(grad.dtype)
    part(both, keep, send)


def conv(bits, me, src, tgt, sides, w, tables, quarters, shard, partial):
    begun = partial is not None
    shapes = [x.shape if begun else x.shape[::-1] for x in tables]
    (listed, rows), (count, channels) = shapes
    kernel = w.shape[0] // channels
    kinds, both = halves((len(quarters) * kernel * channels // 4, channels), shard)
    ext_rows = sum(side.shape[0] for side in sides)
    block = (rows, channels)
    grad = jax.ShapeDtypeStruct((count, channels), BF if begun else F32)
    operands = (me, src, tgt, *sides, w, *tables) + ((partial,) if begun else ())
    return pl.pallas_call(
        functools.partial(
            conv_kernel, conv_plan(kernel, channels, quarters), bits, quarters, begun
        ),
        out_shape=(grad,) + kinds,
        in_specs=[SMEM] * 3 + [VMEM] * (len(operands) - 3),
        out_specs=(VMEM,) * 3,
        scratch_shapes=[
            both,
            pltpu.VMEM((ext_rows // rows,) + block, BF),
            pltpu.VMEM((count, channels), F32),
            pltpu.VMEM((count // rows,) + block, BF),
            pltpu.VMEM((count // rows,) + block, BF),
        ]
        + [
            pltpu.VMEM((rows, listed), jnp.int32),
            pltpu.VMEM((channels, count), BF),
        ]
        * begun,
        compiler_params=pltpu.CompilerParams(vmem_limit_bytes=24 << 20),
        cost_estimate=SMALL,
        name="conv",
    )(*operands)


def moved(x, peers, to):
    pairs = [(i, to(i)) for i in range(peers)]
    return lax.ppermute(x, "space", [(i, j) for i, j in pairs if j is not None and 0 <= j < peers])


def fold(kept, got):
    half = kept.shape[0] // 2
    keep = kept[:half].astype(F32) + got[:half].astype(F32)
    send = kept[half:].astype(F32) + got[half:].astype(F32)
    return keep, send.astype(BF)


def fold_kernel(kept, got, keep, send):
    half = keep.shape[0]
    keep[...] = kept[:half].astype(F32) + got[:half].astype(F32)
    send[...] = (kept[half:].astype(F32) + got[half:].astype(F32)).astype(BF)


def fold_long(kept, got):
    shape = (kept.shape[0] // 2,) + kept.shape[1:]
    return pl.pallas_call(
        fold_kernel,
        out_shape=(jax.ShapeDtypeStruct(shape, F32), jax.ShapeDtypeStruct(shape, BF)),
        in_specs=[VMEM] * 2,
        out_specs=(VMEM,) * 2,
        compiler_params=pltpu.CompilerParams(vmem_limit_bytes=16 << 20),
        cost_estimate=pl.CostEstimate(flops=6 << 30, bytes_accessed=1 << 10, transcendentals=0),
        name="fold",
    )(kept, got)


def per_device(
    feats,
    pre_act,
    coarse_grad,
    w_sub,
    w_down,
    pair_src,
    pair_tgt,
    pair_rows,
    down_rows,
    down_parent,
):
    peers = lax.axis_size("space")
    me = lax.axis_index("space")
    row_count, channels = feats.shape
    block_rows = pair_rows.shape[-1]
    out_width = coarse_grad.shape[1]
    kernel = pair_src.shape[1]
    children = down_rows.shape[1]
    scale = 1.0 / math.sqrt(peers * row_count)
    bits = (peers // 8).bit_length() - 1
    near, far = peers // 4, peers // 2

    halo = HB * block_rows
    ident = me.reshape(1)
    pinned = lax.optimization_barrier
    low_bits = list(zip(*low_order(bits)))

    def across(x):
        return moved(x, peers, lambda i: i ^ 1)

    def xy(x, step):
        return moved(x, peers, lambda i: i ^ (2 << low_bits[step][i % 2]))

    def z_near(x):
        return moved(x, peers, lambda i: i ^ near)

    def z_far(x, wanted=(0, 1, 2, 3)):
        return moved(x, peers, lambda i: i ^ far if (i ^ far) // near in wanted else None)

    def middle(kept, got):
        kept, send = fold_long(kept, got)
        for step in range(1, bits - 1):
            kept, send = fold(kept, xy(send, step))
        return kept, send

    previous = moved(coarse_grad[-block_rows:], peers, lambda i: i + 1)
    prepared = prep(
        pre_act,
        jnp.concatenate([down_rows[0], down_parent[0]], 0),
        w_down,
        coarse_grad,
        block_rows + coarse_grad.shape[0],
    )
    head, tail, low, low_send = down(
        bits, ident, previous, prepared, halo, children * channels // peers
    )

    before = moved(tail, peers, lambda i: i + 1)
    after = moved(head, peers, lambda i: i - 1)
    low_got = across(low_send)
    pairs = pair_rows[0].reshape(-1, block_rows)
    tables = turn(pairs, feats, w_sub)
    before, after, tables, low, low_got = pinned((before, after, tables, low, low_got))
    sides = (before, head, tail, after)
    shard = kernel * channels // peers

    def quarters(numbers, tables, partial=None):
        src, tgt = pair_src[0].T, pair_tgt[0].T
        return conv(bits, ident, src, tgt, sides, w_sub, tables, numbers, shard, partial)

    low, low_send = fold(low, low_got)
    low_got = xy(low_send, 0)
    partial, outer, outer_send = quarters((0, 3), tables)
    partial, low, low_got = pinned((partial, low, low_got))

    outer_got = across(outer_send)
    low, low_send = middle(low, low_got)
    outer_got, low, low_send = pinned((outer_got, low, low_send))
    low_got = xy(low_send, bits - 1)
    outer, outer_send = fold(outer, outer_got)
    partial, outer_send = pinned((partial, outer_send))
    outer_got = xy(outer_send, 0)
    grad_in, inner, inner_send = quarters((1, 2), (pairs, feats), partial)
    grad_in, outer, outer_got, low, low_got = pinned((grad_in, outer, outer_got, low, low_got))

    inner_got = across(inner_send)
    outer, outer_send = middle(outer, outer_got)
    outer_got = xy(outer_send, bits - 1)
    low, low_send = fold(low, low_got)
    low_got = z_near(low_send)
    inner_got, outer, low = pinned((inner_got, outer, low))
    inner, inner_send = fold(inner, inner_got)
    inner_got = xy(inner_send, 0)

    outer, outer_send = fold(outer, outer_got)
    outer_got = z_near(outer_send)
    inner_got, outer, low_got = pinned((inner_got, outer, low_got))
    inner, inner_send = middle(inner, inner_got)
    inner_got = xy(inner_send, bits - 1)
    inner, low_got = pinned((inner, low_got))

    low, low_send = fold(low, low_got)
    low_got = z_far(low_send)
    outer = outer + outer_got.astype(F32)
    outer_got = z_far(outer.astype(BF), (0, 3))
    inner_got, outer, low_got = pinned((inner_got, outer, low_got))
    inner, inner_send = fold(inner, inner_got)
    inner_got = z_near(inner_send)
    inner = inner + inner_got.astype(F32)
    low_sum = (low + low_got.astype(F32)).reshape(-1, out_width) * scale

    outer_sum = outer + outer_got.astype(F32)
    inner, outer_sum = pinned((inner, outer_sum))
    inner_sum = inner + z_far(inner.astype(BF), (1, 2)).astype(F32)

    digit = me // near
    is_outer = (digit == 0) | (digit == 3)
    sub_sum = jnp.where(is_outer, outer_sum, inner_sum)
    return (grad_in, sub_sum.reshape(-1) * scale, low_sum)


def solution(mesh):
    rows = ("scene", "space")
    placed = (
        P(rows, None),
        P(rows, None),
        P(rows, None),
        P(),
        P(),
        P(rows, None, None),
        P(rows, None, None),
        P(rows, None, None, None),
        P(rows, None, None),
        P(rows, None, None),
    )
    return jax.shard_map(
        per_device,
        mesh=mesh,
        in_specs=placed,
        out_specs=(P(rows, None), P(rows), P(rows, None)),
        check_vma=False,
    )
```
